32 devices in a mesh: dp: 8 (over z, y), fsdp: 4 (over x, core).
Axes of the slice: x: 2, y: 2, z: 4, core: 2. Of those that a mesh axis runs over, the one named last changes fastest.
Arguments:
- tokens: bfloat16 [8192, 1024], P(('dp', 'fsdp')), may hold values from -6 to 6
- cotangent: bfloat16 [8192, 1024], P(('dp', 'fsdp')), may hold values from -6 to 6
- seq_lengths: int32 [32, 4], P(('dp', 'fsdp')), may hold values from 0 to 256, as said below
- att_master: float32 [1024, 4096], P(('dp', 'fsdp')), may hold values from -3 to 3
- ffn_master: float32 [2, 1024, 4096], P(None, ('dp', 'fsdp')), may hold values from -1 to 1
- norm_master: float32 [4, 1024], P(None, ('dp', 'fsdp')), may hold values from -2 to 2
- att_moment: float32 [1024, 4096], P(('dp', 'fsdp')), may hold values from -6 to 6
- ffn_moment: float32 [2, 1024, 4096], P(None, ('dp', 'fsdp')), may hold values from -16 to 16
- norm_moment: float32 [4, 1024], P(None, ('dp', 'fsdp')), may hold values from -56 to 56
- att_average: float32 [1024, 4096], P(('dp', 'fsdp')), may hold values from -0.75 to 0.75
- ffn_average: float32 [2, 1024, 4096], P(None, ('dp', 'fsdp')), may hold values from -0.4375 to 0.4375
- norm_average: float32 [4, 1024], P(None, ('dp', 'fsdp')), may hold values from -6 to 6
Outputs:
- layer_output: bfloat16 [8192, 1024], P(('dp', 'fsdp'))
- input_grad: float32 [8192, 1024], P(('dp', 'fsdp'))
- att_grad: float32 [1024, 4096], P(('dp', 'fsdp'))
- att_moment_new: float32 [1024, 4096], P(('dp', 'fsdp'))
- att_new: float32 [1024, 4096], P(('dp', 'fsdp'))
- att_average_new: float32 [1024, 4096], P(('dp', 'fsdp'))
- att_copy: bfloat16 [1024, 4096], P(('dp', 'fsdp'))
- ffn_grad: float32 [2, 1024, 4096], P(None, ('dp', 'fsdp'))
- ffn_moment_new: float32 [2, 1024, 4096], P(None, ('dp', 'fsdp'))
- ffn_new: float32 [2, 1024, 4096], P(None, ('dp', 'fsdp'))
- ffn_average_new: float32 [2, 1024, 4096], P(None, ('dp', 'fsdp'))
- ffn_copy: bfloat16 [2, 1024, 4096], P(None, ('dp', 'fsdp'))
- norm_grad: float32 [4, 1024], P(None, ('dp', 'fsdp'))
- norm_moment_new: float32 [4, 1024], P(None, ('dp', 'fsdp'))
- norm_new: float32 [4, 1024], P(None, ('dp', 'fsdp'))
- norm_average_new: float32 [4, 1024], P(None, ('dp', 'fsdp'))
- norm_copy: bfloat16 [4, 1024], P(None, ('dp', 'fsdp'))
The draws below stay inside these ranges and needn't reach their ends.
Inputs may be any that keep to these rules, and one draw needn't show every extreme that they name: `seq_lengths`: row r holds the lengths of the sequences on device r in its first slots and zeros after them; they sum to at most 256; a row with one sequence has length 256, and some row in every draw is such.
All inputs are finite; a program needn't handle non-finite values.
Results may differ from the reference program's by a relative error of at most 0.018.
Values may be sent and summed in bfloat16 or wider, within the bound.
No kernel may reach another device: no remote copies, remote signals or barrier semaphores. Data moves between devices by JAX's collectives and lax.ppermute only.
A program may use at most 320 MiB of HBM per device.

```python
import math
import jax
import jax.numpy as jnp
from jax import lax

D = 1024
HEAD_DIM = 64
FF = 4096
TOK_DEV = 256
SLOTS = 4
LAYERS = 2
GROUPS = 32
TOKENS = 8192


def draw_seq_lengths(key, part):
    count_key, length_key, chosen_key = jax.random.split(key, 3)
    seq_count = jax.random.randint(count_key, (GROUPS,), 1, SLOTS + 1)
    chosen = jax.random.randint(chosen_key, (), 0, GROUPS)
    seq_count = jnp.where(jnp.arange(GROUPS) == chosen, 1, seq_count)
    short_len = jax.random.randint(length_key, (GROUPS, SLOTS), max(TOK_DEV // 8, 1), TOK_DEV // SLOTS + 1)
    slot_index = jnp.arange(SLOTS)[None, :]
    lengths_out = jnp.where(slot_index < seq_count[:, None], short_len, 0)
    lengths_out = jnp.where(seq_count[:, None] == 1, jnp.where(slot_index == 0, TOK_DEV, 0), lengths_out)
    return lengths_out.astype(jnp.int32)


def draw_att_master(key, part):
    base_normal = jnp.clip(jax.random.normal(key, (D, 4 * D), jnp.float32), -6.0, 6.0)
    column = jnp.arange(4 * D)[None, :]
    return base_normal * jnp.where(column < 3 * D, 1.0, 8.0) / math.sqrt(D)


def draw_ffn_master(key, part):
    base_normal = jnp.clip(jax.random.normal(key, (2, D, FF), jnp.float32), -6.0, 6.0)
    which = jnp.arange(2)[:, None, None]
    return base_normal * jnp.where(which == 0, 1.0 / math.sqrt(D), 1.0 / math.sqrt(FF))


def draw_norm_master(key, part):
    base_normal = jnp.clip(jax.random.normal(key, (4, D), jnp.float32), -6.0, 6.0)
    which = jnp.arange(4)[:, None]
    return jnp.where(which % 2 == 0, 1.0 + 0.1 * base_normal, 0.3 * base_normal)


def shard_levels(stream_key, shape, pieces, low, high):
    loudness = 1.0
    for dim, shards_of in pieces:
        steps = jax.random.uniform(jax.random.fold_in(jax.random.fold_in(stream_key, 6), dim), (shards_of,), jnp.float32, low / len(pieces), high / len(pieces))
        loudness = loudness * jnp.repeat(jnp.exp(steps), shape[dim] // shards_of).reshape((-1,) + (1,) * (len(shape) - 1 - dim))
    return loudness


def centred(own_key, dims, width, most, cuts=(), kind=jnp.bfloat16):
    loudness = shard_levels(own_key, dims, cuts, -0.22, 0.18) if cuts else 1.0
    result = jax.random.normal(own_key, dims, jnp.float32) * width * loudness
    return jnp.minimum(jnp.maximum(result, -most), most).astype(kind)


def setup_inputs(seed: int = 0) -> dict:
    arg_keys = jax.random.split(jax.random.key(seed), 13)
    tokens = centred(arg_keys[0], (TOKENS, D), 1.0, 6.0, ((0, 32),))
    cotangent = centred(arg_keys[1], (TOKENS, D), 1.0, 6.0, ((0, 32),))
    seq_lengths = draw_seq_lengths(jax.random.fold_in(arg_keys[12], 71), 0)
    att_master = draw_att_master(jax.random.fold_in(arg_keys[12], 71), 0)
    ffn_master = draw_ffn_master(jax.random.fold_in(arg_keys[12], 71), 0)
    norm_master = draw_norm_master(jax.random.fold_in(arg_keys[12], 71), 0)
    att_moment = centred(arg_keys[6], (D, 4 * D), (0.02 * TOKENS ** 0.5), 6.0, ((0, 32),), jnp.float32)
    ffn_moment = centred(arg_keys[7], (2, D, FF), (0.03 * TOKENS ** 0.5), 16.0, ((1, 32),), jnp.float32)
    norm_moment = centred(arg_keys[8], (4, D), (0.1 * TOKENS ** 0.5), 56.0, ((1, 32),), jnp.float32)
    att_average = centred(arg_keys[9], (D, 4 * D), 0.05, 0.75, ((0, 32),), jnp.float32)
    ffn_average = centred(arg_keys[10], (2, D, FF), 0.03, 0.4375, ((1, 32),), jnp.float32)
    norm_average = centred(arg_keys[11], (4, D), 0.5, 6.0, ((1, 32),), jnp.float32)
    return {"tokens": tokens, "cotangent": cotangent, "seq_lengths": seq_lengths, "att_master": att_master, "ffn_master": ffn_master, "norm_master": norm_master, "att_moment": att_moment, "ffn_moment": ffn_moment, "norm_moment": norm_moment, "att_average": att_average, "ffn_average": ffn_average, "norm_average": norm_average}


highest_mode = lax.Precision.HIGHEST

@jax.custom_vjp
def low(v):
    return lax.optimization_barrier(v.astype(jnp.bfloat16)).astype(jnp.float32)

@jax.custom_vjp
def low_back(v):
    return v

def low_keep(v):
    return (low(v), None)

def low_pass(kept, grad):
    return (grad,)

def back_keep(v):
    return (v, None)

def back_low(kept, grad):
    return (low(grad),)
low.defvjp(low_keep, low_pass)
low_back.defvjp(back_keep, back_low)

def rounded_copy(weight_in):
    return lax.optimization_barrier(weight_in.astype(jnp.bfloat16)).astype(jnp.float32)

def normalize(values_in, gain_row, bias_row):
    centered = values_in - lax.optimization_barrier(jnp.mean(values_in, axis=-1, keepdims=True))
    spread = lax.optimization_barrier(jnp.mean(centered * centered, axis=-1, keepdims=True))
    return centered * lax.rsqrt(spread + 1e-05) * gain_row + bias_row

def layer_block(rows_in, segment, att_full, ffn_full, norm_full):
    model_width = att_full.shape[0]
    row_count = rows_in.shape[0]
    rows_low = low(rows_in)
    qkv_rows = low(low_back(jnp.dot(rows_low, att_full[:, :3 * model_width], precision=highest_mode)))
    head_rows = qkv_rows.reshape(row_count, 3, model_width // HEAD_DIM, HEAD_DIM)
    query_rows = head_rows[:, 0]
    key_rows = head_rows[:, 1]
    value_rows = head_rows[:, 2]
    scores = low_back(jnp.einsum('qhd,khd->hqk', query_rows, key_rows, precision=highest_mode) * HEAD_DIM ** (-0.5))
    same_seq = segment[:, None] == segment[None, :]
    softmax_rows = jax.nn.softmax(jnp.where(same_seq[None], scores, -1e+30), axis=-1)
    mixed_rows = jnp.einsum('hqk,khd->qhd', low(softmax_rows), value_rows, precision=highest_mode).reshape(row_count, model_width)
    mixed_rows = low(low_back(mixed_rows))
    branch = low_back(jnp.dot(mixed_rows, att_full[:, 3 * model_width:], precision=highest_mode))
    hidden = normalize(rows_in + branch, norm_full[0], norm_full[1])
    inner_rows = low_back(jnp.dot(low(hidden), ffn_full[0], precision=highest_mode))
    active = low(jax.nn.gelu(inner_rows, approximate=True))
    ffn_rows = low_back(jnp.einsum('tf,df->td', active, ffn_full[1], precision=highest_mode))
    return normalize(hidden + ffn_rows, norm_full[2], norm_full[3])

def update(gradient, master, moment, average, step_rate):
    moment_new = 0.9 * moment + gradient
    master_new = master - step_rate * (gradient + 0.9 * moment_new)
    average_new = 0.8 * average + 0.2 * master_new
    return (gradient, moment_new, master_new, average_new, master_new.astype(jnp.bfloat16))

def reference(tokens, cotangent, seq_lengths, att_master, ffn_master, norm_master, att_moment, ffn_moment, norm_moment, att_average, ffn_average, norm_average):
    seq_ends = jnp.cumsum(seq_lengths, axis=1).astype(jnp.int32)
    position = jnp.arange(TOK_DEV, dtype=jnp.int32)
    segment = lax.optimization_barrier(jnp.sum((position[None, :, None] >= seq_ends[:, None, :]).astype(jnp.int32), axis=2)).astype(jnp.int32)
    live_rows = (position[None, :] < seq_ends[:, -1:]).astype(jnp.float32).reshape(TOKENS, 1)
    run_layer = jax.checkpoint(layer_block)

    def forward(rows_in, att_full, ffn_full, norm_full):
        blocks_now = rows_in.reshape(GROUPS, TOK_DEV, D)
        for depth in range(LAYERS):
            blocks_now = lax.map(lambda group_item: run_layer(group_item[0], group_item[1], att_full, ffn_full, norm_full), (blocks_now, segment))
        return blocks_now.reshape(TOKENS, D)
    layer_output, backward = jax.vjp(forward, tokens.astype(jnp.float32), rounded_copy(att_master), rounded_copy(ffn_master), rounded_copy(norm_master))
    input_grad, att_grad, ffn_grad, norm_grad = backward(cotangent.astype(jnp.float32) * live_rows)
    step_rate = 0.1 / math.sqrt(TOKENS)
    att_out = update(att_grad, att_master, att_moment, att_average, step_rate)
    ffn_out = update(ffn_grad, ffn_master, ffn_moment, ffn_average, step_rate)
    norm_out = update(norm_grad, norm_master, norm_moment, norm_average, step_rate)
    return (layer_output.astype(jnp.bfloat16), input_grad, att_out[0], att_out[1], att_out[2], att_out[3], att_out[4], ffn_out[0], ffn_out[1], ffn_out[2], ffn_out[3], ffn_out[4], norm_out[0], norm_out[1], norm_out[2], norm_out[3], norm_out[4])
```

```python
import math

import jax
import jax.numpy as jnp
from jax import lax
from jax.sharding import PartitionSpec as P

HEAD_DIM = 64
LAYERS = 2


head_group = 4


def normalize(values_in, gain_row, bias_row):
    centered = values_in - jnp.mean(values_in, axis=-1, keepdims=True)
    spread = jnp.mean(centered * centered, axis=-1, keepdims=True)
    return centered * lax.rsqrt(spread + 1e-05) * gain_row + bias_row


def gelu_tanh(inner_value):
    return jax.nn.gelu(inner_value, approximate=True)


def split_heads(head_block):
    return head_block.reshape(head_block.shape[0], -1, head_group, HEAD_DIM).transpose(1, 0, 2, 3)


def merge_heads(head_block):
    return head_block.transpose(1, 0, 2, 3).reshape(head_block.shape[1], -1)


def softmax_of(query_rows, key_rows, same_seq):
    scores = jnp.einsum(
        "qhd,khd->hqk", query_rows, key_rows, preferred_element_type=jnp.float32
    ) * HEAD_DIM ** (-0.5)
    scores = jnp.where(same_seq[None], scores, -1e30)
    row_peak = jnp.max(scores, axis=-1, keepdims=True)
    weights = jnp.exp(scores - row_peak)
    return weights / jnp.sum(weights, axis=-1, keepdims=True)


def head_parts(qkv_rows):
    model_width = qkv_rows.shape[1] // 3
    return (
        split_heads(qkv_rows[:, :model_width]),
        split_heads(qkv_rows[:, model_width : 2 * model_width]),
        split_heads(qkv_rows[:, 2 * model_width :]),
    )


def attend(qkv_rows, same_seq):

    def one_group(group_item):
        query_rows, key_rows, value_rows = group_item
        softmax_rows = softmax_of(query_rows, key_rows, same_seq)
        return jnp.einsum(
            "hqk,khd->qhd",
            softmax_rows.astype(jnp.bfloat16),
            value_rows,
            preferred_element_type=jnp.float32,
        )

    return merge_heads(lax.map(one_group, head_parts(qkv_rows)))


def attend_back(qkv_rows, grad_mixed, same_seq):
    query_all, key_all, value_all = head_parts(qkv_rows)

    def one_group(group_item):
        query_rows, key_rows, value_rows, grad_rows = group_item
        softmax_rows = softmax_of(query_rows, key_rows, same_seq)
        grad_probs = jnp.einsum(
            "qhd,khd->hqk", grad_rows, value_rows, preferred_element_type=jnp.float32
        )
        grad_value = jnp.einsum(
            "hqk,qhd->khd",
            softmax_rows.astype(jnp.bfloat16),
            grad_rows,
            preferred_element_type=jnp.float32,
        )
        grad_scores = softmax_rows * (
            grad_probs - jnp.sum(softmax_rows * grad_probs, axis=-1, keepdims=True)
        )
        grad_low = grad_scores.astype(jnp.bfloat16)
        grad_query = jnp.einsum(
            "hqk,khd->qhd", grad_low, key_rows, preferred_element_type=jnp.float32
        ) * HEAD_DIM ** (-0.5)
        grad_key = jnp.einsum(
            "hqk,qhd->khd", grad_low, query_rows, preferred_element_type=jnp.float32
        ) * HEAD_DIM ** (-0.5)
        return (grad_query, grad_key, grad_value)

    grad_query, grad_key, grad_value = lax.map(
        one_group, (query_all, key_all, value_all, split_heads(grad_mixed))
    )
    return jnp.concatenate(
        [merge_heads(grad_query), merge_heads(grad_key), merge_heads(grad_value)], axis=1
    ).astype(jnp.bfloat16)


def layer_states(rows_in, weights, same_seq):
    att_full, ffn_full, norm_full = weights
    model_width = att_full.shape[0]
    norm_values = norm_full.astype(jnp.float32)
    rows_low = rows_in.astype(jnp.bfloat16)
    qkv_rows = jnp.dot(
        rows_low, att_full[:, : 3 * model_width], preferred_element_type=jnp.float32
    ).astype(jnp.bfloat16)
    mixed_rows = attend(qkv_rows, same_seq).astype(jnp.bfloat16)
    branch = jnp.dot(mixed_rows, att_full[:, 3 * model_width :], preferred_element_type=jnp.float32)
    first_sum = rows_in + branch
    hidden = normalize(first_sum, norm_values[0], norm_values[1])
    hidden_low = hidden.astype(jnp.bfloat16)
    inner_rows = jnp.dot(hidden_low, ffn_full[0], preferred_element_type=jnp.float32)
    active = gelu_tanh(inner_rows).astype(jnp.bfloat16)
    second = hidden + jnp.einsum(
        "tf,df->td", active, ffn_full[1], preferred_element_type=jnp.float32
    )
    return (rows_low, qkv_rows, mixed_rows, first_sum, hidden_low, inner_rows, active, second)


def layer_back(states, weights, same_seq, grad_out):
    att_full, ffn_full, norm_full = weights
    model_width = att_full.shape[0]
    norm_values = norm_full.astype(jnp.float32)
    rows_low, qkv_rows, mixed_rows, first_sum, hidden_low, inner_rows, active, second = (
        states
    )
    second_value, second_back = jax.vjp(normalize, second, norm_values[2], norm_values[3])
    grad_second, grad_gain2, grad_bias2 = second_back(grad_out)
    grad_ffn_out = grad_second.astype(jnp.bfloat16)
    grad_active = jnp.dot(grad_ffn_out, ffn_full[1], preferred_element_type=jnp.float32)
    gelu_value, gelu_back = jax.vjp(gelu_tanh, inner_rows)
    grad_inner = gelu_back(grad_active)[0].astype(jnp.bfloat16)
    grad_hidden = grad_second + jnp.einsum(
        "tf,df->td", grad_inner, ffn_full[0], preferred_element_type=jnp.float32
    )
    first_value, first_back = jax.vjp(normalize, first_sum, norm_values[0], norm_values[1])
    grad_first, grad_gain1, grad_bias1 = first_back(grad_hidden)
    grad_branch = grad_first.astype(jnp.bfloat16)
    grad_mixed = jnp.einsum(
        "te,de->td", grad_branch, att_full[:, 3 * model_width :], preferred_element_type=jnp.float32
    ).astype(jnp.bfloat16)
    grad_qkv = attend_back(qkv_rows, grad_mixed, same_seq)
    grad_rows = grad_first + jnp.einsum(
        "te,de->td", grad_qkv, att_full[:, : 3 * model_width], preferred_element_type=jnp.float32
    )
    factors = (
        (grad_ffn_out, active),
        (hidden_low, grad_inner),
        (mixed_rows, grad_branch),
        (rows_low, grad_qkv),
    )
    return (grad_rows, factors, jnp.stack([grad_gain1, grad_bias1, grad_gain2, grad_bias2]))


def weight_sum(layer_pairs):
    left = jnp.concatenate([pair[0] for pair in layer_pairs])
    right = jnp.concatenate([pair[1] for pair in layer_pairs])
    return jnp.einsum("td,tf->df", left, right, preferred_element_type=jnp.float32).astype(
        jnp.bfloat16
    )


def fetch_forward(pieces):
    return (
        lax.all_gather(pieces[0], ("dp", "fsdp"), axis=0, tiled=True),
        lax.all_gather(pieces[1], ("dp", "fsdp"), axis=1, tiled=True),
        lax.all_gather(pieces[2], ("dp", "fsdp"), axis=1, tiled=True),
    )


def owner_sum(term, dim):
    return lax.psum_scatter(term, ("dp", "fsdp"), scatter_dimension=dim, tiled=True).astype(
        jnp.float32
    )


def update(gradient, master, moment, average, step_rate):
    moment_new = 0.9 * moment + gradient
    master_new = master - step_rate * (gradient + 0.9 * moment_new)
    average_new = 0.8 * average + 0.2 * master_new
    return (gradient, moment_new, master_new, average_new, master_new.astype(jnp.bfloat16))


def shards(
    tokens,
    cotangent,
    seq_lengths,
    att_master,
    ffn_master,
    norm_master,
    att_moment,
    ffn_moment,
    norm_moment,
    att_average,
    ffn_average,
    norm_average,
):
    row_count = tokens.shape[0]
    lengths = [seq_lengths[0, slot] for slot in range(seq_lengths.shape[1])]
    seq_ends = jnp.stack([sum(lengths[: slot + 1]) for slot in range(len(lengths))])
    position = jnp.arange(row_count, dtype=jnp.int32)
    segment = jnp.sum((position[:, None] >= seq_ends[None, :]).astype(jnp.int32), axis=1)
    same_seq = segment[:, None] == segment[None, :]
    live_rows = (position < seq_ends[-1]).astype(jnp.float32)[:, None]
    pieces = (
        att_master.astype(jnp.bfloat16),
        ffn_master.astype(jnp.bfloat16),
        norm_master.astype(jnp.bfloat16),
    )
    weights = fetch_forward(pieces)
    norm_values = weights[2].astype(jnp.float32)
    stored = []
    current = tokens.astype(jnp.float32)
    for depth in range(LAYERS):
        stored.append(layer_states(current, weights, same_seq))
        current = normalize(stored[depth][7], norm_values[2], norm_values[3])
    grad_now = cotangent.astype(jnp.float32) * live_rows
    factors, norm_term = [], 0.0
    for depth in reversed(range(LAYERS)):
        grad_now, pairs, norm_part = layer_back(stored[depth], weights, same_seq, grad_now)
        factors.append(pairs)
        norm_term = norm_term + norm_part
    down, up, proj, inproj = [weight_sum(pairs) for pairs in zip(*factors)]
    ffn_total = jnp.stack([owner_sum(up, 0), owner_sum(down, 0)])
    att_total = owner_sum(jnp.concatenate([inproj, proj], axis=1), 0)
    totals = (att_total, ffn_total, owner_sum(norm_term, 1))
    step_rate = 0.1 / math.sqrt(row_count * lax.axis_size(("dp", "fsdp")))
    att_out = update(totals[0], att_master, att_moment, att_average, step_rate)
    ffn_out = update(totals[1], ffn_master, ffn_moment, ffn_average, step_rate)
    norm_out = update(totals[2], norm_master, norm_moment, norm_average, step_rate)
    return (
        current.astype(jnp.bfloat16),
        grad_now,
        att_out[0],
        att_out[1],
        att_out[2],
        att_out[3],
        att_out[4],
        ffn_out[0],
        ffn_out[1],
        ffn_out[2],
        ffn_out[3],
        ffn_out[4],
        norm_out[0],
        norm_out[1],
        norm_out[2],
        norm_out[3],
        norm_out[4],
    )


def solution(mesh):
    return jax.shard_map(
        shards,
        mesh=mesh,
        in_specs=(
            P(("dp", "fsdp"), None),
            P(("dp", "fsdp"), None),
            P(("dp", "fsdp"), None),
            P(("dp", "fsdp"), None),
            P(None, ("dp", "fsdp"), None),
            P(None, ("dp", "fsdp")),
            P(("dp", "fsdp"), None),
            P(None, ("dp", "fsdp"), None),
            P(None, ("dp", "fsdp")),
            P(("dp", "fsdp"), None),
            P(None, ("dp", "fsdp"), None),
            P(None, ("dp", "fsdp")),
        ),
        out_specs=(
            P(("dp", "fsdp"), None),
            P(("dp", "fsdp"), None),
            P(("dp", "fsdp"), None),
            P(("dp", "fsdp"), None),
            P(("dp", "fsdp"), None),
            P(("dp", "fsdp"), None),
            P(("dp", "fsdp"), None),
            P(None, ("dp", "fsdp"), None),
            P(None, ("dp", "fsdp"), None),
            P(None, ("dp", "fsdp"), None),
            P(None, ("dp", "fsdp"), None),
            P(None, ("dp", "fsdp"), None),
            P(None, ("dp", "fsdp")),
            P(None, ("dp", "fsdp")),
            P(None, ("dp", "fsdp")),
            P(None, ("dp", "fsdp")),
            P(None, ("dp", "fsdp")),
        ),
        check_vma=False,
    )
```

```python
import functools
import math

import jax
import jax.numpy as jnp
from jax import lax
from jax.experimental import pallas as pl
from jax.experimental.pallas import tpu as pltpu
from jax.sharding import PartitionSpec as P

HEAD_DIM = 64
LAYERS = 2


head_group = 4


def normalize(values_in, gain_row, bias_row):
    centered = values_in - jnp.mean(values_in, axis=-1, keepdims=True)
    spread = jnp.mean(centered * centered, axis=-1, keepdims=True)
    return centered * lax.rsqrt(spread + 1e-05) * gain_row + bias_row


def gelu_tanh(inner_value):
    return jax.nn.gelu(inner_value, approximate=True)


def split_heads(head_block):
    return head_block.reshape(head_block.shape[0], -1, head_group, HEAD_DIM).transpose(1, 0, 2, 3)


def merge_heads(head_block):
    return head_block.transpose(1, 0, 2, 3).reshape(head_block.shape[1], -1)


def softmax_of(query_rows, key_rows, same_seq):
    scores = jnp.einsum(
        "qhd,khd->hqk", query_rows, key_rows, preferred_element_type=jnp.float32
    ) * HEAD_DIM ** (-0.5)
    scores = jnp.where(same_seq[None], scores, -1e30)
    row_peak = jnp.max(scores, axis=-1, keepdims=True)
    weights = jnp.exp(scores - row_peak)
    return weights / jnp.sum(weights, axis=-1, keepdims=True)


def head_parts(qkv_rows):
    model_width = qkv_rows.shape[1] // 3
    return (
        split_heads(qkv_rows[:, :model_width]),
        split_heads(qkv_rows[:, model_width : 2 * model_width]),
        split_heads(qkv_rows[:, 2 * model_width :]),
    )


def attend(qkv_rows, same_seq):

    def one_group(group_item):
        query_rows, key_rows, value_rows = group_item
        softmax_rows = softmax_of(query_rows, key_rows, same_seq)
        return jnp.einsum(
            "hqk,khd->qhd",
            softmax_rows.astype(jnp.bfloat16),
            value_rows,
            preferred_element_type=jnp.float32,
        )

    return merge_heads(lax.map(one_group, head_parts(qkv_rows)))


def attend_back(qkv_rows, grad_mixed, same_seq):
    query_all, key_all, value_all = head_parts(qkv_rows)

    def one_group(group_item):
        query_rows, key_rows, value_rows, grad_rows = group_item
        softmax_rows = softmax_of(query_rows, key_rows, same_seq)
        grad_probs = jnp.einsum(
            "qhd,khd->hqk", grad_rows, value_rows, preferred_element_type=jnp.float32
        )
        grad_value = jnp.einsum(
            "hqk,qhd->khd",
            softmax_rows.astype(jnp.bfloat16),
            grad_rows,
            preferred_element_type=jnp.float32,
        )
        grad_scores = softmax_rows * (
            grad_probs - jnp.sum(softmax_rows * grad_probs, axis=-1, keepdims=True)
        )
        grad_low = grad_scores.astype(jnp.bfloat16)
        grad_query = jnp.einsum(
            "hqk,khd->qhd", grad_low, key_rows, preferred_element_type=jnp.float32
        ) * HEAD_DIM ** (-0.5)
        grad_key = jnp.einsum(
            "hqk,qhd->khd", grad_low, query_rows, preferred_element_type=jnp.float32
        ) * HEAD_DIM ** (-0.5)
        return (grad_query, grad_key, grad_value)

    grad_query, grad_key, grad_value = lax.map(
        one_group, (query_all, key_all, value_all, split_heads(grad_mixed))
    )
    return jnp.concatenate(
        [merge_heads(grad_query), merge_heads(grad_key), merge_heads(grad_value)], axis=1
    ).astype(jnp.bfloat16)


def layer_states(rows_in, weights, same_seq):
    att_full, ffn_full, norm_full = weights
    model_width = att_full.shape[0]
    norm_values = norm_full.astype(jnp.float32)
    rows_low = rows_in.astype(jnp.bfloat16)
    qkv_rows = jnp.dot(
        rows_low, att_full[:, : 3 * model_width], preferred_element_type=jnp.float32
    ).astype(jnp.bfloat16)
    mixed_rows = attend(qkv_rows, same_seq).astype(jnp.bfloat16)
    branch = jnp.dot(mixed_rows, att_full[:, 3 * model_width :], preferred_element_type=jnp.float32)
    first_sum = rows_in + branch
    hidden = normalize(first_sum, norm_values[0], norm_values[1])
    hidden_low = hidden.astype(jnp.bfloat16)
    inner_rows = jnp.dot(hidden_low, ffn_full[0], preferred_element_type=jnp.float32)
    active = gelu_tanh(inner_rows).astype(jnp.bfloat16)
    second = hidden + jnp.einsum(
        "tf,df->td", active, ffn_full[1], preferred_element_type=jnp.float32
    )
    return (rows_low, qkv_rows, mixed_rows, first_sum, hidden_low, inner_rows, active, second)


def layer_back(states, weights, same_seq, grad_out):
    att_full, ffn_full, norm_full = weights
    model_width = att_full.shape[0]
    norm_values = norm_full.astype(jnp.float32)
    rows_low, qkv_rows, mixed_rows, first_sum, hidden_low, inner_rows, active, second = (
        states
    )
    second_value, second_back = jax.vjp(normalize, second, norm_values[2], norm_values[3])
    grad_second, grad_gain2, grad_bias2 = second_back(grad_out)
    grad_ffn_out = grad_second.astype(jnp.bfloat16)
    grad_active = jnp.dot(grad_ffn_out, ffn_full[1], preferred_element_type=jnp.float32)
    gelu_value, gelu_back = jax.vjp(gelu_tanh, inner_rows)
    grad_inner = gelu_back(grad_active)[0].astype(jnp.bfloat16)
    grad_hidden = grad_second + jnp.einsum(
        "tf,df->td", grad_inner, ffn_full[0], preferred_element_type=jnp.float32
    )
    first_value, first_back = jax.vjp(normalize, first_sum, norm_values[0], norm_values[1])
    grad_first, grad_gain1, grad_bias1 = first_back(grad_hidden)
    grad_branch = grad_first.astype(jnp.bfloat16)
    grad_mixed = jnp.einsum(
        "te,de->td", grad_branch, att_full[:, 3 * model_width :], preferred_element_type=jnp.float32
    ).astype(jnp.bfloat16)
    grad_qkv = attend_back(qkv_rows, grad_mixed, same_seq)
    grad_rows = grad_first + jnp.einsum(
        "te,de->td", grad_qkv, att_full[:, : 3 * model_width], preferred_element_type=jnp.float32
    )
    factors = (
        (grad_ffn_out, active),
        (hidden_low, grad_inner),
        (mixed_rows, grad_branch),
        (rows_low, grad_qkv),
    )
    return (grad_rows, factors, jnp.stack([grad_gain1, grad_bias1, grad_gain2, grad_bias2]))


def weight_sum(layer_pairs, picker):
    left = jnp.concatenate([pair[0] for pair in layer_pairs])
    right = jnp.concatenate([pair[1] for pair in layer_pairs])
    left = jnp.dot(left, picker, preferred_element_type=jnp.float32).astype(jnp.bfloat16)
    return [
        jnp.einsum("td,tf->df", part, right, preferred_element_type=jnp.float32).astype(jnp.bfloat16)
        for part in jnp.split(left, 2, axis=1)
    ]


AXES = ("dp", "fsdp")
NORM_COLS = 128


class Route:
    def __init__(self):
        rows, cols = lax.axis_size("dp"), lax.axis_size("fsdp")
        self.inner = cols // 4
        self.ring_size = rows // 2 * self.inner
        self.cols = cols
        self.world = rows * cols
        row, col = lax.axis_index("dp"), lax.axis_index("fsdp")
        self.q = row // 2 * self.inner + col // 4
        self.y, self.x, self.c = row % 2, col // 2 % 2, col % 2

    def joint(self, q, y, x, c):
        return (q // self.inner * 2 + y) * self.cols + q % self.inner * 4 + x * 2 + c

    def move(self, array, step):
        pairs = []
        for q in range(self.ring_size):
            for y in (0, 1):
                for x in (0, 1):
                    for c in (0, 1):
                        to = step(q, y, x, c)
                        pairs.append((self.joint(q, y, x, c), self.joint(*to)))
        return lax.ppermute(array, AXES, pairs)

    def ring(self, array):
        return self.move(array, lambda q, y, x, c: ((q + 1) % self.ring_size, y, x, c))

    def core(self, array):
        return self.move(array, lambda q, y, x, c: (q, y, x, 1 - c))

    def first(self, array):
        return self.move(array, lambda q, y, x, c: (q, y ^ c, x ^ (1 - c), c))

    def second(self, array):
        return self.move(array, lambda q, y, x, c: (q, y ^ (1 - c), x ^ c, c))

    def owner(self, back, first, second, core):
        c = self.c ^ core
        x = self.x ^ jnp.where(c == 0, first, second)
        y = self.y ^ jnp.where(c == 0, second, first)
        return self.joint((self.q + self.ring_size - back) % self.ring_size, y, x, c)


def gather_ring_first(route, piece):
    slots = [piece]
    for _ in range(route.ring_size - 1):
        slots.append(route.ring(slots[-1]))
    base = jnp.concatenate(slots)
    blocks = [(base, 0, 0), (route.first(base), 1, 0)]
    blocks += [(route.second(block), first, 1) for block, first, _ in blocks]
    arrays, owners = [], []
    for core in (0, 1):
        for block, first, second in blocks:
            arrays.append(route.core(block) if core else block)
            owners += [route.owner(i, first, second, core) for i in range(route.ring_size)]
    return arrays, owners


def gather_ring_middle(route, piece):
    pair = jnp.concatenate([piece, route.first(piece)])
    arrays, owners = [], []
    for i in range(route.ring_size):
        if i:
            pair = route.ring(pair)
        other = route.second(pair)
        for core in (0, 1):
            for second, block in ((0, pair), (1, other)):
                arrays.append(route.core(block) if core else block)
                owners += [route.owner(i, first, second, core) for first in (0, 1)]
    return arrays, owners


def place_kernel(owners_ref, *refs, widths):
    count = len(refs) - len(widths) - 2
    parts, outs, whole, sem = refs[:count], refs[count:-2], refs[-2], refs[-1]
    shard = whole.shape[0] // owners_ref.shape[0]
    copies = []
    for part in parts:
        for local in range(part.shape[0] // shard):
            row = pl.multiple_of(owners_ref[len(copies)] * shard, shard)
            copies.append(
                pltpu.make_async_copy(
                    part.at[pl.ds(local * shard, shard)],
                    whole.at[pl.ds(row, shard)],
                    sem.at[len(copies)],
                )
            )
    for copy in copies:
        copy.start()
    for copy in copies:
        copy.wait()
    column = 0
    copies = []
    for out, width in zip(outs, widths):
        copies.append(
            pltpu.make_async_copy(whole.at[:, pl.ds(column, width)], out, sem.at[len(copies)])
        )
        column += width
    for copy in copies:
        copy.start()
    for copy in copies:
        copy.wait()


def place_rows(arrays, owners, widths):
    owners = jnp.stack(owners).astype(jnp.int32)
    rows = sum(array.shape[0] for array in arrays)
    anywhere = pl.BlockSpec(memory_space=pl.ANY)
    kind = arrays[0].dtype
    return pl.pallas_call(
        functools.partial(place_kernel, widths=widths),
        out_shape=[jax.ShapeDtypeStruct((rows, width), kind) for width in widths],
        in_specs=[pl.BlockSpec(memory_space=pltpu.SMEM)] + [anywhere] * len(arrays),
        out_specs=[anywhere] * len(widths),
        scratch_shapes=[
            pltpu.VMEM((rows, sum(widths)), kind),
            pltpu.SemaphoreType.DMA((owners.size,)),
        ],
        cost_estimate=pl.CostEstimate(
            flops=0, bytes_accessed=4 * rows * sum(widths), transcendentals=0
        ),
        compiler_params=pltpu.CompilerParams(vmem_limit_bytes=16 * 2**20),
    )(owners, *arrays)


def row_picker(owners, shard):
    rows = (jnp.stack(owners)[:, None] * shard + jnp.arange(shard)[None, :]).reshape(1, -1)
    return (jnp.arange(rows.size)[:, None] == rows).astype(jnp.bfloat16)


def add_low(left, right):
    return (left.astype(jnp.float32) + right.astype(jnp.float32)).astype(jnp.bfloat16)


def owners_ring_last(route):
    return [
        route.owner(1 + j, first, second, core)
        for core in (1, 0)
        for second in (1, 0)
        for first in (1, 0)
        for j in range(route.ring_size)
    ]


def scatter_ring_last(route, send, keep):
    for step in (route.core, route.second):
        arrived = step(send)
        half = keep.shape[0] // 2
        send, keep = add_low(keep[:half], arrived[:half]), add_low(keep[half:], arrived[half:])
    arrived = route.first(send)
    pieces = [
        add_low(a, b) for a, b in zip(cut(keep, route.ring_size), cut(arrived, route.ring_size))
    ]
    moving = pieces[0]
    for piece in pieces[1:-1]:
        moving = add_low(piece, route.ring(moving))
    return pieces[-1].astype(jnp.float32) + route.ring(moving).astype(jnp.float32)


def owners_ring_middle(route):
    return [
        route.owner(1 + j, first, second, core)
        for core in (1, 0)
        for second in (1, 0)
        for j in range(route.ring_size)
        for first in (1, 0)
    ]


def cut(array, count):
    size = array.shape[0] // count
    return [array[k * size : (k + 1) * size] for k in range(count)]


def scatter_whole(route, upper, lower):
    return lax.psum_scatter(
        jnp.concatenate([upper, lower]), AXES, scatter_dimension=0, tiled=True
    ).astype(jnp.float32)


def scatter_ring_middle(route, send, keep):
    arrived = route.core(send)
    half = keep.shape[0] // 2
    pieces = route.ring_size
    sends = [
        add_low(a, b) for a, b in zip(cut(keep[:half], pieces), cut(arrived[:half], pieces))
    ]
    keeps = [
        add_low(a, b) for a, b in zip(cut(keep[half:], pieces), cut(arrived[half:], pieces))
    ]
    moving = None
    for j in range(pieces):
        local = add_low(keeps[j], route.second(sends[j]))
        moving = local if moving is None else add_low(local, route.ring(moving))
    shard = moving.shape[0] // 2
    return moving[shard:].astype(jnp.float32) + route.first(moving[:shard]).astype(jnp.float32)


def update(gradient, master, moment, average, step_rate):
    moment_new = 0.9 * moment + gradient
    master_new = master - step_rate * (gradient + 0.9 * moment_new)
    average_new = 0.8 * average + 0.2 * master_new
    return (gradient, moment_new, master_new, average_new, master_new.astype(jnp.bfloat16))


def shards(
    tokens,
    cotangent,
    seq_lengths,
    att_master,
    ffn_master,
    norm_master,
    att_moment,
    ffn_moment,
    norm_moment,
    att_average,
    ffn_average,
    norm_average,
):
    row_count = tokens.shape[0]
    lengths = [seq_lengths[0, slot] for slot in range(seq_lengths.shape[1])]
    seq_ends = jnp.stack([sum(lengths[: slot + 1]) for slot in range(len(lengths))])
    position = jnp.arange(row_count, dtype=jnp.int32)
    segment = jnp.sum((position[:, None] >= seq_ends[None, :]).astype(jnp.int32), axis=1)
    same_seq = segment[:, None] == segment[None, :]
    live_rows = (position < seq_ends[-1]).astype(jnp.float32)[:, None]
    route = Route()
    shard = att_master.shape[0]
    norm_piece = jnp.pad(norm_master.T, ((0, 0), (0, NORM_COLS - norm_master.shape[0])))
    att_piece = jnp.concatenate([att_master, norm_piece], axis=1).astype(jnp.bfloat16)
    ffn_pieces = ffn_master.astype(jnp.bfloat16)
    width = att_master.shape[1]
    tiled = shard % 16 == 0
    if tiled:
        att_full, norm_full = place_rows(
            *gather_ring_middle(route, att_piece), (width, NORM_COLS)
        )
        [up_full] = place_rows(*gather_ring_middle(route, ffn_pieces[0]), (width,))
        [down_full] = place_rows(*gather_ring_first(route, ffn_pieces[1]), (width,))
    else:
        whole = [
            lax.all_gather(piece, AXES, axis=0, tiled=True)
            for piece in (att_piece, ffn_pieces[0], ffn_pieces[1])
        ]
        att_full, norm_full, up_full, down_full = whole[0][:, :width], whole[0][:, width:], *whole[1:]
    weights = (att_full, (up_full, down_full), norm_full[:, : norm_master.shape[0]].T)
    norm_values = weights[2].astype(jnp.float32)
    stored = []
    current = tokens.astype(jnp.float32)
    for depth in range(LAYERS):
        stored.append(layer_states(current, weights, same_seq))
        current = normalize(stored[depth][7], norm_values[2], norm_values[3])
    grad_now = cotangent.astype(jnp.float32) * live_rows
    factors, norm_term = [], 0.0
    for depth in reversed(range(LAYERS)):
        grad_now, pairs, norm_part = layer_back(stored[depth], weights, same_seq, grad_now)
        factors.append(pairs)
        norm_term = norm_term + norm_part
    downs, ups, projs, inprojs = zip(*factors)
    middle = row_picker(owners_ring_middle(route), shard)
    last = row_picker(owners_ring_last(route), shard)
    scatter_middle, scatter_last = scatter_ring_middle, scatter_ring_last
    if not tiled:
        middle = last = row_picker(list(range(route.world)), shard)
        scatter_middle = scatter_last = scatter_whole
    down_share = scatter_middle(route, *weight_sum(downs, middle))
    up_share = scatter_middle(route, *weight_sum(ups, middle))
    norm_rows = jnp.pad(norm_term.T, ((0, 0), (0, NORM_COLS - norm_term.shape[0])))
    norm_rows = jnp.einsum(
        "dr,dn->rn", last, norm_rows.astype(jnp.bfloat16), preferred_element_type=jnp.float32
    ).astype(jnp.bfloat16)
    att_parts = zip(weight_sum(inprojs, last), weight_sum(projs, last), jnp.split(norm_rows, 2))
    att_halves = [jnp.concatenate(parts, axis=1) for parts in att_parts]
    att_share = scatter_last(route, *att_halves)
    totals = (
        att_share[:, :width],
        jnp.stack([up_share, down_share]),
        att_share[:, width : width + norm_master.shape[0]].T,
    )
    step_rate = 0.1 / math.sqrt(row_count * lax.axis_size(("dp", "fsdp")))
    att_out = update(totals[0], att_master, att_moment, att_average, step_rate)
    ffn_out = update(totals[1], ffn_master, ffn_moment, ffn_average, step_rate)
    norm_out = update(totals[2], norm_master, norm_moment, norm_average, step_rate)
    return (
        current.astype(jnp.bfloat16),
        grad_now,
        att_out[0],
        att_out[1],
        att_out[2],
        att_out[3],
        att_out[4],
        ffn_out[0],
        ffn_out[1],
        ffn_out[2],
        ffn_out[3],
        ffn_out[4],
        norm_out[0],
        norm_out[1],
        norm_out[2],
        norm_out[3],
        norm_out[4],
    )


def solution(mesh):
    return jax.shard_map(
        shards,
        mesh=mesh,
        in_specs=(
            P(("dp", "fsdp"), None),
            P(("dp", "fsdp"), None),
            P(("dp", "fsdp"), None),
            P(("dp", "fsdp"), None),
            P(None, ("dp", "fsdp"), None),
            P(None, ("dp", "fsdp")),
            P(("dp", "fsdp"), None),
            P(None, ("dp", "fsdp"), None),
            P(None, ("dp", "fsdp")),
            P(("dp", "fsdp"), None),
            P(None, ("dp", "fsdp"), None),
            P(None, ("dp", "fsdp")),
        ),
        out_specs=(
            P(("dp", "fsdp"), None),
            P(("dp", "fsdp"), None),
            P(("dp", "fsdp"), None),
            P(("dp", "fsdp"), None),
            P(("dp", "fsdp"), None),
            P(("dp", "fsdp"), None),
            P(("dp", "fsdp"), None),
            P(None, ("dp", "fsdp"), None),
            P(None, ("dp", "fsdp"), None),
            P(None, ("dp", "fsdp"), None),
            P(None, ("dp", "fsdp"), None),
            P(None, ("dp", "fsdp"), None),
            P(None, ("dp", "fsdp")),
            P(None, ("dp", "fsdp")),
            P(None, ("dp", "fsdp")),
            P(None, ("dp", "fsdp")),
            P(None, ("dp", "fsdp")),
        ),
        check_vma=False,
    )
```

```python
import functools
import math

import jax
import jax.numpy as jnp
from jax import lax
from jax.experimental import pallas as pl
from jax.experimental.pallas import tpu as pltpu
from jax.sharding import PartitionSpec as P

HEAD_DIM = 64
LAYERS = 2


LOW = jnp.bfloat16
SCALE = HEAD_DIM ** (-0.5)
PAIR = 2 * HEAD_DIM
TILE = 256
FF_TILE = 512
ROWS = 64
GELU_RATE = math.sqrt(2.0 / math.pi)
ANYWHERE = pl.BlockSpec(memory_space=pl.ANY)
SCALARS = pl.BlockSpec(memory_space=pltpu.SMEM)
VECTORS = pl.BlockSpec(memory_space=pltpu.VMEM)


def product(left, right, left_dim=1, right_dim=0):
    dims = (((left_dim,), (right_dim,)), ((), ()))
    return lax.dot_general(left, right, dims, preferred_element_type=jnp.float32)


def columns(index, width):
    return pl.ds(pl.multiple_of(index * width, width), width)


def column_copy(source, target, sem, index, width):
    part = pl.ds(index * width, width)
    return pltpu.make_async_copy(source.at[:, part], target.at[:, part], sem.at[index])


def fill_mask(lengths_ref, mask_ref):
    shape = mask_ref.shape
    key_row = lax.broadcasted_iota(jnp.int32, shape, 0)
    query_row = lax.broadcasted_iota(jnp.int32, shape, 1)
    end = 0
    key_segment = jnp.zeros(shape, jnp.int32)
    query_segment = jnp.zeros(shape, jnp.int32)
    for slot in range(lengths_ref.shape[1]):
        end = end + lengths_ref[0, slot]
        key_segment += (key_row >= end).astype(jnp.int32)
        query_segment += (query_row >= end).astype(jnp.int32)
    mask_ref[...] = jnp.where(key_segment == query_segment, 0.0, -1e30)


def row_blocks(count, body):
    def step(block, carry):
        body(pl.ds(pl.multiple_of(block * ROWS, ROWS), ROWS))
        return carry

    lax.fori_loop(0, count // ROWS, step, 0)


def normalize(values, gain, bias):
    centered = values - jnp.mean(values, axis=-1, keepdims=True)
    spread = jnp.mean(centered * centered, axis=-1, keepdims=True)
    inverse = lax.rsqrt(spread + 1e-05)
    unit = centered * inverse
    return unit, inverse, unit * gain + bias


def normalize_back(grad, unit, inverse, gain):
    scaled = grad * gain
    mean = jnp.mean(scaled, axis=-1, keepdims=True)
    along = jnp.mean(scaled * unit, axis=-1, keepdims=True)
    return inverse * (scaled - mean - unit * along)


def half_lanes(rows, half):
    lane = lax.broadcasted_iota(jnp.int32, (rows, PAIR), 1)
    return (lane >= HEAD_DIM) == bool(half)


def attend_forward_kernel(
    lengths_ref,
    rows_ref,
    norm_ref,
    weight_ref,
    low_ref,
    qkv_ref,
    mixed_ref,
    lse_ref,
    hidden_ref,
    unit_ref,
    inverse_ref,
    held_ref,
    mask_ref,
    sum_ref,
    sem,
):
    count, width = rows_ref.shape
    chunks = [column_copy(weight_ref, held_ref, sem, k, width) for k in range(4)]
    for copy in chunks:
        copy.start()
    low_ref[...] = rows_ref[...].astype(LOW)
    fill_mask(lengths_ref, mask_ref)
    tiles = width // TILE
    for k in range(3):
        chunks[k].wait()

        def project(tile, carry):
            part = columns(k * tiles + tile, TILE)
            qkv_ref[:, part] = product(low_ref[...], held_ref[:, part]).astype(LOW)
            return carry

        lax.fori_loop(0, tiles, project, 0)

    def one_pair(pair, carry):
        query = qkv_ref[:, columns(pair, PAIR)] * jnp.asarray(SCALE, LOW)
        key = qkv_ref[:, columns(width // PAIR + pair, PAIR)]
        value = qkv_ref[:, columns(2 * width // PAIR + pair, PAIR)]
        halves, sums = [], []
        for half in (0, 1):
            own = jnp.where(half_lanes(count, half), query, jnp.zeros_like(query))
            scores = product(key, own, 1, 1) + mask_ref[...]
            peak = jnp.max(scores, axis=0, keepdims=True)
            weights = jnp.exp(scores - peak)
            total = jnp.sum(weights, axis=0, keepdims=True)
            sums.append(peak + jnp.log(total))
            mixed = product(value, weights.astype(LOW), 0, 0)
            halves.append(mixed[half * HEAD_DIM : (half + 1) * HEAD_DIM] * (1.0 / total))
        lse_ref[pair] = jnp.concatenate(sums, axis=0)
        mixed_ref[:, columns(pair, PAIR)] = jnp.concatenate(halves, axis=0).T.astype(LOW)
        return carry

    lax.fori_loop(0, width // PAIR, one_pair, 0)
    chunks[3].wait()

    def project_out(tile, carry):
        part = columns(tile, TILE)
        branch = product(mixed_ref[...], held_ref[:, columns(3 * tiles + tile, TILE)])
        sum_ref[:, part] = rows_ref[:, part].astype(jnp.float32) + branch
        return carry

    lax.fori_loop(0, tiles, project_out, 0)

    def norm_rows(block):
        unit, inverse, hidden = normalize(sum_ref[block, :], norm_ref[0:1], norm_ref[1:2])
        hidden_ref[block, :] = hidden
        unit_ref[block, :] = unit
        inverse_ref[block, :] = jnp.broadcast_to(inverse, (ROWS, 128))

    row_blocks(count, norm_rows)


def attend_forward(lengths, rows, norm, weight):
    count, width = rows.shape
    shape = jax.ShapeDtypeStruct
    return pl.pallas_call(
        attend_forward_kernel,
        out_shape=[
            shape((count, width), LOW),
            shape((count, 3 * width), LOW),
            shape((count, width), LOW),
            shape((width // PAIR, 2, count), jnp.float32),
            shape((count, width), jnp.float32),
            shape((count, width), jnp.float32),
            shape((count, 128), jnp.float32),
        ],
        in_specs=[SCALARS, VECTORS, VECTORS, ANYWHERE],
        out_specs=[VECTORS] * 7,
        scratch_shapes=[
            pltpu.VMEM(weight.shape, LOW),
            pltpu.VMEM((count, count), jnp.float32),
            pltpu.VMEM((count, width), jnp.float32),
            pltpu.SemaphoreType.DMA((4,)),
        ],
        cost_estimate=pl.CostEstimate(
            flops=2 * count * weight.size + 4 * count * count * width,
            bytes_accessed=2 * weight.size + 20 * count * width,
            transcendentals=count * count * width // HEAD_DIM,
        ),
        compiler_params=pltpu.CompilerParams(vmem_limit_bytes=32 * 2**20),
    )(lengths, rows, norm, weight)


def ffn_forward_kernel(
    hidden_ref,
    norm_ref,
    up_ref,
    down_ref,
    low_ref,
    active_ref,
    slope_ref,
    unit_ref,
    inverse_ref,
    out_ref,
    held_up,
    held_down,
    sum_ref,
    up_sem,
    down_sem,
):
    count, _ = hidden_ref.shape
    tiles = up_ref.shape[1] // FF_TILE
    for tile in range(tiles):
        column_copy(up_ref, held_up, up_sem, tile, FF_TILE).start()
        column_copy(down_ref, held_down, down_sem, tile, FF_TILE).start()
    low_ref[...] = hidden_ref[...].astype(LOW)
    sum_ref[...] = hidden_ref[...]
    for tile in range(tiles):
        part = pl.ds(tile * FF_TILE, FF_TILE)
        column_copy(up_ref, held_up, up_sem, tile, FF_TILE).wait()
        inner = product(low_ref[...], held_up[:, part])
        square = inner * inner
        bend = jnp.tanh(GELU_RATE * inner * (1.0 + 0.044715 * square))
        rise = 0.5 + 0.5 * bend
        active = (inner * rise).astype(LOW)
        active_ref[:, part] = active
        slope = rise + (0.5 * GELU_RATE) * inner * (1.0 - bend * bend) * (
            1.0 + 3 * 0.044715 * square
        )
        slope_ref[:, part] = slope.astype(LOW)
        column_copy(down_ref, held_down, down_sem, tile, FF_TILE).wait()
        sum_ref[...] += product(active, held_down[:, part], 1, 1)

    def norm_rows(block):
        unit, inverse, values = normalize(sum_ref[block, :], norm_ref[2:3], norm_ref[3:4])
        out_ref[block, :] = values.astype(out_ref.dtype)
        unit_ref[block, :] = unit
        inverse_ref[block, :] = jnp.broadcast_to(inverse, (ROWS, 128))

    row_blocks(count, norm_rows)


def ffn_forward(hidden, norm, up, down, out_type):
    count, width = hidden.shape
    inner = up.shape[1]
    tiles = inner // FF_TILE
    shape = jax.ShapeDtypeStruct
    return pl.pallas_call(
        ffn_forward_kernel,
        out_shape=[
            shape((count, width), LOW),
            shape((count, inner), LOW),
            shape((count, inner), LOW),
            shape((count, width), jnp.float32),
            shape((count, 128), jnp.float32),
            shape((count, width), out_type),
        ],
        in_specs=[VECTORS, VECTORS, ANYWHERE, ANYWHERE],
        out_specs=[VECTORS] * 6,
        scratch_shapes=[
            pltpu.VMEM(up.shape, LOW),
            pltpu.VMEM(down.shape, LOW),
            pltpu.VMEM((count, width), jnp.float32),
            pltpu.SemaphoreType.DMA((tiles,)),
            pltpu.SemaphoreType.DMA((tiles,)),
        ],
        cost_estimate=pl.CostEstimate(
            flops=4 * count * up.size,
            bytes_accessed=4 * up.size + 4 * count * inner + 16 * count * width,
            transcendentals=count * inner,
        ),
        compiler_params=pltpu.CompilerParams(vmem_limit_bytes=48 * 2**20),
    )(hidden, norm, up, down)


def ffn_backward_kernel(
    grad_ref,
    unit2_ref,
    inverse2_ref,
    slope_ref,
    unit1_ref,
    inverse1_ref,
    norm_ref,
    up_ref,
    down_ref,
    out_low_ref,
    inner_low_ref,
    first_ref,
    first_low_ref,
    norm_grad_ref,
    held_up,
    held_down,
    sum_ref,
    up_sem,
    down_sem,
):
    count, _ = grad_ref.shape
    tiles = up_ref.shape[1] // FF_TILE
    for tile in range(tiles):
        column_copy(down_ref, held_down, down_sem, tile, FF_TILE).start()
        column_copy(up_ref, held_up, up_sem, tile, FF_TILE).start()
    norm_grad_ref[...] = jnp.zeros_like(norm_grad_ref)

    def second_norm(block):
        grad, unit = grad_ref[block, :], unit2_ref[block, :]
        norm_grad_ref[2:3] += jnp.sum(grad * unit, axis=0, keepdims=True)
        norm_grad_ref[3:4] += jnp.sum(grad, axis=0, keepdims=True)
        second = normalize_back(grad, unit, inverse2_ref[block, 0:1], norm_ref[2:3])
        sum_ref[block, :] = second
        out_low_ref[block, :] = second.astype(LOW)

    row_blocks(count, second_norm)
    for tile in range(tiles):
        part = pl.ds(tile * FF_TILE, FF_TILE)
        column_copy(down_ref, held_down, down_sem, tile, FF_TILE).wait()
        active = product(out_low_ref[...], held_down[:, part])
        inner = (active * slope_ref[:, part].astype(jnp.float32)).astype(LOW)
        inner_low_ref[:, part] = inner
        column_copy(up_ref, held_up, up_sem, tile, FF_TILE).wait()
        sum_ref[...] += product(inner, held_up[:, part], 1, 1)

    def first_norm(block):
        grad, unit = sum_ref[block, :], unit1_ref[block, :]
        norm_grad_ref[0:1] += jnp.sum(grad * unit, axis=0, keepdims=True)
        norm_grad_ref[1:2] += jnp.sum(grad, axis=0, keepdims=True)
        first = normalize_back(grad, unit, inverse1_ref[block, 0:1], norm_ref[0:1])
        first_ref[block, :] = first
        first_low_ref[block, :] = first.astype(LOW)

    row_blocks(count, first_norm)


def ffn_backward(grad, unit2, inverse2, slope, unit1, inverse1, norm, up, down):
    count, width = grad.shape
    inner = up.shape[1]
    tiles = inner // FF_TILE
    shape = jax.ShapeDtypeStruct
    return pl.pallas_call(
        ffn_backward_kernel,
        out_shape=[
            shape((count, width), LOW),
            shape((count, inner), LOW),
            shape((count, width), jnp.float32),
            shape((count, width), LOW),
            shape(norm.shape, jnp.float32),
        ],
        in_specs=[VECTORS] * 7 + [ANYWHERE] * 2,
        out_specs=[VECTORS] * 5,
        scratch_shapes=[
            pltpu.VMEM(up.shape, LOW),
            pltpu.VMEM(down.shape, LOW),
            pltpu.VMEM((count, width), jnp.float32),
            pltpu.SemaphoreType.DMA((tiles,)),
            pltpu.SemaphoreType.DMA((tiles,)),
        ],
        cost_estimate=pl.CostEstimate(
            flops=4 * count * up.size,
            bytes_accessed=4 * up.size + 4 * count * inner + 20 * count * width,
            transcendentals=0,
        ),
        compiler_params=pltpu.CompilerParams(vmem_limit_bytes=48 * 2**20),
    )(grad, unit2, inverse2, slope, unit1, inverse1, norm, up, down)


def attend_backward_kernel(
    lengths_ref,
    first_ref,
    first_low_ref,
    qkv_ref,
    lse_ref,
    weight_ref,
    qkv_grad_ref,
    rows_grad_ref,
    held_ref,
    mask_ref,
    mixed_ref,
    sem,
):
    count, width = first_ref.shape
    chunks = [column_copy(weight_ref, held_ref, sem, k, width) for k in range(4)]
    for copy in reversed(chunks):
        copy.start()
    fill_mask(lengths_ref, mask_ref)
    chunks[3].wait()
    tiles = width // TILE

    def back_out(tile, carry):
        part = columns(tile, TILE)
        mixed_ref[:, part] = product(
            first_low_ref[...], held_ref[part, pl.ds(3 * width, width)], 1, 1
        ).astype(LOW)
        return carry

    lax.fori_loop(0, tiles, back_out, 0)

    def one_pair(pair, carry):
        query_part = columns(pair, PAIR)
        key_part = columns(width // PAIR + pair, PAIR)
        value_part = columns(2 * width // PAIR + pair, PAIR)
        query = qkv_ref[:, query_part] * jnp.asarray(SCALE, LOW)
        key = qkv_ref[:, key_part]
        value = qkv_ref[:, value_part]
        grad = mixed_ref[:, query_part]
        lse = lse_ref[pair]
        key_grads, value_grads, query_grads = [], [], []
        for half in (0, 1):
            lanes = half_lanes(count, half)
            own_query = jnp.where(lanes, query, jnp.zeros_like(query))
            own_grad = jnp.where(lanes, grad, jnp.zeros_like(grad))
            scores = product(key, own_query, 1, 1) + mask_ref[...]
            weights = jnp.exp(scores - lse[half : half + 1])
            weight_grad = product(value, own_grad, 1, 1)
            value_grads.append(product(weights.astype(LOW), grad))
            along = jnp.sum(weights * weight_grad, axis=0, keepdims=True)
            low = (weights * (weight_grad - along)).astype(LOW)
            key_grads.append(product(low, query))
            back = product(key, low, 0, 0)
            query_grads.append(back[half * HEAD_DIM : (half + 1) * HEAD_DIM])
        lanes = half_lanes(count, 1)
        query_grad = jnp.concatenate(query_grads, axis=0).T * SCALE
        qkv_grad_ref[:, query_part] = query_grad.astype(LOW)
        qkv_grad_ref[:, key_part] = jnp.where(lanes, key_grads[1], key_grads[0]).astype(LOW)
        qkv_grad_ref[:, value_part] = jnp.where(lanes, value_grads[1], value_grads[0]).astype(LOW)
        return carry

    lax.fori_loop(0, width // PAIR, one_pair, 0)
    for k in range(3):
        chunks[k].wait()

    def back_in(tile, carry):
        part = columns(tile, TILE)
        rows_grad_ref[:, part] = first_ref[:, part] + product(
            qkv_grad_ref[...], held_ref[part, pl.ds(0, 3 * width)], 1, 1
        )
        return carry

    lax.fori_loop(0, tiles, back_in, 0)


def attend_backward(lengths, first, first_low, qkv, lse, weight):
    count, width = first.shape
    shape = jax.ShapeDtypeStruct
    return pl.pallas_call(
        attend_backward_kernel,
        out_shape=[shape((count, 3 * width), LOW), shape((count, width), jnp.float32)],
        in_specs=[SCALARS] + [VECTORS] * 4 + [ANYWHERE],
        out_specs=[VECTORS] * 2,
        scratch_shapes=[
            pltpu.VMEM(weight.shape, LOW),
            pltpu.VMEM((count, count), jnp.float32),
            pltpu.VMEM((count, width), LOW),
            pltpu.SemaphoreType.DMA((4,)),
        ],
        cost_estimate=pl.CostEstimate(
            flops=2 * count * weight.size + 10 * count * count * width,
            bytes_accessed=2 * weight.size + 24 * count * width,
            transcendentals=count * count * width // HEAD_DIM,
        ),
        compiler_params=pltpu.CompilerParams(vmem_limit_bytes=32 * 2**20),
    )(lengths, first, first_low, qkv, lse, weight)


def weight_sum_kernel(picker_ref, left_a, left_b, right_a, right_b, send_ref, keep_ref, turned):
    count = left_a.shape[0]
    half = send_ref.shape[0]

    @pl.when(pl.program_id(0) == 0)
    def _():
        for layer, left in enumerate((left_a, left_b)):
            turned[:, layer * count : (layer + 1) * count] = product(
                picker_ref[...], left[...], 1, 1
            ).astype(LOW)

    right = jnp.concatenate([right_a[...], right_b[...]], axis=0)
    for block in range(2 * half // TILE):
        rows = slice(block * TILE, (block + 1) * TILE)
        total = product(turned[rows], right).astype(LOW)
        if block * TILE < half:
            send_ref[rows] = total
        else:
            keep_ref[block * TILE - half : (block + 1) * TILE - half] = total


def weight_sum(layer_pairs, picker):
    (left_a, right_a), (left_b, right_b) = layer_pairs
    count, rows = left_a.shape
    wide = right_a.shape[1]
    whole = pl.BlockSpec((count, rows), lambda tile: (0, 0))
    right = pl.BlockSpec((count, FF_TILE), lambda tile: (0, tile))
    out = pl.BlockSpec((rows // 2, FF_TILE), lambda tile: (0, tile))
    return pl.pallas_call(
        weight_sum_kernel,
        grid=(wide // FF_TILE,),
        out_shape=[jax.ShapeDtypeStruct((rows // 2, wide), LOW)] * 2,
        in_specs=[
            pl.BlockSpec((rows, rows), lambda tile: (0, 0)),
            whole,
            whole,
            right,
            right,
        ],
        out_specs=[out, out],
        scratch_shapes=[pltpu.VMEM((rows, 2 * count), LOW)],
        cost_estimate=pl.CostEstimate(
            flops=4 * count * rows * (wide + rows),
            bytes_accessed=2 * rows * (wide + rows) + 4 * count * (wide + rows),
            transcendentals=0,
        ),
        compiler_params=pltpu.CompilerParams(vmem_limit_bytes=32 * 2**20),
    )(picker, left_a, left_b, right_a, right_b)


AXES = ("dp", "fsdp")
NORM_COLS = 128


class Route:
    def __init__(self):
        rows, cols = lax.axis_size("dp"), lax.axis_size("fsdp")
        self.inner = cols // 4
        self.ring_size = rows // 2 * self.inner
        self.cols = cols
        self.world = rows * cols
        row, col = lax.axis_index("dp"), lax.axis_index("fsdp")
        self.q = row // 2 * self.inner + col // 4
        self.y, self.x, self.c = row % 2, col // 2 % 2, col % 2

    def joint(self, q, y, x, c):
        return (q // self.inner * 2 + y) * self.cols + q % self.inner * 4 + x * 2 + c

    def move(self, array, step):
        pairs = []
        for q in range(self.ring_size):
            for y in (0, 1):
                for x in (0, 1):
                    for c in (0, 1):
                        to = step(q, y, x, c)
                        pairs.append((self.joint(q, y, x, c), self.joint(*to)))
        return lax.ppermute(array, AXES, pairs)

    def ring(self, array):
        return self.move(array, lambda q, y, x, c: ((q + 1) % self.ring_size, y, x, c))

    def core(self, array):
        return self.move(array, lambda q, y, x, c: (q, y, x, 1 - c))

    def first(self, array):
        return self.move(array, lambda q, y, x, c: (q, y ^ c, x ^ (1 - c), c))

    def second(self, array):
        return self.move(array, lambda q, y, x, c: (q, y ^ (1 - c), x ^ c, c))

    def owner(self, back, first, second, core):
        c = self.c ^ core
        x = self.x ^ jnp.where(c == 0, first, second)
        y = self.y ^ jnp.where(c == 0, second, first)
        return self.joint((self.q + self.ring_size - back) % self.ring_size, y, x, c)


def gather_ring_first(route, piece):
    slots = [piece]
    for _ in range(route.ring_size - 1):
        slots.append(route.ring(slots[-1]))
    base = jnp.concatenate(slots)
    blocks = [(base, 0, 0), (route.first(base), 1, 0)]
    blocks += [(route.second(block), first, 1) for block, first, _ in blocks]
    arrays, owners = [], []
    for core in (0, 1):
        for block, first, second in blocks:
            arrays.append(route.core(block) if core else block)
            owners += [route.owner(i, first, second, core) for i in range(route.ring_size)]
    return arrays, owners


def gather_ring_middle(route, piece):
    pair = jnp.concatenate([piece, route.first(piece)])
    arrays, owners = [], []
    for i in range(route.ring_size):
        if i:
            pair = route.ring(pair)
        other = route.second(pair)
        for core in (0, 1):
            for second, block in ((0, pair), (1, other)):
                arrays.append(route.core(block) if core else block)
                owners += [route.owner(i, first, second, core) for first in (0, 1)]
    return arrays, owners


def place_kernel(owners_ref, *refs, widths):
    count = len(refs) - len(widths) - 2
    parts, outs, whole, sem = refs[:count], refs[count:-2], refs[-2], refs[-1]
    shard = whole.shape[0] // owners_ref.shape[0]
    copies = []
    for part in parts:
        for local in range(part.shape[0] // shard):
            row = pl.multiple_of(owners_ref[len(copies)] * shard, shard)
            copies.append(
                pltpu.make_async_copy(
                    part.at[pl.ds(local * shard, shard)],
                    whole.at[pl.ds(row, shard)],
                    sem.at[len(copies)],
                )
            )
    for copy in copies:
        copy.start()
    for copy in copies:
        copy.wait()
    column = 0
    copies = []
    for out, width in zip(outs, widths):
        copies.append(
            pltpu.make_async_copy(whole.at[:, pl.ds(column, width)], out, sem.at[len(copies)])
        )
        column += width
    for copy in copies:
        copy.start()
    for copy in copies:
        copy.wait()


def place_rows(arrays, owners, widths):
    owners = jnp.stack(owners).astype(jnp.int32)
    rows = sum(array.shape[0] for array in arrays)
    anywhere = pl.BlockSpec(memory_space=pl.ANY)
    kind = arrays[0].dtype
    return pl.pallas_call(
        functools.partial(place_kernel, widths=widths),
        out_shape=[jax.ShapeDtypeStruct((rows, width), kind) for width in widths],
        in_specs=[pl.BlockSpec(memory_space=pltpu.SMEM)] + [anywhere] * len(arrays),
        out_specs=[anywhere] * len(widths),
        scratch_shapes=[
            pltpu.VMEM((rows, sum(widths)), kind),
            pltpu.SemaphoreType.DMA((owners.size,)),
        ],
        cost_estimate=pl.CostEstimate(
            flops=0, bytes_accessed=4 * rows * sum(widths), transcendentals=0
        ),
        compiler_params=pltpu.CompilerParams(vmem_limit_bytes=16 * 2**20),
    )(owners, *arrays)


def row_picker(owners, shard):
    rows = (jnp.stack(owners)[:, None] * shard + jnp.arange(shard)[None, :]).reshape(-1, 1)
    return (rows == jnp.arange(rows.size)[None, :]).astype(jnp.bfloat16)


def add_low(left, right):
    return (left.astype(jnp.float32) + right.astype(jnp.float32)).astype(jnp.bfloat16)


def owners_ring_last(route):
    return [
        route.owner(1 + j, first, second, core)
        for core in (1, 0)
        for second in (1, 0)
        for first in (1, 0)
        for j in range(route.ring_size)
    ]


def scatter_ring_last(route, send, keep):
    for step in (route.core, route.second):
        arrived = step(send)
        half = keep.shape[0] // 2
        send, keep = add_low(keep[:half], arrived[:half]), add_low(keep[half:], arrived[half:])
    arrived = route.first(send)
    pieces = [
        add_low(a, b) for a, b in zip(cut(keep, route.ring_size), cut(arrived, route.ring_size))
    ]
    moving = pieces[0]
    for piece in pieces[1:-1]:
        moving = add_low(piece, route.ring(moving))
    return pieces[-1].astype(jnp.float32) + route.ring(moving).astype(jnp.float32)


def owners_ring_middle(route):
    return [
        route.owner(1 + j, first, second, core)
        for core in (1, 0)
        for second in (1, 0)
        for j in range(route.ring_size)
        for first in (1, 0)
    ]


def cut(array, count):
    size = array.shape[0] // count
    return [array[k * size : (k + 1) * size] for k in range(count)]


def scatter_whole(route, upper, lower):
    return lax.psum_scatter(
        jnp.concatenate([upper, lower]), AXES, scatter_dimension=0, tiled=True
    ).astype(jnp.float32)


def scatter_ring_middle(route, send, keep):
    arrived = route.core(send)
    half = keep.shape[0] // 2
    pieces = route.ring_size
    sends = [
        add_low(a, b) for a, b in zip(cut(keep[:half], pieces), cut(arrived[:half], pieces))
    ]
    keeps = [
        add_low(a, b) for a, b in zip(cut(keep[half:], pieces), cut(arrived[half:], pieces))
    ]
    moving = None
    for j in range(pieces):
        local = add_low(keeps[j], route.second(sends[j]))
        moving = local if moving is None else add_low(local, route.ring(moving))
    shard = moving.shape[0] // 2
    return moving[shard:].astype(jnp.float32) + route.first(moving[:shard]).astype(jnp.float32)


def update(gradient, master, moment, average, step_rate):
    moment_new = 0.9 * moment + gradient
    master_new = master - step_rate * (gradient + 0.9 * moment_new)
    average_new = 0.8 * average + 0.2 * master_new
    return (gradient, moment_new, master_new, average_new, master_new.astype(jnp.bfloat16))


def shards(
    tokens,
    cotangent,
    seq_lengths,
    att_master,
    ffn_master,
    norm_master,
    att_moment,
    ffn_moment,
    norm_moment,
    att_average,
    ffn_average,
    norm_average,
):
    row_count = tokens.shape[0]
    lengths = [seq_lengths[0, slot] for slot in range(seq_lengths.shape[1])]
    live_rows = (jnp.arange(row_count) < sum(lengths)).astype(jnp.float32)[:, None]
    route = Route()
    shard = att_master.shape[0]
    norm_piece = jnp.pad(norm_master.T, ((0, 0), (0, NORM_COLS - norm_master.shape[0])))
    att_piece = jnp.concatenate([att_master, norm_piece], axis=1).astype(jnp.bfloat16)
    ffn_pieces = ffn_master.astype(jnp.bfloat16)
    width = att_master.shape[1]
    tiled = shard % 16 == 0
    if tiled:
        att_full, norm_full = place_rows(
            *gather_ring_middle(route, att_piece), (width, NORM_COLS)
        )
        [up_full] = place_rows(*gather_ring_middle(route, ffn_pieces[0]), (width,))
        [down_full] = place_rows(*gather_ring_first(route, ffn_pieces[1]), (width,))
    else:
        whole = [
            lax.all_gather(piece, AXES, axis=0, tiled=True)
            for piece in (att_piece, ffn_pieces[0], ffn_pieces[1])
        ]
        att_full, norm_full, up_full, down_full = whole[0][:, :width], whole[0][:, width:], *whole[1:]
    norm_values = norm_full[:, : norm_master.shape[0]].T.astype(jnp.float32)
    stored = []
    current = tokens
    for depth in range(LAYERS):
        low, qkv, mixed, lse, hidden, unit1, inverse1 = attend_forward(
            seq_lengths, current, norm_values, att_full
        )
        hidden_low, active, slope, unit2, inverse2, current = ffn_forward(
            hidden,
            norm_values,
            up_full,
            down_full,
            jnp.bfloat16 if depth == LAYERS - 1 else jnp.float32,
        )
        stored.append(
            (low, qkv, mixed, lse, unit1, inverse1, hidden_low, active, slope, unit2, inverse2)
        )
    grad_now = cotangent.astype(jnp.float32) * live_rows
    downs, ups, projs, inprojs = [], [], [], []
    norm_term = 0.0
    for depth in reversed(range(LAYERS)):
        low, qkv, mixed, lse, unit1, inverse1, hidden_low, active, slope, unit2, inverse2 = stored[
            depth
        ]
        out_low, inner_low, first, first_low, norm_part = ffn_backward(
            grad_now, unit2, inverse2, slope, unit1, inverse1, norm_values, up_full, down_full
        )
        qkv_low, grad_now = attend_backward(seq_lengths, first, first_low, qkv, lse, att_full)
        norm_term = norm_term + norm_part
        downs.append((out_low, active))
        ups.append((hidden_low, inner_low))
        projs.append((mixed, first_low))
        inprojs.append((low, qkv_low))
    middle = row_picker(owners_ring_middle(route), shard)
    last = row_picker(owners_ring_last(route), shard)
    scatter_middle, scatter_last = scatter_ring_middle, scatter_ring_last
    if not tiled:
        middle = last = row_picker(list(range(route.world)), shard)
        scatter_middle = scatter_last = scatter_whole
    down_share = scatter_middle(route, *weight_sum(downs, middle))
    up_share = scatter_middle(route, *weight_sum(ups, middle))
    norm_rows = jnp.pad(norm_term.T, ((0, 0), (0, NORM_COLS - norm_term.shape[0])))
    norm_rows = jnp.einsum(
        "rd,dn->rn", last, norm_rows.astype(jnp.bfloat16), preferred_element_type=jnp.float32
    ).astype(jnp.bfloat16)
    att_parts = zip(weight_sum(inprojs, last), weight_sum(projs, last), jnp.split(norm_rows, 2))
    att_halves = [jnp.concatenate(parts, axis=1) for parts in att_parts]
    att_share = scatter_last(route, *att_halves)
    totals = (
        att_share[:, :width],
        jnp.stack([up_share, down_share]),
        att_share[:, width : width + norm_master.shape[0]].T,
    )
    step_rate = 0.1 / math.sqrt(row_count * lax.axis_size(("dp", "fsdp")))
    att_out = update(totals[0], att_master, att_moment, att_average, step_rate)
    ffn_out = update(totals[1], ffn_master, ffn_moment, ffn_average, step_rate)
    norm_out = update(totals[2], norm_master, norm_moment, norm_average, step_rate)
    return (
        current,
        grad_now,
        att_out[0],
        att_out[1],
        att_out[2],
        att_out[3],
        att_out[4],
        ffn_out[0],
        ffn_out[1],
        ffn_out[2],
        ffn_out[3],
        ffn_out[4],
        norm_out[0],
        norm_out[1],
        norm_out[2],
        norm_out[3],
        norm_out[4],
    )


def solution(mesh):
    return jax.shard_map(
        shards,
        mesh=mesh,
        in_specs=(
            P(("dp", "fsdp"), None),
            P(("dp", "fsdp"), None),
            P(("dp", "fsdp"), None),
            P(("dp", "fsdp"), None),
            P(None, ("dp", "fsdp"), None),
            P(None, ("dp", "fsdp")),
            P(("dp", "fsdp"), None),
            P(None, ("dp", "fsdp"), None),
            P(None, ("dp", "fsdp")),
            P(("dp", "fsdp"), None),
            P(None, ("dp", "fsdp"), None),
            P(None, ("dp", "fsdp")),
        ),
        out_specs=(
            P(("dp", "fsdp"), None),
            P(("dp", "fsdp"), None),
            P(("dp", "fsdp"), None),
            P(("dp", "fsdp"), None),
            P(("dp", "fsdp"), None),
            P(("dp", "fsdp"), None),
            P(("dp", "fsdp"), None),
            P(None, ("dp", "fsdp"), None),
            P(None, ("dp", "fsdp"), None),
            P(None, ("dp", "fsdp"), None),
            P(None, ("dp", "fsdp"), None),
            P(None, ("dp", "fsdp"), None),
            P(None, ("dp", "fsdp")),
            P(None, ("dp", "fsdp")),
            P(None, ("dp", "fsdp")),
            P(None, ("dp", "fsdp")),
            P(None, ("dp", "fsdp")),
        ),
        check_vma=False,
    )
```

```python
import functools
import math
import types

import jax
import jax.numpy as jnp
from jax import lax
from jax.experimental import pallas as pl
from jax.experimental.pallas import tpu as pltpu
from jax.sharding import PartitionSpec as P

HEAD_DIM = 64


LOW = jnp.bfloat16
SCALE = HEAD_DIM ** (-0.5)
PAIR = 2 * HEAD_DIM
TILE = 512
FF_TILE = 1024
ROWS = 32
NORM_COLS = 128
GELU_RATE = math.sqrt(2.0 / math.pi)
ANYWHERE = pl.BlockSpec(memory_space=pl.ANY)
IN_HBM = pl.BlockSpec(memory_space=pltpu.HBM)
SCALARS = pl.BlockSpec(memory_space=pltpu.SMEM)
VECTORS = pl.BlockSpec(memory_space=pltpu.VMEM)


def launch(body, given, made, scratch, products, moved, limit):
    names, specs, arrays = [], [], []
    for name, (spec, value) in given.items():
        group = value if isinstance(value, list) else [value]
        names += [(name, isinstance(value, list))] * len(group)
        specs += [spec] * len(group)
        arrays += group
    names += [(name, False) for name in (*made, *scratch)]

    def kernel(*refs):
        held = {}
        for (name, grouped), ref in zip(names, refs):
            if grouped:
                held.setdefault(name, []).append(ref)
            else:
                held[name] = ref
        body(types.SimpleNamespace(**held))

    outs = pl.pallas_call(
        kernel,
        out_shape=[jax.ShapeDtypeStruct(shape, kind) for _, shape, kind in made.values()],
        in_specs=specs,
        out_specs=[spec for spec, _, _ in made.values()],
        scratch_shapes=list(scratch.values()),
        cost_estimate=pl.CostEstimate(
            flops=2 * products, bytes_accessed=moved, transcendentals=0
        ),
        compiler_params=pltpu.CompilerParams(vmem_limit_bytes=limit * 2**20),
    )(*arrays)
    return types.SimpleNamespace(**dict(zip(made, outs)))


class Copies:
    def __init__(self, sem):
        self.sem, self.used, self.open = sem, 0, []

    def start(self, source, target, keep=True):
        copy = pltpu.make_async_copy(source, target, self.sem.at[self.used])
        self.used += 1
        copy.start()
        if keep:
            self.open.append(copy)
        return copy

    def rows(self, parts, owners_ref, target):
        if len(parts) == 1:
            return [self.start(parts[0], target, False)]
        shard = target.shape[0] // owners_ref.shape[0]
        copies = []
        for part in parts:
            for local in range(part.shape[0] // shard):
                row = pl.multiple_of(owners_ref[len(copies)] * shard, shard)
                source = part.at[pl.ds(local * shard, shard)]
                copies.append(self.start(source, target.at[pl.ds(row, shard)], False))
        return copies

    def finish(self):
        for copy in self.open:
            copy.wait()


def wait_all(copies):
    for copy in copies:
        copy.wait()


def product(left, right, left_dim=1, right_dim=0):
    dims = (((left_dim,), (right_dim,)), ((), ()))
    return lax.dot_general(left, right, dims, preferred_element_type=jnp.float32)


def tiles(total, size):
    return [slice(start, start + size) for start in range(0, total, size)]


def fill_mask(lengths_ref, mask_ref):
    shape = mask_ref.shape
    key_row = lax.broadcasted_iota(jnp.int32, shape, 0)
    query_row = lax.broadcasted_iota(jnp.int32, shape, 1)
    end = 0
    key_segment = jnp.zeros(shape, jnp.int32)
    query_segment = jnp.zeros(shape, jnp.int32)
    for slot in range(lengths_ref.shape[1]):
        end = end + lengths_ref[0, slot]
        key_segment += (key_row >= end).astype(jnp.int32)
        query_segment += (query_row >= end).astype(jnp.int32)
    mask_ref[...] = jnp.where(key_segment == query_segment, 0.0, -1e30)


def normalize(values, gain, bias):
    centered = values - jnp.mean(values, axis=-1, keepdims=True)
    spread = jnp.mean(centered * centered, axis=-1, keepdims=True)
    inverse = lax.rsqrt(spread + 1e-05)
    unit = centered * inverse
    return unit, inverse, unit * gain + bias


def normalize_back(grad, unit, inverse, gain):
    scaled = grad * gain
    mean = jnp.mean(scaled, axis=-1, keepdims=True)
    along = jnp.mean(scaled * unit, axis=-1, keepdims=True)
    return inverse * (scaled - mean - unit * along)


def half_lanes(rows, half):
    lane = lax.broadcasted_iota(jnp.int32, (rows, PAIR), 1)
    return (lane >= HEAD_DIM) == bool(half)


def add_norm_grad(norm_grad, row, grad, unit):
    norm_grad[row : row + 1] += jnp.sum(grad * unit, axis=0, keepdims=True)
    norm_grad[row + 1 : row + 2] += jnp.sum(grad, axis=0, keepdims=True)


def attend_forward(rows, low, att, att_ready, mask, qkv, mixed, lse, total, norm, hidden, unit, inverse):
    count, width = low.shape
    att_ready()
    for part in tiles(3 * width, TILE):
        qkv[:, part] = product(low[...], att[:, part]).astype(LOW)
    for pair, part in enumerate(tiles(width, PAIR)):
        query = qkv[:, part] * jnp.asarray(SCALE, LOW)
        key = qkv[:, slice(width + part.start, width + part.stop)]
        value = qkv[:, slice(2 * width + part.start, 2 * width + part.stop)]
        halves, sums = [], []
        for half in (0, 1):
            own = jnp.where(half_lanes(count, half), query, jnp.zeros_like(query))
            scores = product(key, own, 1, 1) + mask[...]
            peak = jnp.max(scores, axis=0, keepdims=True)
            weights = jnp.exp(scores - peak)
            sum_all = jnp.sum(weights, axis=0, keepdims=True)
            sums.append(peak + jnp.log(sum_all))
            out = product(value, weights.astype(LOW), 0, 0)
            halves.append(out[half * HEAD_DIM : (half + 1) * HEAD_DIM] * (1.0 / sum_all))
        lse[pair] = jnp.concatenate(sums, axis=0)
        mixed[:, part] = jnp.concatenate(halves, axis=0).T.astype(LOW)
    for part in tiles(width, TILE):
        out = slice(3 * width + part.start, 3 * width + part.stop)
        total[:, part] = rows[:, part].astype(jnp.float32) + product(mixed[...], att[:, out])
    for block in tiles(count, ROWS):
        unit[block], inverse[block], hidden[block] = normalize(total[block], norm[0:1], norm[1:2])


def ffn_forward(hidden, low, up, down, up_ready, down_ready, active, slope, total):
    low[...] = hidden[...].astype(LOW)
    total[...] = hidden[...]
    up_ready()
    for part in tiles(active.shape[1], FF_TILE):
        inner = product(low[...], up[:, part])
        square = inner * inner
        bend = jnp.tanh(GELU_RATE * inner * (1.0 + 0.044715 * square))
        rise = 0.5 + 0.5 * bend
        act = (inner * rise).astype(LOW)
        active[:, part] = act
        slope[:, part] = (
            rise
            + (0.5 * GELU_RATE) * inner * (1.0 - bend * bend) * (1.0 + 3 * 0.044715 * square)
        ).astype(LOW)
        if part.start == 0:
            down_ready()
        total[...] += product(act, down[:, part], 1, 1)


def ffn_backward(second, out_low, slope, up, down, unit, inverse, norm, inner_low, total, first, first_low, norm_grad, ready=None):
    count, _ = second.shape
    total[...] = second[...]
    for index, part in enumerate(tiles(slope.shape[1], FF_TILE)):
        if ready:
            ready(index)
        act = product(out_low[...], down[:, part])
        inner = (act * slope[:, part].astype(jnp.float32)).astype(LOW)
        inner_low[:, part] = inner
        total[...] += product(inner, up[:, part], 1, 1)
    for block in tiles(count, ROWS):
        grad, unit_rows = total[block], unit[block]
        add_norm_grad(norm_grad, 0, grad, unit_rows)
        out = normalize_back(grad, unit_rows, inverse[block], norm[0:1])
        first[block] = out
        first_low[block] = out.astype(LOW)


def attend_backward(first, first_low, qkv, lse, mask, att, mixed_grad, qkv_grad, rows_grad, ready=None):
    count, width = first.shape
    if ready:
        ready(3)
    for part in tiles(width, TILE):
        mixed_grad[:, part] = product(
            first_low[...], att[part, 3 * width : 4 * width], 1, 1
        ).astype(LOW)
    for pair, part in enumerate(tiles(width, PAIR)):
        key_part = slice(width + part.start, width + part.stop)
        value_part = slice(2 * width + part.start, 2 * width + part.stop)
        query = qkv[:, part] * jnp.asarray(SCALE, LOW)
        key, value, grad = qkv[:, key_part], qkv[:, value_part], mixed_grad[:, part]
        sums = lse[pair]
        key_grads, value_grads, query_grads = [], [], []
        for half in (0, 1):
            lanes = half_lanes(count, half)
            own_query = jnp.where(lanes, query, jnp.zeros_like(query))
            own_grad = jnp.where(lanes, grad, jnp.zeros_like(grad))
            weights = jnp.exp(product(key, own_query, 1, 1) + mask[...] - sums[half : half + 1])
            weight_grad = product(value, own_grad, 1, 1)
            value_grads.append(product(weights.astype(LOW), grad))
            along = jnp.sum(weights * weight_grad, axis=0, keepdims=True)
            low = (weights * (weight_grad - along)).astype(LOW)
            key_grads.append(product(low, query))
            back = product(key, low, 0, 0)
            query_grads.append(back[half * HEAD_DIM : (half + 1) * HEAD_DIM])
        lanes = half_lanes(count, 1)
        qkv_grad[:, part] = (jnp.concatenate(query_grads, axis=0).T * SCALE).astype(LOW)
        qkv_grad[:, key_part] = jnp.where(lanes, key_grads[1], key_grads[0]).astype(LOW)
        qkv_grad[:, value_part] = jnp.where(lanes, value_grads[1], value_grads[0]).astype(LOW)
    if ready:
        for chunk in range(3):
            ready(chunk)
    for part in tiles(width, TILE):
        rows_grad[:, part] = first[:, part] + product(qkv_grad[...], att[part, : 3 * width], 1, 1)


def weight_sum(picker, lefts, rights, turned, whole, copies, send, keep):
    count = lefts[0].shape[0]
    half = send.shape[0]
    for layer, left in enumerate(lefts):
        turned[:, layer * count : (layer + 1) * count] = product(
            picker[...], left[...], 1, 1
        ).astype(LOW)
    for part in tiles(rights[0].shape[1], TILE):
        right = jnp.concatenate([ref[:, part] for ref in rights], axis=0)
        whole[:, part] = product(turned[...], right).astype(LOW)
        columns = pl.ds(part.start, TILE)
        copies.start(whole.at[pl.ds(0, half), columns], send.at[:, columns])
        copies.start(whole.at[pl.ds(half, half), columns], keep.at[:, columns])


def first_attention(lengths, owners, tokens, parts):
    count, width = tokens.shape
    wide = parts[0].shape[1]

    def body(r):
        copies = Copies(r.sem)
        rows = copies.rows(r.parts, r.owners, r.held)
        fill_mask(r.lengths, r.mask)
        r.low[...] = r.tokens[...]

        def ready():
            wait_all(rows)
            copies.start(r.held.at[:, pl.ds(0, 4 * width)], r.att)
            r.turned[...] = r.held[:, 4 * width :].astype(jnp.float32).T
            r.norm[...] = r.turned[0:4]

        attend_forward(
            r.tokens,
            r.low,
            r.held,
            ready,
            r.mask,
            r.qkv,
            r.mixed,
            r.lse,
            r.total,
            r.norm,
            r.hidden,
            r.unit,
            r.inverse,
        )
        copies.finish()

    size = (count, width)
    return launch(
        body,
        {
            "lengths": (SCALARS, lengths),
            "owners": (SCALARS, owners),
            "tokens": (VECTORS, tokens),
            "parts": (IN_HBM, parts),
        },
        {
            "att": (IN_HBM, (width, 4 * width), LOW),
            "norm": (VECTORS, (4, width), jnp.float32),
            "qkv": (VECTORS, (count, 3 * width), LOW),
            "mixed": (VECTORS, size, LOW),
            "lse": (VECTORS, (width // PAIR, 2, count), jnp.float32),
            "hidden": (VECTORS, size, jnp.float32),
            "unit": (VECTORS, size, jnp.float32),
            "inverse": (VECTORS, (count, 1), jnp.float32),
        },
        {
            "held": pltpu.VMEM((width, wide), LOW),
            "low": pltpu.VMEM(size, LOW),
            "mask": pltpu.VMEM((count, count), jnp.float32),
            "total": pltpu.VMEM(size, jnp.float32),
            "turned": pltpu.VMEM((NORM_COLS, width), jnp.float32),
            "sem": pltpu.SemaphoreType.DMA((owners.size + 1,)),
        },
        4 * count * width * width + 2 * count * count * width,
        16 * width * width + 20 * count * width,
        40,
    )


def middle_layers(lengths, norm, hidden, cotangent, att, up_parts, up_owners, down_parts, down_owners, picker):
    count, width = hidden.shape
    inner = up_parts[0].shape[1]
    size, f32 = (count, width), jnp.float32
    results = {
        "hidden_low1": (size, LOW),
        "active1": ((count, inner), LOW),
        "slope1": ((count, inner), LOW),
        "low2": (size, LOW),
        "mixed2": (size, LOW),
        "hidden_low2": (size, LOW),
        "layer_output": (size, LOW),
        "inner_low2": ((count, inner), LOW),
        "first_low2": (size, LOW),
        "qkv_grad2": ((count, 3 * width), LOW),
        "second1": (size, f32),
        "out_low1": (size, LOW),
        "norm_grad": (norm.shape, f32),
    }

    def body(r):
        copies = Copies(r.sem)
        up_rows = copies.rows(r.up_parts, r.up_owners, r.held_up)
        down_rows = copies.rows(r.down_parts, r.down_owners, r.held_down)
        att_copy = copies.start(r.att, r.held_att, False)
        picker_copy = copies.start(r.picker, r.held_picker, False)
        fill_mask(r.lengths, r.mask)
        kept = []

        def up_ready():
            wait_all(up_rows)
            kept.append(copies.start(r.held_up, r.up_full, False))

        def down_ready():
            wait_all(down_rows)
            copies.start(r.held_down, r.down_full)

        def give(name):
            copies.start(getattr(r, "own_" + name), getattr(r, name))

        ffn_forward(
            r.hidden,
            r.own_hidden_low1,
            r.held_up,
            r.held_down,
            up_ready,
            down_ready,
            r.own_active1,
            r.own_slope1,
            r.total,
        )
        for name in ("hidden_low1", "active1", "slope1"):
            give(name)
        for block in tiles(count, ROWS):
            r.unit2[block], r.inverse2[block], rows = normalize(
                r.total[block], r.norm[2:3], r.norm[3:4]
            )
            r.rows[block] = rows
            r.own_low2[block] = rows.astype(LOW)
        give("low2")
        attend_forward(
            r.rows,
            r.own_low2,
            r.held_att,
            att_copy.wait,
            r.mask,
            r.qkv,
            r.own_mixed2,
            r.lse,
            r.total,
            r.norm,
            r.hidden2,
            r.unit1,
            r.inverse1,
        )
        give("mixed2")
        ffn_forward(
            r.hidden2,
            r.own_hidden_low2,
            r.held_up,
            r.held_down,
            lambda: None,
            lambda: None,
            r.active2,
            r.slope2,
            r.total,
        )
        give("hidden_low2")
        r.own_norm_grad[...] = jnp.zeros_like(r.own_norm_grad)
        live = 0
        for slot in range(r.lengths.shape[1]):
            live = live + r.lengths[0, slot]
        for block in tiles(count, ROWS):
            unit, inverse, rows = normalize(r.total[block], r.norm[2:3], r.norm[3:4])
            r.own_layer_output[block] = rows.astype(LOW)
            position = block.start + lax.broadcasted_iota(jnp.int32, unit.shape, 0)
            grad = jnp.where(position < live, r.cotangent[block].astype(f32), 0.0)
            add_norm_grad(r.own_norm_grad, 2, grad, unit)
            second = normalize_back(grad, unit, inverse, r.norm[2:3])
            r.rows[block] = second
            r.out_low2[block] = second.astype(LOW)
        give("layer_output")
        ffn_backward(
            r.rows,
            r.out_low2,
            r.slope2,
            r.held_up,
            r.held_down,
            r.unit1,
            r.inverse1,
            r.norm,
            r.own_inner_low2,
            r.total,
            r.rows,
            r.own_first_low2,
            r.own_norm_grad,
        )
        for name in ("inner_low2", "first_low2"):
            give(name)
        attend_backward(
            r.rows,
            r.own_first_low2,
            r.qkv,
            r.lse,
            r.mask,
            r.held_att,
            r.mixed_grad,
            r.own_qkv_grad2,
            r.total,
        )
        give("qkv_grad2")
        for block in tiles(count, ROWS):
            grad, unit = r.total[block], r.unit2[block]
            add_norm_grad(r.own_norm_grad, 2, grad, unit)
            second = normalize_back(grad, unit, r.inverse2[block], r.norm[2:3])
            r.own_second1[block] = second
            r.own_out_low1[block] = second.astype(LOW)
        for name in ("second1", "out_low1", "norm_grad"):
            give(name)
        picker_copy.wait()
        wait_all(kept)
        weight_sum(
            r.held_picker,
            (r.out_low2, r.own_out_low1),
            (r.active2, r.own_active1),
            r.turned,
            r.held_up,
            copies,
            r.send,
            r.keep,
        )
        copies.finish()

    made = {name: (IN_HBM, shape, kind) for name, (shape, kind) in results.items()}
    for name in ("up_full", "down_full"):
        made[name] = (IN_HBM, (width, inner), LOW)
    for name in ("send", "keep"):
        made[name] = (IN_HBM, (width // 2, inner), LOW)
    scratch = {"own_" + name: pltpu.VMEM(shape, kind) for name, (shape, kind) in results.items()}
    scratch |= {
        "held_up": pltpu.VMEM((width, inner), LOW),
        "held_down": pltpu.VMEM((width, inner), LOW),
        "held_att": pltpu.VMEM((width, 4 * width), LOW),
        "held_picker": pltpu.VMEM((width, width), LOW),
        "turned": pltpu.VMEM((width, 2 * count), LOW),
        "mask": pltpu.VMEM((count, count), f32),
        "qkv": pltpu.VMEM((count, 3 * width), LOW),
        "lse": pltpu.VMEM((width // PAIR, 2, count), f32),
        "active2": pltpu.VMEM((count, inner), LOW),
        "slope2": pltpu.VMEM((count, inner), LOW),
        "out_low2": pltpu.VMEM(size, LOW),
        "mixed_grad": pltpu.VMEM(size, LOW),
        "inverse1": pltpu.VMEM((count, 1), f32),
        "inverse2": pltpu.VMEM((count, 1), f32),
    }
    for name in ("total", "rows", "hidden2", "unit1", "unit2"):
        scratch[name] = pltpu.VMEM(size, f32)
    loads = len(up_parts) + len(down_parts) + 2 * up_owners.size
    scratch["sem"] = pltpu.SemaphoreType.DMA((loads + len(results) + 4 + 2 * (inner // TILE),))
    return launch(
        body,
        {
            "lengths": (SCALARS, lengths),
            "up_owners": (SCALARS, up_owners),
            "down_owners": (SCALARS, down_owners),
            "norm": (VECTORS, norm),
            "hidden": (VECTORS, hidden),
            "cotangent": (VECTORS, cotangent),
            "att": (IN_HBM, att),
            "picker": (IN_HBM, picker),
            "up_parts": (IN_HBM, up_parts),
            "down_parts": (IN_HBM, down_parts),
        },
        made,
        scratch,
        count * width * (8 * inner + 8 * width) + 7 * count * count * width,
        12 * width * inner,
        60,
    )


def first_ffn_backward(m, norm, unit, inverse, mixed, picker_up, picker_out):
    count, width = mixed.shape
    inner = m.slope1.shape[1]
    size, f32 = (count, width), jnp.float32
    late = {
        "picker_up": picker_up,
        "hidden_low2": m.hidden_low2,
        "hidden_low1": m.hidden_low1,
        "inner_low2": m.inner_low2,
        "picker_out": picker_out,
        "mixed2": m.mixed2,
        "mixed1": mixed,
        "first_low2": m.first_low2,
    }

    def body(r):
        copies = Copies(r.sem)
        parts = [pl.ds(part.start, FF_TILE) for part in tiles(inner, FF_TILE)]
        weights = [
            (
                copies.start(r.down.at[:, part], r.held_down.at[:, part], False),
                copies.start(r.up.at[:, part], r.held_up.at[:, part], False),
            )
            for part in parts
        ]
        loads = [copies.start(getattr(r, n), getattr(r, "own_" + n), False) for n in late]
        r.norm_grad[...] = jnp.zeros_like(r.norm_grad)
        ffn_backward(
            r.second,
            r.out_low,
            r.slope,
            r.held_up,
            r.held_down,
            r.unit,
            r.inverse,
            r.norm,
            r.inner_low,
            r.total,
            r.first,
            r.first_low,
            r.norm_grad,
            lambda index: wait_all(weights[index]),
        )
        wait_all(loads)
        weight_sum(
            r.own_picker_up,
            (r.own_hidden_low2, r.own_hidden_low1),
            (r.own_inner_low2, r.inner_low),
            r.turned,
            r.held_up,
            copies,
            r.send_up,
            r.keep_up,
        )
        weight_sum(
            r.own_picker_out,
            (r.own_mixed2, r.own_mixed1),
            (r.own_first_low2, r.first_low),
            r.turned,
            r.held_down,
            copies,
            r.send_out,
            r.keep_out,
        )
        copies.finish()

    given = {
        "second": (VECTORS, m.second1),
        "out_low": (VECTORS, m.out_low1),
        "slope": (VECTORS, m.slope1),
        "unit": (VECTORS, unit),
        "inverse": (VECTORS, inverse),
        "norm": (VECTORS, norm),
        "up": (IN_HBM, m.up_full),
        "down": (IN_HBM, m.down_full),
    }
    given |= {name: (IN_HBM, value) for name, value in late.items()}
    scratch = {"own_" + name: pltpu.VMEM(value.shape, LOW) for name, value in late.items()}
    scratch |= {
        "held_up": pltpu.VMEM((width, inner), LOW),
        "held_down": pltpu.VMEM((width, inner), LOW),
        "turned": pltpu.VMEM((width, 2 * count), LOW),
        "inner_low": pltpu.VMEM((count, inner), LOW),
        "total": pltpu.VMEM(size, f32),
        "sem": pltpu.SemaphoreType.DMA(
            (2 * (inner // FF_TILE) + len(late) + 2 * (inner + width) // TILE,)
        ),
    }
    return launch(
        body,
        given,
        {
            "first": (VECTORS, size, f32),
            "first_low": (VECTORS, size, LOW),
            "norm_grad": (VECTORS, norm.shape, f32),
            "send_up": (IN_HBM, (width // 2, inner), LOW),
            "keep_up": (IN_HBM, (width // 2, inner), LOW),
            "send_out": (IN_HBM, (width // 2, width), LOW),
            "keep_out": (IN_HBM, (width // 2, width), LOW),
        },
        scratch,
        count * width * (4 * inner + 2 * width),
        8 * width * inner,
        60,
    )


def first_attention_backward(lengths, first, first_low, qkv, lse, att, tokens, low2, qkv_grad2, norm_grads, picker):
    count, width = first.shape
    size, f32 = (count, width), jnp.float32
    late = {"picker": picker, "low2": low2, "tokens": tokens, "qkv_grad2": qkv_grad2}
    wide = 3 * width + NORM_COLS

    def body(r):
        copies = Copies(r.sem)
        chunks = [None] * 4
        for chunk in (3, 0, 1, 2):
            part = pl.ds(chunk * width, width)
            chunks[chunk] = copies.start(r.att.at[:, part], r.held.at[:, part], False)
        loads = [copies.start(getattr(r, n), getattr(r, "own_" + n), False) for n in late]
        fill_mask(r.lengths, r.mask)
        attend_backward(
            r.first,
            r.first_low,
            r.qkv,
            r.lse,
            r.mask,
            r.held,
            r.mixed_grad,
            r.qkv_grad,
            r.input_grad,
            lambda chunk: chunks[chunk].wait(),
        )
        wait_all(loads)
        r.norm_rows[...] = jnp.zeros_like(r.norm_rows)
        r.norm_rows[0:4] = (r.norm_a[...] + r.norm_b[...]).astype(LOW)
        extra = product(r.own_picker[...], r.norm_rows[...], 1, 1).astype(LOW)
        half = width // 2
        r.extra[...] = extra
        columns = pl.ds(3 * width, NORM_COLS)
        copies.start(r.extra.at[pl.ds(0, half)], r.send.at[:, columns])
        copies.start(r.extra.at[pl.ds(half, half)], r.keep.at[:, columns])
        weight_sum(
            r.own_picker,
            (r.own_low2, r.own_tokens),
            (r.own_qkv_grad2, r.qkv_grad),
            r.turned,
            r.whole,
            copies,
            r.send,
            r.keep,
        )
        copies.finish()

    given = {
        "lengths": (SCALARS, lengths),
        "first": (VECTORS, first),
        "first_low": (VECTORS, first_low),
        "qkv": (VECTORS, qkv),
        "lse": (VECTORS, lse),
        "norm_a": (VECTORS, norm_grads[0]),
        "norm_b": (VECTORS, norm_grads[1]),
        "att": (IN_HBM, att),
    }
    given |= {name: (IN_HBM, value) for name, value in late.items()}
    scratch = {"own_" + name: pltpu.VMEM(value.shape, LOW) for name, value in late.items()}
    scratch |= {
        "held": pltpu.VMEM((width, 4 * width), LOW),
        "mask": pltpu.VMEM((count, count), f32),
        "mixed_grad": pltpu.VMEM(size, LOW),
        "qkv_grad": pltpu.VMEM((count, 3 * width), LOW),
        "turned": pltpu.VMEM((width, 2 * count), LOW),
        "whole": pltpu.VMEM((width, 3 * width), LOW),
        "norm_rows": pltpu.VMEM((NORM_COLS, width), LOW),
        "extra": pltpu.VMEM((width, NORM_COLS), LOW),
        "sem": pltpu.SemaphoreType.DMA((4 + len(late) + 2 + 2 * (3 * width // TILE),)),
    }
    return launch(
        body,
        given,
        {
            "input_grad": (VECTORS, size, f32),
            "send": (IN_HBM, (width // 2, wide), LOW),
            "keep": (IN_HBM, (width // 2, wide), LOW),
        },
        scratch,
        count * width * 10 * width + 5 * count * count * width,
        16 * width * width,
        60,
    )


AXES = ("dp", "fsdp")


class Route:
    def __init__(self):
        rows, cols = lax.axis_size("dp"), lax.axis_size("fsdp")
        self.inner = cols // 4
        self.ring_size = rows // 2 * self.inner
        self.cols = cols
        self.world = rows * cols
        row, col = lax.axis_index("dp"), lax.axis_index("fsdp")
        self.q = row // 2 * self.inner + col // 4
        self.y, self.x, self.c = row % 2, col // 2 % 2, col % 2

    def joint(self, q, y, x, c):
        return (q // self.inner * 2 + y) * self.cols + q % self.inner * 4 + x * 2 + c

    def move(self, array, step):
        pairs = []
        for q in range(self.ring_size):
            for y in (0, 1):
                for x in (0, 1):
                    for c in (0, 1):
                        to = step(q, y, x, c)
                        pairs.append((self.joint(q, y, x, c), self.joint(*to)))
        return lax.ppermute(array, AXES, pairs)

    def ring(self, array):
        return self.move(array, lambda q, y, x, c: ((q + 1) % self.ring_size, y, x, c))

    def core(self, array):
        return self.move(array, lambda q, y, x, c: (q, y, x, 1 - c))

    def first(self, array):
        return self.move(array, lambda q, y, x, c: (q, y ^ c, x ^ (1 - c), c))

    def second(self, array):
        return self.move(array, lambda q, y, x, c: (q, y ^ (1 - c), x ^ c, c))

    def owner(self, back, first, second, core):
        c = self.c ^ core
        x = self.x ^ jnp.where(c == 0, first, second)
        y = self.y ^ jnp.where(c == 0, second, first)
        return self.joint((self.q + self.ring_size - back) % self.ring_size, y, x, c)


def after(value, *earlier):
    return lax.optimization_barrier((value, earlier))[0]


class RingFirst:
    def __init__(self, route, piece):
        self.route, self.slots = route, [piece]

    def step(self, *earlier):
        self.slots.append(self.route.ring(after(self.slots[-1], *earlier)))

    def finish(self):
        route = self.route
        base = jnp.concatenate(self.slots)
        blocks = [(base, 0, 0), (route.first(base), 1, 0)]
        blocks += [(route.second(block), first, 1) for block, first, _ in blocks]
        arrays, owners = [], []
        for core in (0, 1):
            for block, first, second in blocks:
                arrays.append(route.core(block) if core else block)
                owners += [route.owner(i, first, second, core) for i in range(route.ring_size)]
        return arrays, owners


class RingMiddle:
    def __init__(self, route, piece):
        self.route = route
        self.pairs = [jnp.concatenate([piece, route.first(piece)])]

    def step(self, *earlier):
        self.pairs.append(self.route.ring(after(self.pairs[-1], *earlier)))

    def finish(self):
        route = self.route
        arrays, owners = [], []
        for i, pair in enumerate(self.pairs):
            other = route.second(pair)
            for core in (0, 1):
                for second, block in ((0, pair), (1, other)):
                    arrays.append(route.core(block) if core else block)
                    owners += [route.owner(i, first, second, core) for first in (0, 1)]
        return arrays, owners


def row_picker(owners, shard):
    rows = (jnp.stack(owners)[:, None] * shard + jnp.arange(shard)[None, :]).reshape(-1, 1)
    return (rows == jnp.arange(rows.size)[None, :]).astype(jnp.bfloat16)


def add_low(left, right):
    return (left.astype(jnp.float32) + right.astype(jnp.float32)).astype(jnp.bfloat16)


def owners_ring_last(route):
    return [
        route.owner(1 + j, first, second, core)
        for core in (1, 0)
        for second in (1, 0)
        for first in (1, 0)
        for j in range(route.ring_size)
    ]


def owners_ring_middle(route):
    return [
        route.owner(1 + j, first, second, core)
        for core in (1, 0)
        for second in (1, 0)
        for j in range(route.ring_size)
        for first in (1, 0)
    ]


def cut(array, count):
    size = array.shape[0] // count
    return [array[k * size : (k + 1) * size] for k in range(count)]


class SumWhole:
    def __init__(self, route, upper, lower):
        self.term = jnp.concatenate([upper, lower])

    def spread(self, *earlier):
        return ()

    def step(self, *earlier):
        return ()

    def finish(self):
        return lax.psum_scatter(self.term, AXES, scatter_dimension=0, tiled=True).astype(
            jnp.float32
        )


class SumRingLast:
    def __init__(self, route, send, keep):
        self.route, self.keep = route, keep
        self.arrived = route.core(send)

    def fold(self, *earlier):
        half = self.keep.shape[0] // 2
        keep, arrived = after((self.keep, self.arrived), *earlier)
        send = add_low(keep[:half], arrived[:half])
        self.keep = add_low(keep[half:], arrived[half:])
        return send

    def finish(self):
        self.arrived = self.route.second(self.sent)
        self.arrived = self.route.first(self.fold())
        count = self.route.ring_size
        pieces = [add_low(a, b) for a, b in zip(cut(self.keep, count), cut(self.arrived, count))]
        moving = pieces[0]
        for piece in pieces[1:-1]:
            moving = add_low(piece, self.route.ring(moving))
        return pieces[-1].astype(jnp.float32) + self.route.ring(moving).astype(jnp.float32)

    def spread(self, *earlier):
        self.sent = self.fold(*earlier)
        return self.sent


class SumRingMiddle:
    def __init__(self, route, send, keep):
        self.route, self.keep = route, keep
        self.arrived = route.core(send)

    def spread(self, *earlier):
        half, count = self.keep.shape[0] // 2, self.route.ring_size
        keep, arrived = after((self.keep, self.arrived), *earlier)
        sends = [add_low(a, b) for a, b in zip(cut(keep[:half], count), cut(arrived[:half], count))]
        self.keeps = [
            add_low(a, b) for a, b in zip(cut(keep[half:], count), cut(arrived[half:], count))
        ]
        self.others = [self.route.second(send) for send in sends]
        self.moving = None
        self.done = 0
        return sends

    def step(self, *earlier):
        local = add_low(after(self.keeps[self.done], *earlier), self.others[self.done])
        self.moving = local if self.moving is None else add_low(local, self.route.ring(self.moving))
        self.done += 1
        return self.moving

    def finish(self):
        while self.done < len(self.keeps):
            self.step()
        shard = self.moving.shape[0] // 2
        other = self.route.first(self.moving[:shard])
        return self.moving[shard:].astype(jnp.float32) + other.astype(jnp.float32)


def update(gradient, master, moment, average, step_rate):
    moment_new = 0.9 * moment + gradient
    master_new = master - step_rate * (gradient + 0.9 * moment_new)
    average_new = 0.8 * average + 0.2 * master_new
    return (gradient, moment_new, master_new, average_new, master_new.astype(jnp.bfloat16))


def shards(
    tokens,
    cotangent,
    seq_lengths,
    att_master,
    ffn_master,
    norm_master,
    att_moment,
    ffn_moment,
    norm_moment,
    att_average,
    ffn_average,
    norm_average,
):
    row_count = tokens.shape[0]
    route = Route()
    shard = att_master.shape[0]
    norm_piece = jnp.pad(norm_master.T, ((0, 0), (0, NORM_COLS - norm_master.shape[0])))
    att_piece = jnp.concatenate([att_master, norm_piece], axis=1).astype(jnp.bfloat16)
    ffn_pieces = ffn_master.astype(jnp.bfloat16)
    width = att_master.shape[1]
    tiled = shard % 16 == 0
    if tiled:
        middle = row_picker(owners_ring_middle(route), shard)
        last = row_picker(owners_ring_last(route), shard)
        down = RingFirst(route, ffn_pieces[1])
        down.step()
        att = RingMiddle(route, att_piece)
        up = RingMiddle(route, ffn_pieces[0])
        att.step()
        for _ in range(route.ring_size - 2):
            down.step()
            att.step()
            up.step(down.slots[-1])
        up.step()
        att, down, up = att.finish(), down.finish(), up.finish()
        sum_middle, sum_last = SumRingMiddle, SumRingLast
    else:
        middle = last = row_picker(list(range(route.world)), shard)
        att, down, up = [
            ([lax.all_gather(piece, AXES, axis=0, tiled=True)], [0])
            for piece in (att_piece, ffn_pieces[1], ffn_pieces[0])
        ]
        sum_middle = sum_last = SumWhole
    (att_parts, att_owners), (down_parts, down_owners), (up_parts, up_owners) = [
        (parts, jnp.stack(owners).astype(jnp.int32) if tiled else jnp.zeros(1, jnp.int32))
        for parts, owners in (att, down, up)
    ]
    f = first_attention(seq_lengths, att_owners, tokens, att_parts)
    m = middle_layers(
        seq_lengths,
        f.norm,
        f.hidden,
        cotangent,
        f.att,
        up_parts,
        up_owners,
        down_parts,
        down_owners,
        middle,
    )
    down_sum = sum_middle(route, m.send, m.keep)
    b = first_ffn_backward(m, f.norm, f.unit, f.inverse, f.mixed, middle, last)
    up_sum = sum_middle(route, b.send_up, b.keep_up)
    out_sum = sum_last(route, b.send_out, b.keep_out)
    sends = down_sum.spread(b.first_low)
    a = first_attention_backward(
        seq_lengths,
        after(b.first, sends),
        b.first_low,
        f.qkv,
        f.lse,
        f.att,
        tokens,
        m.low2,
        m.qkv_grad2,
        (m.norm_grad, b.norm_grad),
        last,
    )
    in_sum = sum_last(route, a.send, a.keep)
    sends = up_sum.spread(a.input_grad)
    moving = down_sum.step(sends)
    sends = out_sum.spread(moving)
    sends = in_sum.spread(sends)
    down_share, up_share = down_sum.finish(), up_sum.finish()
    proj_share, inproj_share = out_sum.finish(), in_sum.finish()
    wide = 3 * width // 4
    totals = (
        jnp.concatenate([inproj_share[:, :wide], proj_share], axis=1),
        jnp.stack([up_share, down_share]),
        inproj_share[:, wide : wide + norm_master.shape[0]].T,
    )
    step_rate = 0.1 / math.sqrt(row_count * lax.axis_size(("dp", "fsdp")))
    att_out = update(totals[0], att_master, att_moment, att_average, step_rate)
    ffn_out = update(totals[1], ffn_master, ffn_moment, ffn_average, step_rate)
    norm_out = update(totals[2], norm_master, norm_moment, norm_average, step_rate)
    return (
        m.layer_output,
        a.input_grad,
        att_out[0],
        att_out[1],
        att_out[2],
        att_out[3],
        att_out[4],
        ffn_out[0],
        ffn_out[1],
        ffn_out[2],
        ffn_out[3],
        ffn_out[4],
        norm_out[0],
        norm_out[1],
        norm_out[2],
        norm_out[3],
        norm_out[4],
    )


def solution(mesh):
    return jax.shard_map(
        shards,
        mesh=mesh,
        in_specs=(
            P(("dp", "fsdp"), None),
            P(("dp", "fsdp"), None),
            P(("dp", "fsdp"), None),
            P(("dp", "fsdp"), None),
            P(None, ("dp", "fsdp"), None),
            P(None, ("dp", "fsdp")),
            P(("dp", "fsdp"), None),
            P(None, ("dp", "fsdp"), None),
            P(None, ("dp", "fsdp")),
            P(("dp", "fsdp"), None),
            P(None, ("dp", "fsdp"), None),
            P(None, ("dp", "fsdp")),
        ),
        out_specs=(
            P(("dp", "fsdp"), None),
            P(("dp", "fsdp"), None),
            P(("dp", "fsdp"), None),
            P(("dp", "fsdp"), None),
            P(("dp", "fsdp"), None),
            P(("dp", "fsdp"), None),
            P(("dp", "fsdp"), None),
            P(None, ("dp", "fsdp"), None),
            P(None, ("dp", "fsdp"), None),
            P(None, ("dp", "fsdp"), None),
            P(None, ("dp", "fsdp"), None),
            P(None, ("dp", "fsdp"), None),
            P(None, ("dp", "fsdp")),
            P(None, ("dp", "fsdp")),
            P(None, ("dp", "fsdp")),
            P(None, ("dp", "fsdp")),
            P(None, ("dp", "fsdp")),
        ),
        check_vma=False,
    )
```

```python
import functools
import math
import types

import jax
import jax.numpy as jnp
from jax import lax
from jax.experimental import pallas as pl
from jax.experimental.pallas import tpu as pltpu
from jax.sharding import PartitionSpec as P

HEAD_DIM = 64


LOW = jnp.bfloat16
SCALE = HEAD_DIM ** (-0.5)
PAIR = 2 * HEAD_DIM
TILE = 512
FF_TILE = 1024
ROWS = 32
NORM_COLS = 128
GELU_RATE = math.sqrt(2.0 / math.pi)
ANYWHERE = pl.BlockSpec(memory_space=pl.ANY)
IN_HBM = pl.BlockSpec(memory_space=pltpu.HBM)
SCALARS = pl.BlockSpec(memory_space=pltpu.SMEM)
VECTORS = pl.BlockSpec(memory_space=pltpu.VMEM)


def launch(body, given, made, scratch, own, products, moved, limit):
    names, specs, arrays = [], [], []
    for name, (spec, value) in given.items():
        group = value if isinstance(value, list) else [value]
        names += [(0, name, isinstance(value, list))] * len(group)
        specs += [spec] * len(group)
        arrays += group
    names += [(0, name, False) for name in (*made, *scratch)]
    names += [(1, name, False) for name in own]

    def kernel(*refs):
        held = ({}, {})
        for (which, name, grouped), ref in zip(names, refs):
            if grouped:
                held[which].setdefault(name, []).append(ref)
            else:
                held[which][name] = ref
        body(*(types.SimpleNamespace(**group) for group in held))

    outs = pl.pallas_call(
        kernel,
        out_shape=[jax.ShapeDtypeStruct(shape, kind) for _, shape, kind in made.values()],
        in_specs=specs,
        out_specs=[spec for spec, _, _ in made.values()],
        scratch_shapes=[*scratch.values(), *own.values()],
        cost_estimate=pl.CostEstimate(
            flops=16 * products, bytes_accessed=moved, transcendentals=0
        ),
        compiler_params=pltpu.CompilerParams(vmem_limit_bytes=limit * 2**20),
    )(*arrays)
    return types.SimpleNamespace(**dict(zip(made, outs)))


class Copies:
    def __init__(self, sem):
        self.sem, self.used, self.open = sem, 0, []

    def start(self, source, target, keep=True):
        copy = pltpu.make_async_copy(source, target, self.sem.at[self.used])
        self.used += 1
        copy.start()
        if keep:
            self.open.append(copy)
        return copy

    def rows(self, parts, owners_ref, target):
        if len(parts) == 1:
            return [self.start(parts[0], target, False)]
        shard = target.shape[0] // owners_ref.shape[0]
        copies = []
        for part in parts:
            for local in range(part.shape[0] // shard):
                row = pl.multiple_of(owners_ref[len(copies)] * shard, shard)
                source = part.at[pl.ds(local * shard, shard)]
                copies.append(self.start(source, target.at[pl.ds(row, shard)], False))
        return copies

    def finish(self):
        for copy in self.open:
            copy.wait()


def wait_all(copies):
    for copy in copies:
        copy.wait()


def product(left, right, left_dim=1, right_dim=0):
    dims = (((left_dim,), (right_dim,)), ((), ()))
    return lax.dot_general(left, right, dims, preferred_element_type=jnp.float32)


def tiles(total, size):
    return [slice(start, start + size) for start in range(0, total, size)]


def fill_mask(lengths_ref, mask_ref):
    shape = mask_ref.shape
    key_row = lax.broadcasted_iota(jnp.int32, shape, 0)
    query_row = lax.broadcasted_iota(jnp.int32, shape, 1)
    end = 0
    key_segment = jnp.zeros(shape, jnp.int32)
    query_segment = jnp.zeros(shape, jnp.int32)
    for slot in range(lengths_ref.shape[1]):
        end = end + lengths_ref[0, slot]
        key_segment += (key_row >= end).astype(jnp.int32)
        query_segment += (query_row >= end).astype(jnp.int32)
    mask_ref[...] = jnp.where(key_segment == query_segment, 0.0, -1e30)


def normalize(values, gain, bias):
    centered = values - jnp.mean(values, axis=-1, keepdims=True)
    spread = jnp.mean(centered * centered, axis=-1, keepdims=True)
    inverse = lax.rsqrt(spread + 1e-05)
    unit = centered * inverse
    return unit, inverse, unit * gain + bias


def normalize_back(grad, unit, inverse, gain):
    scaled = grad * gain
    mean = jnp.mean(scaled, axis=-1, keepdims=True)
    along = jnp.mean(scaled * unit, axis=-1, keepdims=True)
    return inverse * (scaled - mean - unit * along)


def half_lanes(rows, half):
    lane = lax.broadcasted_iota(jnp.int32, (rows, PAIR), 1)
    return (lane >= HEAD_DIM) == bool(half)


def add_norm_grad(norm_grad, row, grad, unit):
    norm_grad[row : row + 1] += jnp.sum(grad * unit, axis=0, keepdims=True)
    norm_grad[row + 1 : row + 2] += jnp.sum(grad, axis=0, keepdims=True)


def attend_forward(rows, low, att, att_ready, mask, qkv, mixed, lse, total, norm, hidden, unit, inverse):
    count, width = low.shape
    att_ready()
    for part in tiles(3 * width, TILE):
        qkv[:, part] = product(low[...], att[:, part]).astype(LOW)
    for pair, part in enumerate(tiles(width, PAIR)):
        query = qkv[:, part] * jnp.asarray(SCALE, LOW)
        key = qkv[:, slice(width + part.start, width + part.stop)]
        value = qkv[:, slice(2 * width + part.start, 2 * width + part.stop)]
        halves, sums = [], []
        for half in (0, 1):
            own = jnp.where(half_lanes(count, half), query, jnp.zeros_like(query))
            scores = product(key, own, 1, 1) + mask[...]
            peak = jnp.max(scores, axis=0, keepdims=True)
            weights = jnp.exp(scores - peak)
            sum_all = jnp.sum(weights, axis=0, keepdims=True)
            sums.append(peak + jnp.log(sum_all))
            out = product(value, weights.astype(LOW), 0, 0)
            halves.append(out[half * HEAD_DIM : (half + 1) * HEAD_DIM] * (1.0 / sum_all))
        lse[pair] = jnp.concatenate(sums, axis=0)
        mixed[:, part] = jnp.concatenate(halves, axis=0).T.astype(LOW)
    for part in tiles(width, TILE):
        out = slice(3 * width + part.start, 3 * width + part.stop)
        total[:, part] = rows[:, part].astype(jnp.float32) + product(mixed[...], att[:, out])
    for block in tiles(count, ROWS):
        unit[block], inverse[block], hidden[block] = normalize(total[block], norm[0:1], norm[1:2])


def ffn_forward(hidden, low, up, down, up_ready, down_ready, active, slope, total):
    low[...] = hidden[...].astype(LOW)
    total[...] = hidden[...]
    up_ready()
    for part in tiles(active.shape[1], FF_TILE):
        inner = product(low[...], up[:, part])
        square = inner * inner
        bend = jnp.tanh(GELU_RATE * inner * (1.0 + 0.044715 * square))
        rise = 0.5 + 0.5 * bend
        act = (inner * rise).astype(LOW)
        active[:, part] = act
        slope[:, part] = (
            rise
            + (0.5 * GELU_RATE) * inner * (1.0 - bend * bend) * (1.0 + 3 * 0.044715 * square)
        ).astype(LOW)
        if part.start == 0:
            down_ready()
        total[...] += product(act, down[:, part], 1, 1)


def ffn_backward(second, out_low, slope, up, down, unit, inverse, norm, inner_low, total, first, first_low, norm_grad, ready=None, norm_ready=None):
    count, _ = second.shape
    total[...] = second[...]
    for index, part in enumerate(tiles(slope.shape[1], FF_TILE)):
        if ready:
            ready(index)
        act = product(out_low[...], down[:, part])
        inner = (act * slope[:, part].astype(jnp.float32)).astype(LOW)
        inner_low[:, part] = inner
        total[...] += product(inner, up[:, part], 1, 1)
    if norm_ready:
        norm_ready()
    for block in tiles(count, ROWS):
        grad, unit_rows = total[block], unit[block]
        add_norm_grad(norm_grad, 0, grad, unit_rows)
        out = normalize_back(grad, unit_rows, inverse[block], norm[0:1])
        first[block] = out
        first_low[block] = out.astype(LOW)


def attend_backward(first, first_low, qkv, lse, mask, att, mixed_grad, qkv_grad, rows_grad, ready=None):
    count, width = first.shape
    if ready:
        ready(3)
    for part in tiles(width, TILE):
        mixed_grad[:, part] = product(
            first_low[...], att[part, 3 * width : 4 * width], 1, 1
        ).astype(LOW)
    for pair, part in enumerate(tiles(width, PAIR)):
        key_part = slice(width + part.start, width + part.stop)
        value_part = slice(2 * width + part.start, 2 * width + part.stop)
        query = qkv[:, part] * jnp.asarray(SCALE, LOW)
        key, value, grad = qkv[:, key_part], qkv[:, value_part], mixed_grad[:, part]
        sums = lse[pair]
        key_grads, value_grads, query_grads = [], [], []
        for half in (0, 1):
            lanes = half_lanes(count, half)
            own_query = jnp.where(lanes, query, jnp.zeros_like(query))
            own_grad = jnp.where(lanes, grad, jnp.zeros_like(grad))
            weights = jnp.exp(product(key, own_query, 1, 1) + mask[...] - sums[half : half + 1])
            weight_grad = product(value, own_grad, 1, 1)
            value_grads.append(product(weights.astype(LOW), grad))
            along = jnp.sum(weights * weight_grad, axis=0, keepdims=True)
            low = (weights * (weight_grad - along)).astype(LOW)
            key_grads.append(product(low, query))
            back = product(key, low, 0, 0)
            query_grads.append(back[half * HEAD_DIM : (half + 1) * HEAD_DIM])
        lanes = half_lanes(count, 1)
        qkv_grad[:, part] = (jnp.concatenate(query_grads, axis=0).T * SCALE).astype(LOW)
        qkv_grad[:, key_part] = jnp.where(lanes, key_grads[1], key_grads[0]).astype(LOW)
        qkv_grad[:, value_part] = jnp.where(lanes, value_grads[1], value_grads[0]).astype(LOW)
    if ready:
        for chunk in range(3):
            ready(chunk)
    for part in tiles(width, TILE):
        rows_grad[:, part] = first[:, part] + product(qkv_grad[...], att[part, : 3 * width], 1, 1)


def weight_sum(picker, lefts, rights, turned, whole, copies, send, keep, offset=0, ready=None):
    count = lefts[0].shape[0]
    half = send.shape[0]
    for layer, left in enumerate(lefts):
        turned[:, layer * count : (layer + 1) * count] = product(
            picker[...], left[...], 1, 1
        ).astype(LOW)
    for index, part in enumerate(tiles(rights[0].shape[1], TILE)):
        if ready:
            ready(index)
        right = jnp.concatenate([ref[:, part] for ref in rights], axis=0)
        start = offset + part.start
        whole[:, start : start + TILE] = product(turned[...], right).astype(LOW)
        columns = pl.ds(start, TILE)
        copies.start(whole.at[pl.ds(0, half), columns], send.at[:, columns])
        copies.start(whole.at[pl.ds(half, half), columns], keep.at[:, columns])


def both_layers(lengths, tokens, cotangent, att_parts, att_owners, up_parts, up_owners, down_parts, down_owners, picker):
    count, width = tokens.shape
    inner = up_parts[0].shape[1]
    wide = att_parts[0].shape[1]
    size, f32 = (count, width), jnp.float32
    results = dict(
        qkv1=((count, 3 * width), LOW),
        mixed1=(size, LOW),
        lse1=((width // PAIR, 2, count), f32),
        unit_first=(size, f32),
        inverse_first=((count, 1), f32),
        norm=((4, width), f32),
        hidden_low1=(size, LOW),
        active1=((count, inner), LOW),
        slope1=((count, inner), LOW),
        low2=(size, LOW),
        mixed2=(size, LOW),
        hidden_low2=(size, LOW),
        layer_output=(size, LOW),
        inner_low2=((count, inner), LOW),
        first_low2=(size, LOW),
        qkv_grad2=((count, 3 * width), LOW),
        second1=(size, f32),
        out_low1=(size, LOW),
        norm_grad=((4, width), f32),
    )

    def body(r, own):
        copies = Copies(r.sem)
        att_rows = copies.rows(r.att_parts, r.att_owners, r.held_att)
        up_rows = copies.rows(r.up_parts, r.up_owners, r.held_up)
        down_rows = copies.rows(r.down_parts, r.down_owners, r.held_down)
        picker_copy = copies.start(r.picker, r.held_picker, False)
        fill_mask(r.lengths, r.mask)
        kept = []

        def up_ready():
            wait_all(up_rows)
            kept.append(copies.start(r.held_up, r.up_full, False))

        def down_ready():
            wait_all(down_rows)
            copies.start(r.held_down, r.down_full)

        def give(name):
            copies.start(getattr(own, name), getattr(r, name))

        def att_ready():
            wait_all(att_rows)
            copies.start(r.held_att.at[:, pl.ds(0, 4 * width)], r.att_full)
            turned = r.held_att[:, 4 * width :].astype(f32).T
            own.norm[...] = turned[0:4]

        attend_forward(
            r.tokens,
            r.tokens,
            r.held_att,
            att_ready,
            r.mask,
            own.qkv1,
            own.mixed1,
            own.lse1,
            r.total,
            own.norm,
            r.hidden2,
            own.unit_first,
            own.inverse_first,
        )
        for name in ("norm", "qkv1", "mixed1", "lse1", "unit_first", "inverse_first"):
            give(name)
        ffn_forward(
            r.hidden2,
            own.hidden_low1,
            r.held_up,
            r.held_down,
            up_ready,
            down_ready,
            own.active1,
            own.slope1,
            r.total,
        )
        for name in ("hidden_low1", "active1", "slope1"):
            give(name)
        for block in tiles(count, ROWS):
            r.unit2[block], r.inverse2[block], rows = normalize(
                r.total[block], own.norm[2:3], own.norm[3:4]
            )
            r.rows[block] = rows
            own.low2[block] = rows.astype(LOW)
        give("low2")
        attend_forward(
            r.rows,
            own.low2,
            r.held_att,
            lambda: None,
            r.mask,
            r.qkv,
            own.mixed2,
            r.lse,
            r.total,
            own.norm,
            r.hidden2,
            r.unit1,
            r.inverse1,
        )
        give("mixed2")
        ffn_forward(
            r.hidden2,
            own.hidden_low2,
            r.held_up,
            r.held_down,
            lambda: None,
            lambda: None,
            r.active2,
            own.inner_low2,
            r.total,
        )
        give("hidden_low2")
        own.norm_grad[...] = jnp.zeros_like(own.norm_grad)
        live = 0
        for slot in range(r.lengths.shape[1]):
            live = live + r.lengths[0, slot]
        for block in tiles(count, ROWS):
            unit, inverse, rows = normalize(r.total[block], own.norm[2:3], own.norm[3:4])
            own.layer_output[block] = rows.astype(LOW)
            position = block.start + lax.broadcasted_iota(jnp.int32, unit.shape, 0)
            grad = jnp.where(position < live, r.cotangent[block].astype(f32), 0.0)
            add_norm_grad(own.norm_grad, 2, grad, unit)
            second = normalize_back(grad, unit, inverse, own.norm[2:3])
            r.rows[block] = second
            r.out_low2[block] = second.astype(LOW)
        give("layer_output")
        ffn_backward(
            r.rows,
            r.out_low2,
            own.inner_low2,
            r.held_up,
            r.held_down,
            r.unit1,
            r.inverse1,
            own.norm,
            own.inner_low2,
            r.total,
            r.rows,
            own.first_low2,
            own.norm_grad,
        )
        for name in ("inner_low2", "first_low2"):
            give(name)
        attend_backward(
            r.rows,
            own.first_low2,
            r.qkv,
            r.lse,
            r.mask,
            r.held_att,
            r.mixed_grad,
            own.qkv_grad2,
            r.total,
        )
        give("qkv_grad2")
        for block in tiles(count, ROWS):
            grad, unit = r.total[block], r.unit2[block]
            add_norm_grad(own.norm_grad, 2, grad, unit)
            second = normalize_back(grad, unit, r.inverse2[block], own.norm[2:3])
            own.second1[block] = second
            own.out_low1[block] = second.astype(LOW)
        for name in ("second1", "out_low1", "norm_grad"):
            give(name)
        picker_copy.wait()
        wait_all(kept)
        weight_sum(
            r.held_picker,
            (r.out_low2, own.out_low1),
            (r.active2, own.active1),
            r.turned,
            r.held_up,
            copies,
            r.send,
            r.keep,
        )
        copies.finish()

    made = {name: (IN_HBM, shape, kind) for name, (shape, kind) in results.items()}
    made |= dict(
        att_full=(IN_HBM, (width, 4 * width), LOW),
        up_full=(IN_HBM, (width, inner), LOW),
        down_full=(IN_HBM, (width, inner), LOW),
        send=(IN_HBM, (width // 2, inner), LOW),
        keep=(IN_HBM, (width // 2, inner), LOW),
    )
    own = {name: pltpu.VMEM(shape, kind) for name, (shape, kind) in results.items()}
    rows_f32 = pltpu.VMEM(size, f32)
    scratch = dict(
        held_up=pltpu.VMEM((width, inner), LOW),
        held_down=pltpu.VMEM((width, inner), LOW),
        held_att=pltpu.VMEM((width, wide), LOW),
        held_picker=pltpu.VMEM((width, width), LOW),
        turned=pltpu.VMEM((width, 2 * count), LOW),
        mask=pltpu.VMEM((count, count), f32),
        qkv=pltpu.VMEM((count, 3 * width), LOW),
        lse=pltpu.VMEM((width // PAIR, 2, count), f32),
        active2=pltpu.VMEM((count, inner), LOW),
        out_low2=pltpu.VMEM(size, LOW),
        mixed_grad=pltpu.VMEM(size, LOW),
        inverse1=pltpu.VMEM((count, 1), f32),
        inverse2=pltpu.VMEM((count, 1), f32),
        total=rows_f32,
        rows=rows_f32,
        hidden2=rows_f32,
        unit1=rows_f32,
        unit2=rows_f32,
    )
    loads = 3 * up_owners.size
    copies = loads + len(results) + 5 + 2 * (inner // TILE)
    scratch |= dict(sem=pltpu.SemaphoreType.DMA((copies,)))
    return launch(
        body,
        dict(
            lengths=(SCALARS, lengths),
            up_owners=(SCALARS, up_owners),
            down_owners=(SCALARS, down_owners),
            att_owners=(SCALARS, att_owners),
            tokens=(VECTORS, tokens),
            cotangent=(VECTORS, cotangent),
            att_parts=(IN_HBM, att_parts),
            picker=(IN_HBM, picker),
            up_parts=(IN_HBM, up_parts),
            down_parts=(IN_HBM, down_parts),
        ),
        made,
        scratch,
        own,
        count * width * (8 * inner + 12 * width) + 9 * count * count * width,
        12 * width * inner,
        60,
    )


def first_ffn_backward(m, norm, unit, inverse):
    count, width = m.second1.shape
    inner = m.slope1.shape[1]
    size, f32 = (count, width), jnp.float32

    def body(r, own):
        copies = Copies(r.sem)
        slope = copies.start(r.slope, own.slope, False)
        weights = []
        for part in tiles(inner, FF_TILE):
            part = pl.ds(part.start, FF_TILE)
            pair = ((r.down, own.down), (r.up, own.up))
            weights.append([copies.start(a.at[:, part], b.at[:, part], False) for a, b in pair])
        unit_copy = copies.start(r.unit, own.unit, False)
        r.norm_grad[...] = jnp.zeros_like(r.norm_grad)

        def ready(index):
            if index == 0:
                slope.wait()
            wait_all(weights[index])

        def norm_ready():
            unit_copy.wait()
            copies.start(own.inner_low, r.inner_low)

        ffn_backward(
            r.second,
            r.out_low,
            own.slope,
            own.up,
            own.down,
            own.unit,
            r.inverse,
            r.norm,
            own.inner_low,
            r.total,
            r.first,
            r.first_low,
            r.norm_grad,
            ready,
            norm_ready,
        )
        copies.finish()

    return launch(
        body,
        dict(
            second=(VECTORS, m.second1),
            out_low=(VECTORS, m.out_low1),
            inverse=(VECTORS, inverse),
            norm=(VECTORS, norm),
            slope=(IN_HBM, m.slope1),
            unit=(IN_HBM, unit),
            up=(IN_HBM, m.up_full),
            down=(IN_HBM, m.down_full),
        ),
        dict(
            first=(VECTORS, size, f32),
            first_low=(VECTORS, size, LOW),
            norm_grad=(VECTORS, norm.shape, f32),
            inner_low=(IN_HBM, (count, inner), LOW),
        ),
        dict(
            total=pltpu.VMEM(size, f32),
            sem=pltpu.SemaphoreType.DMA((2 * (inner // FF_TILE) + 3,)),
        ),
        dict(
            up=pltpu.VMEM((width, inner), LOW),
            down=pltpu.VMEM((width, inner), LOW),
            slope=pltpu.VMEM((count, inner), LOW),
            inner_low=pltpu.VMEM((count, inner), LOW),
            unit=pltpu.VMEM(size, f32),
        ),
        count * width * 4 * inner,
        4 * width * inner,
        60,
    )


def up_and_out_gradients(lefts_up, rights_up, lefts_out, rights_out, picker):
    count, width = lefts_up[0].shape
    inner = rights_up[0].shape[1]
    late = dict(right_up=rights_up, left_out=lefts_out, right_out=rights_out)

    def body(r, own):
        copies = Copies(r.sem)
        parts = [
            [
                [
                    copies.start(ref.at[:, pl.ds(part.start, TILE)], to.at[:, pl.ds(part.start, TILE)], False)
                    for ref, to in zip(r.right_up, (own.up_a, own.up_b))
                ]
                for part in tiles(inner, TILE)
            ]
        ][0]
        loads = [
            copies.start(ref, to, False)
            for ref, to in zip(
                (*r.left_out, *r.right_out), (own.left_a, own.left_b, own.out_a, own.out_b)
            )
        ]
        weight_sum(
            r.picker,
            r.left_up,
            (own.up_a, own.up_b),
            r.turned,
            r.whole,
            copies,
            r.send,
            r.keep,
            0,
            lambda index: wait_all(parts[index]),
        )
        wait_all(loads)
        weight_sum(
            r.picker,
            (own.left_a, own.left_b),
            (own.out_a, own.out_b),
            r.turned,
            r.whole,
            copies,
            r.send,
            r.keep,
            inner,
        )
        copies.finish()

    given = dict(picker=(VECTORS, picker), left_up=(VECTORS, list(lefts_up)))
    given |= {name: (IN_HBM, list(pair)) for name, pair in late.items()}
    low = pltpu.VMEM((count, width), LOW)
    return launch(
        body,
        given,
        dict(
            send=(IN_HBM, (width // 2, inner + width), LOW),
            keep=(IN_HBM, (width // 2, inner + width), LOW),
        ),
        dict(
            whole=pltpu.VMEM((width, inner + width), LOW),
            turned=pltpu.VMEM((width, 2 * count), LOW),
            sem=pltpu.SemaphoreType.DMA((4 + 2 * (inner // TILE) + 2 * (inner + width) // TILE,)),
        ),
        dict(
            up_a=pltpu.VMEM((count, inner), LOW),
            up_b=pltpu.VMEM((count, inner), LOW),
            left_a=low,
            left_b=low,
            out_a=low,
            out_b=low,
        ),
        count * width * 2 * (inner + 3 * width),
        4 * width * inner,
        60,
    )


def first_attention_backward(lengths, first, first_low, qkv, lse, att, tokens, low2, qkv_grad2, norm_grads, picker):
    count, width = first.shape
    size, f32 = (count, width), jnp.float32
    late = dict(picker=picker, low2=low2, tokens=tokens, qkv_grad2=qkv_grad2)
    wide = 3 * width + NORM_COLS

    def body(r, own):
        copies = Copies(r.sem)
        chunks = [None] * 4
        for chunk in (3, 0, 1, 2):
            part = pl.ds(chunk * width, width)
            chunks[chunk] = copies.start(r.att.at[:, part], r.held.at[:, part], False)
        loads = [copies.start(getattr(r, n), getattr(own, n), False) for n in late]
        fill_mask(r.lengths, r.mask)
        attend_backward(
            r.first,
            r.first_low,
            r.qkv,
            r.lse,
            r.mask,
            r.held,
            r.mixed_grad,
            r.qkv_grad,
            r.input_grad,
            lambda chunk: chunks[chunk].wait(),
        )
        wait_all(loads)
        r.norm_rows[...] = jnp.zeros_like(r.norm_rows)
        r.norm_rows[0:4] = (r.norm_a[...] + r.norm_b[...]).astype(LOW)
        extra = product(own.picker[...], r.norm_rows[...], 1, 1).astype(LOW)
        half = width // 2
        r.extra[...] = extra
        columns = pl.ds(3 * width, NORM_COLS)
        copies.start(r.extra.at[pl.ds(0, half)], r.send.at[:, columns])
        copies.start(r.extra.at[pl.ds(half, half)], r.keep.at[:, columns])
        weight_sum(
            own.picker,
            (own.low2, own.tokens),
            (own.qkv_grad2, r.qkv_grad),
            r.turned,
            r.whole,
            copies,
            r.send,
            r.keep,
        )
        copies.finish()

    given = dict(
        lengths=(SCALARS, lengths),
        first=(VECTORS, first),
        first_low=(VECTORS, first_low),
        qkv=(VECTORS, qkv),
        lse=(VECTORS, lse),
        norm_a=(VECTORS, norm_grads[0]),
        norm_b=(VECTORS, norm_grads[1]),
        att=(IN_HBM, att),
    )
    given |= {name: (IN_HBM, value) for name, value in late.items()}
    own = {name: pltpu.VMEM(value.shape, LOW) for name, value in late.items()}
    scratch = dict(
        held=pltpu.VMEM((width, 4 * width), LOW),
        mask=pltpu.VMEM((count, count), f32),
        mixed_grad=pltpu.VMEM(size, LOW),
        qkv_grad=pltpu.VMEM((count, 3 * width), LOW),
        turned=pltpu.VMEM((width, 2 * count), LOW),
        whole=pltpu.VMEM((width, 3 * width), LOW),
        norm_rows=pltpu.VMEM((NORM_COLS, width), LOW),
        extra=pltpu.VMEM((width, NORM_COLS), LOW),
        sem=pltpu.SemaphoreType.DMA((4 + len(late) + 2 + 2 * (3 * width // TILE),)),
    )
    return launch(
        body,
        given,
        dict(
            input_grad=(VECTORS, size, f32),
            send=(IN_HBM, (width // 2, wide), LOW),
            keep=(IN_HBM, (width // 2, wide), LOW),
        ),
        scratch,
        own,
        count * width * 10 * width + 5 * count * count * width,
        16 * width * width,
        60,
    )


AXES = ("dp", "fsdp")


class Route:
    def __init__(self):
        rows, cols = lax.axis_size("dp"), lax.axis_size("fsdp")
        self.inner = cols // 4
        self.ring_size = rows // 2 * self.inner
        self.cols = cols
        self.world = rows * cols
        row, col = lax.axis_index("dp"), lax.axis_index("fsdp")
        self.q = row // 2 * self.inner + col // 4
        self.y, self.x, self.c = row % 2, col // 2 % 2, col % 2

    def joint(self, q, y, x, c):
        return (q // self.inner * 2 + y) * self.cols + q % self.inner * 4 + x * 2 + c

    def move(self, array, step):
        pairs = []
        for q in range(self.ring_size):
            for y in (0, 1):
                for x in (0, 1):
                    for c in (0, 1):
                        to = step(q, y, x, c)
                        pairs.append((self.joint(q, y, x, c), self.joint(*to)))
        return lax.ppermute(array, AXES, pairs)

    def ring(self, array, hops=1):
        return self.move(array, lambda q, y, x, c: ((q + hops) % self.ring_size, y, x, c))

    def core(self, array):
        return self.move(array, lambda q, y, x, c: (q, y, x, 1 - c))

    def first(self, array):
        return self.move(array, lambda q, y, x, c: (q, y ^ c, x ^ (1 - c), c))

    def second(self, array):
        return self.move(array, lambda q, y, x, c: (q, y ^ (1 - c), x ^ c, c))

    def owner(self, back, first, second, core):
        c = self.c ^ core
        x = self.x ^ jnp.where(c == 0, first, second)
        y = self.y ^ jnp.where(c == 0, second, first)
        return self.joint((self.q + self.ring_size - back) % self.ring_size, y, x, c)


def after(value, *earlier):
    return lax.optimization_barrier((value, earlier))[0]


def gather_all(route, att, up, down):
    last = route.ring_size - 1
    pairs = [[jnp.concatenate([piece, route.first(piece)])] for piece in (att, up)]
    chains = (*pairs, [down])
    others = ([], [])
    turns = [2] + [which for _ in range(last - 1) for which in (0, 2)] + [1, 0] + [1] * (last - 1)
    arrived = [(), ()]
    for turn, which in enumerate(turns):
        here = after(chains[which][-1], arrived[turn])
        chains[which].append(route.ring(here))
        arrived.append(chains[which][-1])
        if which < 2:
            others[which].append(route.second(here))
    base = jnp.concatenate(chains[2])
    first, both = route.first(base), route.second(base)
    crossed = route.second(after(first, pairs[1][1]))
    others[0].append(route.second(after(pairs[0][last], first)))
    others[1].append(route.second(pairs[1][last]))
    arrays, owners = [[], [], []], [[], [], []]

    def add(which, block, second, blocks, when):
        for core in (0, 1):
            arrays[which].append(route.core(after(block, when)) if core else block)
            owners[which] += [route.owner(back, flip, second, core) for back, flip in blocks]

    for which, chain in enumerate(pairs):
        for k in range(last + 1):
            blocks = [(k, 0), (k, 1)]
            add(which, chain[k], 0, blocks, ())
            add(which, others[which][k], 1, blocks, pairs[1][min(k + 1 + which, last)])
    rows = range(last + 1)
    add(2, base, 0, [(k, 0) for k in rows], pairs[0][last])
    add(2, first, 0, [(k, 1) for k in rows], pairs[1][max(last - 1, 0)])
    add(2, both, 1, [(k, 0) for k in rows], pairs[1][last])
    add(2, crossed, 1, [(k, 1) for k in rows], pairs[1][last])
    return arrays, owners


def row_picker(owners, shard):
    rows = (jnp.stack(owners)[:, None] * shard + jnp.arange(shard)[None, :]).reshape(-1, 1)
    return (rows == jnp.arange(rows.size)[None, :]).astype(jnp.bfloat16)


def add_all(*terms):
    total = terms[0].astype(jnp.float32)
    for term in terms[1:]:
        total = total + term.astype(jnp.float32)
    return total


def add_low(*terms):
    return add_all(*terms).astype(jnp.bfloat16)


def owners_ring_last(route):
    return [
        route.owner(1 + j, first, second, core)
        for core in (1, 0)
        for second in (1, 0)
        for first in (1, 0)
        for j in range(route.ring_size)
    ]


def owners_ring_middle(route):
    return [
        route.owner(1 + j, first, second, core)
        for core in (1, 0)
        for second in (1, 0)
        for j in range(route.ring_size)
        for first in (1, 0)
    ]


def cut(array, count):
    size = array.shape[0] // count
    return [array[k * size : (k + 1) * size] for k in range(count)]


class SumWhole:
    def __init__(self, route, upper, lower):
        self.term = jnp.concatenate([upper, lower])

    def steps(self):
        return iter(())

    def total(self):
        return lax.psum_scatter(self.term, AXES, scatter_dimension=0, tiled=True).astype(
            jnp.float32
        )


class SumRingMiddle:
    def __init__(self, route, send, keep):
        self.route, self.terms = route, (keep, route.core(send))
        self.result = None

    def steps(self):
        route, terms = self.route, self.terms
        count = route.ring_size
        half = terms[0].shape[0] // 2
        block = half // count
        earlier = yield
        near = after(terms, earlier)
        sends = [add_low(*(part[: half // 2] for part in near))]
        sends.append(add_low(*(part[half // 2 : half] for part in near)))
        others = [route.second(send) for send in sends]
        earlier = yield sends
        moving = None
        for j in range(count):
            arrived = [] if moving is None else [route.ring(moving)]
            near, far, arrived = after((terms, others if j else others[:1], arrived), earlier)
            start = half + j * block
            local = [part[start : start + block] for part in near]
            offset = j * block % (half // 2)
            local.append(far[2 * j // count][offset : offset + block])
            local += arrived
            if j < count - 1:
                moving = add_low(*local)
                earlier = yield moving
        shard = block // 2
        turned = add_low(*(part[:shard] for part in local))
        rest = add_all(*(part[shard:] for part in local))
        earlier = yield (turned, rest)
        self.result = rest + after(route.first(turned), earlier).astype(jnp.float32)
        yield self.result

    def total(self):
        return self.result


class SumRingLast:
    def __init__(self, route, send, keep):
        self.route, self.terms = route, [keep, route.core(send)]
        self.result = None

    def steps(self):
        route, terms = self.route, self.terms
        earlier = yield
        start, total = 0, terms[0].shape[0]
        for step in (route.second, route.first):
            half = (total - start) // 2
            near = after(terms, earlier)
            send = add_low(*self.part(near, start, half))
            start += half
            terms = terms + [step(send)]
            earlier = yield send
        block = (total - start) // route.ring_size
        moving = None
        for j in range(route.ring_size):
            arrived = [] if moving is None else [route.ring(moving)]
            near, arrived = after((terms, arrived), earlier)
            local = self.part(near, start + j * block, block) + arrived
            if j < route.ring_size - 1:
                moving = add_low(*local)
                earlier = yield moving
        self.result = add_all(*local)
        yield self.result

    @staticmethod
    def part(terms, start, size):
        total = terms[0].shape[0]
        skips = [start - (total - term.shape[0]) for term in terms]
        return [term[skip : skip + size] for term, skip in zip(terms, skips)]

    def total(self):
        return self.result


def advance(chain, earlier):
    try:
        return chain.send(earlier)
    except StopIteration:
        return None


def update(gradient, master, moment, average, step_rate):
    moment_new = 0.9 * moment + gradient
    master_new = master - step_rate * (gradient + 0.9 * moment_new)
    average_new = 0.8 * average + 0.2 * master_new
    return (gradient, moment_new, master_new, average_new, master_new.astype(jnp.bfloat16))


def shards(
    tokens,
    cotangent,
    seq_lengths,
    att_master,
    ffn_master,
    norm_master,
    att_moment,
    ffn_moment,
    norm_moment,
    att_average,
    ffn_average,
    norm_average,
):
    row_count = tokens.shape[0]
    route = Route()
    shard = att_master.shape[0]
    norm_piece = jnp.pad(norm_master.T, ((0, 0), (0, NORM_COLS - norm_master.shape[0])))
    att_piece = jnp.concatenate([att_master, norm_piece], axis=1).astype(jnp.bfloat16)
    ffn_pieces = ffn_master.astype(jnp.bfloat16)
    width = att_master.shape[1]
    tiled = shard % 16 == 0
    if tiled:
        middle = row_picker(owners_ring_middle(route), shard)
        last = row_picker(owners_ring_last(route), shard)
        arrays, owners = gather_all(route, att_piece, *ffn_pieces)
        middle, last = lax.optimization_barrier((middle, last))
        sum_middle, sum_last = SumRingMiddle, SumRingLast
    else:
        middle = last = row_picker(list(range(route.world)), shard)
        pieces = (att_piece, *ffn_pieces)
        arrays = [[lax.all_gather(piece, AXES, axis=0, tiled=True)] for piece in pieces]
        owners = [[0]] * 3
        sum_middle = sum_last = SumWhole
    owned = [
        jnp.stack(rows).astype(jnp.int32) if tiled else jnp.zeros(1, jnp.int32) for rows in owners
    ]
    m = both_layers(
        seq_lengths,
        tokens,
        cotangent,
        arrays[0],
        owned[0],
        arrays[1],
        owned[1],
        arrays[2],
        owned[2],
        middle,
    )
    down_sum = sum_middle(route, m.send, m.keep)
    down_steps = down_sum.steps()
    next(down_steps, None)
    b = first_ffn_backward(m, m.norm, m.unit_first, m.inverse_first)
    sends = down_steps.send(b.norm_grad) if tiled else ()
    c = up_and_out_gradients(
        after((m.hidden_low2, m.hidden_low1), sends),
        (m.inner_low2, b.inner_low),
        (m.mixed2, m.mixed1),
        (m.first_low2, b.first_low),
        middle,
    )
    up_sum = sum_middle(route, c.send, c.keep)
    sends = down_steps.send(c.send) if tiled else ()
    a = first_attention_backward(
        seq_lengths,
        after(b.first, sends),
        b.first_low,
        m.qkv1,
        m.lse1,
        m.att_full,
        tokens,
        m.low2,
        m.qkv_grad2,
        (m.norm_grad, b.norm_grad),
        last,
    )
    in_sum = sum_last(route, a.send, a.keep)
    if tiled:
        up_steps, in_steps = up_sum.steps(), in_sum.steps()
        next(up_steps)
        next(in_steps)
        order = [down_steps, up_steps, down_steps, up_steps, in_steps, down_steps, up_steps]
        order += [in_steps, down_steps, up_steps, in_steps, up_steps, in_steps, up_steps, in_steps]
        earlier = a.input_grad
        for chain in order:
            earlier = chain.send(earlier)
        for chain in (down_steps, up_steps, in_steps):
            for earlier in iter(functools.partial(advance, chain, earlier), None):
                pass
    down_share, up_share, inproj_share = down_sum.total(), up_sum.total(), in_sum.total()
    inner = ffn_master.shape[2]
    proj_share = up_share[:, inner:]
    up_share = up_share[:, :inner]
    wide = 3 * width // 4
    totals = (
        jnp.concatenate([inproj_share[:, :wide], proj_share], axis=1),
        jnp.stack([up_share, down_share]),
        inproj_share[:, wide : wide + norm_master.shape[0]].T,
    )
    step_rate = 0.1 / math.sqrt(row_count * lax.axis_size(("dp", "fsdp")))
    att_out = update(totals[0], att_master, att_moment, att_average, step_rate)
    ffn_out = update(totals[1], ffn_master, ffn_moment, ffn_average, step_rate)
    norm_out = update(totals[2], norm_master, norm_moment, norm_average, step_rate)
    return (
        m.layer_output,
        a.input_grad,
        att_out[0],
        att_out[1],
        att_out[2],
        att_out[3],
        att_out[4],
        ffn_out[0],
        ffn_out[1],
        ffn_out[2],
        ffn_out[3],
        ffn_out[4],
        norm_out[0],
        norm_out[1],
        norm_out[2],
        norm_out[3],
        norm_out[4],
    )


def solution(mesh):
    return jax.shard_map(
        shards,
        mesh=mesh,
        in_specs=(
            P(("dp", "fsdp"), None),
            P(("dp", "fsdp"), None),
            P(("dp", "fsdp"), None),
            P(("dp", "fsdp"), None),
            P(None, ("dp", "fsdp"), None),
            P(None, ("dp", "fsdp")),
            P(("dp", "fsdp"), None),
            P(None, ("dp", "fsdp"), None),
            P(None, ("dp", "fsdp")),
            P(("dp", "fsdp"), None),
            P(None, ("dp", "fsdp"), None),
            P(None, ("dp", "fsdp")),
        ),
        out_specs=(
            P(("dp", "fsdp"), None),
            P(("dp", "fsdp"), None),
            P(("dp", "fsdp"), None),
            P(("dp", "fsdp"), None),
            P(("dp", "fsdp"), None),
            P(("dp", "fsdp"), None),
            P(("dp", "fsdp"), None),
            P(None, ("dp", "fsdp"), None),
            P(None, ("dp", "fsdp"), None),
            P(None, ("dp", "fsdp"), None),
            P(None, ("dp", "fsdp"), None),
            P(None, ("dp", "fsdp"), None),
            P(None, ("dp", "fsdp")),
            P(None, ("dp", "fsdp")),
            P(None, ("dp", "fsdp")),
            P(None, ("dp", "fsdp")),
            P(None, ("dp", "fsdp")),
        ),
        check_vma=False,
    )
```

```python
import functools
import math
import types

import jax
import jax.numpy as jnp
from jax import lax
from jax.experimental import pallas as pl
from jax.experimental.pallas import tpu as pltpu
from jax.sharding import PartitionSpec as P

HEAD_DIM = 64


LOW = jnp.bfloat16
SCALE = HEAD_DIM ** (-0.5)
PAIR = 2 * HEAD_DIM
TILE = 512
FF_TILE = 1024
ROWS = 32
NORM_COLS = 128
GELU_RATE = math.sqrt(2.0 / math.pi)
ANYWHERE = pl.BlockSpec(memory_space=pl.ANY)
IN_HBM = pl.BlockSpec(memory_space=pltpu.HBM)
SCALARS = pl.BlockSpec(memory_space=pltpu.SMEM)
VECTORS = pl.BlockSpec(memory_space=pltpu.VMEM)


def launch(body, given, made, scratch, own, products, moved, limit):
    names, specs, arrays = [], [], []
    for name, (spec, value) in given.items():
        group = value if isinstance(value, list) else [value]
        names += [(0, name, isinstance(value, list))] * len(group)
        specs += [spec] * len(group)
        arrays += group
    names += [(0, name, False) for name in (*made, *scratch)]
    names += [(1, name, False) for name in own]

    def kernel(*refs):
        held = ({}, {})
        for (which, name, grouped), ref in zip(names, refs):
            if grouped:
                held[which].setdefault(name, []).append(ref)
            else:
                held[which][name] = ref
        body(*(types.SimpleNamespace(**group) for group in held))

    outs = pl.pallas_call(
        kernel,
        out_shape=[jax.ShapeDtypeStruct(shape, kind) for _, shape, kind in made.values()],
        in_specs=specs,
        out_specs=[spec for spec, _, _ in made.values()],
        scratch_shapes=[*scratch.values(), *own.values()],
        cost_estimate=pl.CostEstimate(
            flops=16 * products, bytes_accessed=moved, transcendentals=0
        ),
        compiler_params=pltpu.CompilerParams(vmem_limit_bytes=limit * 2**20),
    )(*arrays)
    return types.SimpleNamespace(**dict(zip(made, outs)))


class Copies:
    def __init__(self, sem):
        self.sem, self.used, self.open = sem, 0, []

    def start(self, source, target, keep=True):
        copy = pltpu.make_async_copy(source, target, self.sem.at[self.used])
        self.used += 1
        copy.start()
        if keep:
            self.open.append(copy)
        return copy

    def rows(self, parts, owners_ref, target):
        if len(parts) == 1:
            return [self.start(parts[0], target, False)]
        shard = target.shape[0] // owners_ref.shape[0]
        copies = []
        for part in parts:
            for local in range(part.shape[0] // shard):
                row = pl.multiple_of(owners_ref[len(copies)] * shard, shard)
                source = part.at[pl.ds(local * shard, shard)]
                copies.append(self.start(source, target.at[pl.ds(row, shard)], False))
        return copies

    def finish(self):
        for copy in self.open:
            copy.wait()


def wait_all(copies):
    for copy in copies:
        copy.wait()


def product(left, right, left_dim=1, right_dim=0):
    dims = (((left_dim,), (right_dim,)), ((), ()))
    return lax.dot_general(left, right, dims, preferred_element_type=jnp.float32)


def tiles(total, size):
    return [slice(start, start + size) for start in range(0, total, size)]


def fill_mask(lengths_ref, mask_ref):
    shape = mask_ref.shape
    key_row = lax.broadcasted_iota(jnp.int32, shape, 0)
    query_row = lax.broadcasted_iota(jnp.int32, shape, 1)
    end = 0
    key_segment = jnp.zeros(shape, jnp.int32)
    query_segment = jnp.zeros(shape, jnp.int32)
    for slot in range(lengths_ref.shape[1]):
        end = end + lengths_ref[0, slot]
        key_segment += (key_row >= end).astype(jnp.int32)
        query_segment += (query_row >= end).astype(jnp.int32)
    mask_ref[...] = jnp.where(key_segment == query_segment, 0.0, -1e30)


def normalize(values, gain, bias):
    centered = values - jnp.mean(values, axis=-1, keepdims=True)
    spread = jnp.mean(centered * centered, axis=-1, keepdims=True)
    inverse = lax.rsqrt(spread + 1e-05)
    unit = centered * inverse
    return unit, inverse, unit * gain + bias


def normalize_back(grad, unit, inverse, gain):
    scaled = grad * gain
    mean = jnp.mean(scaled, axis=-1, keepdims=True)
    along = jnp.mean(scaled * unit, axis=-1, keepdims=True)
    return inverse * (scaled - mean - unit * along)


def half_lanes(rows, half):
    lane = lax.broadcasted_iota(jnp.int32, (rows, PAIR), 1)
    return (lane >= HEAD_DIM) == bool(half)


def add_norm_grad(norm_grad, row, grad, unit):
    norm_grad[row : row + 1] += jnp.sum(grad * unit, axis=0, keepdims=True)
    norm_grad[row + 1 : row + 2] += jnp.sum(grad, axis=0, keepdims=True)


def attend_forward(rows, low, att, att_ready, mask, qkv, mixed, lse, total, norm, hidden, unit, inverse):
    count, width = low.shape
    att_ready()
    for part in tiles(3 * width, TILE):
        qkv[:, part] = product(low[...], att[:, part]).astype(LOW)
    for pair, part in enumerate(tiles(width, PAIR)):
        query = qkv[:, part] * jnp.asarray(SCALE, LOW)
        key = qkv[:, slice(width + part.start, width + part.stop)]
        value = qkv[:, slice(2 * width + part.start, 2 * width + part.stop)]
        halves, sums = [], []
        for half in (0, 1):
            own = jnp.where(half_lanes(count, half), query, jnp.zeros_like(query))
            scores = product(key, own, 1, 1) + mask[...]
            peak = jnp.max(scores, axis=0, keepdims=True)
            weights = jnp.exp(scores - peak)
            sum_all = jnp.sum(weights, axis=0, keepdims=True)
            sums.append(peak + jnp.log(sum_all))
            out = product(value, weights.astype(LOW), 0, 0)
            halves.append(out[half * HEAD_DIM : (half + 1) * HEAD_DIM] * (1.0 / sum_all))
        lse[pair] = jnp.concatenate(sums, axis=0)
        mixed[:, part] = jnp.concatenate(halves, axis=0).T.astype(LOW)
    for part in tiles(width, TILE):
        out = slice(3 * width + part.start, 3 * width + part.stop)
        total[:, part] = rows[:, part].astype(jnp.float32) + product(mixed[...], att[:, out])
    for block in tiles(count, ROWS):
        unit[block], inverse[block], hidden[block] = normalize(total[block], norm[0:1], norm[1:2])


def ffn_forward(hidden, low, up, down, up_ready, down_ready, active, slope, total):
    low[...] = hidden[...].astype(LOW)
    total[...] = hidden[...]
    up_ready()
    for part in tiles(active.shape[1], FF_TILE):
        inner = product(low[...], up[:, part])
        square = inner * inner
        bend = jnp.tanh(GELU_RATE * inner * (1.0 + 0.044715 * square))
        rise = 0.5 + 0.5 * bend
        act = (inner * rise).astype(LOW)
        active[:, part] = act
        slope[:, part] = (
            rise
            + (0.5 * GELU_RATE) * inner * (1.0 - bend * bend) * (1.0 + 3 * 0.044715 * square)
        ).astype(LOW)
        if part.start == 0:
            down_ready()
        total[...] += product(act, down[:, part], 1, 1)


def ffn_backward(second, out_low, slope, up, down, unit, inverse, norm, inner_low, total, first, first_low, norm_grad, ready=None, norm_ready=None):
    count, _ = second.shape
    total[...] = second[...]
    for index, part in enumerate(tiles(slope.shape[1], FF_TILE)):
        if ready:
            ready(index)
        act = product(out_low[...], down[:, part])
        inner = (act * slope[:, part].astype(jnp.float32)).astype(LOW)
        inner_low[:, part] = inner
        total[...] += product(inner, up[:, part], 1, 1)
    if norm_ready:
        norm_ready()
    for block in tiles(count, ROWS):
        grad, unit_rows = total[block], unit[block]
        add_norm_grad(norm_grad, 0, grad, unit_rows)
        out = normalize_back(grad, unit_rows, inverse[block], norm[0:1])
        first[block] = out
        first_low[block] = out.astype(LOW)


def attend_backward(first, first_low, qkv, lse, mask, att, mixed_grad, qkv_grad, rows_grad, ready=None):
    count, width = first.shape
    if ready:
        ready(3)
    for part in tiles(width, TILE):
        mixed_grad[:, part] = product(
            first_low[...], att[part, 3 * width : 4 * width], 1, 1
        ).astype(LOW)
    for pair, part in enumerate(tiles(width, PAIR)):
        key_part = slice(width + part.start, width + part.stop)
        value_part = slice(2 * width + part.start, 2 * width + part.stop)
        query = qkv[:, part] * jnp.asarray(SCALE, LOW)
        key, value, grad = qkv[:, key_part], qkv[:, value_part], mixed_grad[:, part]
        sums = lse[pair]
        key_grads, value_grads, query_grads = [], [], []
        for half in (0, 1):
            lanes = half_lanes(count, half)
            own_query = jnp.where(lanes, query, jnp.zeros_like(query))
            own_grad = jnp.where(lanes, grad, jnp.zeros_like(grad))
            weights = jnp.exp(product(key, own_query, 1, 1) + mask[...] - sums[half : half + 1])
            weight_grad = product(value, own_grad, 1, 1)
            value_grads.append(product(weights.astype(LOW), grad))
            along = jnp.sum(weights * weight_grad, axis=0, keepdims=True)
            low = (weights * (weight_grad - along)).astype(LOW)
            key_grads.append(product(low, query))
            back = product(key, low, 0, 0)
            query_grads.append(back[half * HEAD_DIM : (half + 1) * HEAD_DIM])
        lanes = half_lanes(count, 1)
        qkv_grad[:, part] = (jnp.concatenate(query_grads, axis=0).T * SCALE).astype(LOW)
        qkv_grad[:, key_part] = jnp.where(lanes, key_grads[1], key_grads[0]).astype(LOW)
        qkv_grad[:, value_part] = jnp.where(lanes, value_grads[1], value_grads[0]).astype(LOW)
    if ready:
        for chunk in range(3):
            ready(chunk)
    for part in tiles(width, TILE):
        rows_grad[:, part] = first[:, part] + product(qkv_grad[...], att[part, : 3 * width], 1, 1)


def weight_sum(picker, lefts, rights, turned, whole, copies, send, keep, offset=0, ready=None):
    count = lefts[0].shape[0]
    half = send.shape[0]
    for layer, left in enumerate(lefts):
        turned[:, layer * count : (layer + 1) * count] = product(
            picker[...], left[...], 1, 1
        ).astype(LOW)
    for index, part in enumerate(tiles(rights[0].shape[1], TILE)):
        if ready:
            ready(index)
        right = jnp.concatenate([ref[:, part] for ref in rights], axis=0)
        start = offset + part.start
        whole[:, start : start + TILE] = product(turned[...], right).astype(LOW)
        columns = pl.ds(start, TILE)
        copies.start(whole.at[pl.ds(0, half), columns], send.at[:, columns])
        copies.start(whole.at[pl.ds(half, half), columns], keep.at[:, columns])


def both_layers(lengths, tokens, cotangent, att_parts, att_owners, up_parts, up_owners, down_parts, down_owners, picker):
    count, width = tokens.shape
    inner = up_parts[0].shape[1]
    wide = att_parts[0].shape[1]
    size, f32 = (count, width), jnp.float32
    results = dict(
        qkv1=((count, 3 * width), LOW),
        mixed1=(size, LOW),
        lse1=((width // PAIR, 2, count), f32),
        hidden_low1=(size, LOW),
        active1=((count, inner), LOW),
        inner_low1=((count, inner), LOW),
        first_low1=(size, LOW),
        low2=(size, LOW),
        mixed2=(size, LOW),
        hidden_low2=(size, LOW),
        layer_output=(size, LOW),
        inner_low2=((count, inner), LOW),
        first_low2=(size, LOW),
        qkv_grad2=((count, 3 * width), LOW),
        norm_grad=((4, width), f32),
    )

    def body(r, own):
        copies = Copies(r.sem)
        att_rows = copies.rows(r.att_parts, r.att_owners, r.held_att)
        up_rows = copies.rows(r.up_parts, r.up_owners, r.held_up)
        down_rows = copies.rows(r.down_parts, r.down_owners, r.held_down)
        picker_copy = copies.start(r.picker, r.held_picker, False)
        fill_mask(r.lengths, r.mask)

        def up_ready():
            wait_all(up_rows)

        def down_ready():
            wait_all(down_rows)

        def give(name):
            copies.start(getattr(own, name), getattr(r, name))

        def att_ready():
            wait_all(att_rows)
            copies.start(r.held_att.at[:, pl.ds(0, 4 * width)], r.att_full)
            turned = r.held_att[:, 4 * width :].astype(f32).T
            r.norm[...] = turned[0:4]

        attend_forward(
            r.tokens,
            r.tokens,
            r.held_att,
            att_ready,
            r.mask,
            own.qkv1,
            own.mixed1,
            own.lse1,
            r.total,
            r.norm,
            r.hidden2,
            r.unit_first,
            r.inverse_first,
        )
        for name in ("qkv1", "mixed1", "lse1"):
            give(name)
        ffn_forward(
            r.hidden2,
            own.hidden_low1,
            r.held_up,
            r.held_down,
            up_ready,
            down_ready,
            own.active1,
            own.inner_low1,
            r.total,
        )
        for name in ("hidden_low1", "active1"):
            give(name)
        for block in tiles(count, ROWS):
            r.unit2[block], r.inverse2[block], rows = normalize(
                r.total[block], r.norm[2:3], r.norm[3:4]
            )
            r.rows[block] = rows
            own.low2[block] = rows.astype(LOW)
        give("low2")
        attend_forward(
            r.rows,
            own.low2,
            r.held_att,
            lambda: None,
            r.mask,
            r.qkv,
            own.mixed2,
            r.lse,
            r.total,
            r.norm,
            r.hidden2,
            r.unit1,
            r.inverse1,
        )
        give("mixed2")
        ffn_forward(
            r.hidden2,
            own.hidden_low2,
            r.held_up,
            r.held_down,
            lambda: None,
            lambda: None,
            r.active2,
            own.inner_low2,
            r.total,
        )
        give("hidden_low2")
        own.norm_grad[...] = jnp.zeros_like(own.norm_grad)
        live = 0
        for slot in range(r.lengths.shape[1]):
            live = live + r.lengths[0, slot]
        for block in tiles(count, ROWS):
            unit, inverse, rows = normalize(r.total[block], r.norm[2:3], r.norm[3:4])
            own.layer_output[block] = rows.astype(LOW)
            position = block.start + lax.broadcasted_iota(jnp.int32, unit.shape, 0)
            grad = jnp.where(position < live, r.cotangent[block].astype(f32), 0.0)
            add_norm_grad(own.norm_grad, 2, grad, unit)
            second = normalize_back(grad, unit, inverse, r.norm[2:3])
            r.rows[block] = second
            r.out_low2[block] = second.astype(LOW)
        give("layer_output")
        ffn_backward(
            r.rows,
            r.out_low2,
            own.inner_low2,
            r.held_up,
            r.held_down,
            r.unit1,
            r.inverse1,
            r.norm,
            own.inner_low2,
            r.total,
            r.rows,
            own.first_low2,
            own.norm_grad,
        )
        for name in ("inner_low2", "first_low2"):
            give(name)
        attend_backward(
            r.rows,
            own.first_low2,
            r.qkv,
            r.lse,
            r.mask,
            r.held_att,
            r.mixed_grad,
            own.qkv_grad2,
            r.total,
        )
        give("qkv_grad2")
        for block in tiles(count, ROWS):
            grad, unit = r.total[block], r.unit2[block]
            add_norm_grad(own.norm_grad, 2, grad, unit)
            second = normalize_back(grad, unit, r.inverse2[block], r.norm[2:3])
            r.rows[block] = second
            r.out_low1[block] = second.astype(LOW)
        ffn_backward(
            r.rows,
            r.out_low1,
            own.inner_low1,
            r.held_up,
            r.held_down,
            r.unit_first,
            r.inverse_first,
            r.norm,
            own.inner_low1,
            r.total,
            r.rows,
            own.first_low1,
            own.norm_grad,
        )
        copies.start(r.rows, r.first1)
        for name in ("inner_low1", "first_low1", "norm_grad"):
            give(name)
        picker_copy.wait()
        weight_sum(
            r.held_picker,
            (r.out_low2, r.out_low1),
            (r.active2, own.active1),
            r.turned,
            r.held_up,
            copies,
            r.send,
            r.keep,
        )
        copies.finish()

    made = {name: (IN_HBM, shape, kind) for name, (shape, kind) in results.items()}
    made |= dict(
        att_full=(IN_HBM, (width, 4 * width), LOW),
        first1=(IN_HBM, size, f32),
        send=(IN_HBM, (width // 2, inner), LOW),
        keep=(IN_HBM, (width // 2, inner), LOW),
    )
    own = {name: pltpu.VMEM(shape, kind) for name, (shape, kind) in results.items()}
    rows_f32 = pltpu.VMEM(size, f32)
    scratch = dict(
        held_up=pltpu.VMEM((width, inner), LOW),
        held_down=pltpu.VMEM((width, inner), LOW),
        held_att=pltpu.VMEM((width, wide), LOW),
        held_picker=pltpu.VMEM((width, width), LOW),
        turned=pltpu.VMEM((width, 2 * count), LOW),
        mask=pltpu.VMEM((count, count), f32),
        qkv=pltpu.VMEM((count, 3 * width), LOW),
        lse=pltpu.VMEM((width // PAIR, 2, count), f32),
        active2=pltpu.VMEM((count, inner), LOW),
        out_low1=pltpu.VMEM(size, LOW),
        out_low2=pltpu.VMEM(size, LOW),
        unit_first=rows_f32,
        inverse_first=pltpu.VMEM((count, 1), f32),
        mixed_grad=pltpu.VMEM(size, LOW),
        inverse1=pltpu.VMEM((count, 1), f32),
        inverse2=pltpu.VMEM((count, 1), f32),
        norm=pltpu.VMEM((4, width), f32),
        total=rows_f32,
        rows=rows_f32,
        hidden2=rows_f32,
        unit1=rows_f32,
        unit2=rows_f32,
    )
    loads = 3 * up_owners.size
    copies = loads + len(results) + 5 + 2 * (inner // TILE)
    scratch |= dict(sem=pltpu.SemaphoreType.DMA((copies,)))
    return launch(
        body,
        dict(
            lengths=(SCALARS, lengths),
            up_owners=(SCALARS, up_owners),
            down_owners=(SCALARS, down_owners),
            att_owners=(SCALARS, att_owners),
            tokens=(VECTORS, tokens),
            cotangent=(VECTORS, cotangent),
            att_parts=(IN_HBM, att_parts),
            picker=(IN_HBM, picker),
            up_parts=(IN_HBM, up_parts),
            down_parts=(IN_HBM, down_parts),
        ),
        made,
        scratch,
        own,
        count * width * (10 * inner + 12 * width) + 9 * count * count * width,
        12 * width * inner,
        60,
    )


def up_gradient(lefts, rights, picker):
    count, width = lefts[0].shape
    inner = rights[0].shape[1]

    def body(r, own):
        copies = Copies(r.sem)
        parts = []
        for part in tiles(inner, TILE):
            part = pl.ds(part.start, TILE)
            pair = zip(r.rights, (own.right_a, own.right_b))
            parts.append([copies.start(a.at[:, part], b.at[:, part], False) for a, b in pair])
        weight_sum(
            r.picker,
            r.lefts,
            (own.right_a, own.right_b),
            r.turned,
            r.whole,
            copies,
            r.send,
            r.keep,
            0,
            lambda index: wait_all(parts[index]),
        )
        copies.finish()

    right = pltpu.VMEM((count, inner), LOW)
    return launch(
        body,
        dict(
            picker=(VECTORS, picker),
            lefts=(VECTORS, list(lefts)),
            rights=(IN_HBM, list(rights)),
        ),
        dict(
            send=(IN_HBM, (width // 2, inner), LOW),
            keep=(IN_HBM, (width // 2, inner), LOW),
        ),
        dict(
            whole=pltpu.VMEM((width, inner), LOW),
            turned=pltpu.VMEM((width, 2 * count), LOW),
            sem=pltpu.SemaphoreType.DMA((4 * (inner // TILE),)),
        ),
        dict(right_a=right, right_b=right),
        count * width * 2 * (inner + width),
        4 * width * inner,
        60,
    )


def first_attention_backward(lengths, first, first_low, qkv, lse, att, tokens, low2, qkv_grad2, mixed, first_low2, norm_grad, picker):
    count, width = first.shape
    size, f32 = (count, width), jnp.float32
    late = dict(
        picker=picker,
        low2=low2,
        tokens=tokens,
        qkv_grad2=qkv_grad2,
        mixed1=mixed[0],
        mixed2=mixed[1],
        first_low2=first_low2,
    )
    wide = 4 * width + NORM_COLS

    def body(r, own):
        copies = Copies(r.sem)
        chunks = [None] * 4
        for chunk in (3, 0, 1, 2):
            part = pl.ds(chunk * width, width)
            chunks[chunk] = copies.start(r.att.at[:, part], r.held.at[:, part], False)
        loads = [copies.start(getattr(r, n), getattr(own, n), False) for n in late]
        fill_mask(r.lengths, r.mask)
        attend_backward(
            r.first,
            r.first_low,
            r.qkv,
            r.lse,
            r.mask,
            r.held,
            r.mixed_grad,
            r.qkv_grad,
            r.input_grad,
            lambda chunk: chunks[chunk].wait(),
        )
        wait_all(loads)
        weight_sum(
            own.picker,
            (own.low2, own.tokens),
            (own.qkv_grad2, r.qkv_grad),
            r.turned,
            r.whole,
            copies,
            r.send,
            r.keep,
        )
        weight_sum(
            own.picker,
            (own.mixed2, own.mixed1),
            (own.first_low2, r.first_low),
            r.turned,
            r.whole,
            copies,
            r.send,
            r.keep,
            3 * width,
        )
        r.norm_rows[...] = jnp.zeros_like(r.norm_rows)
        r.norm_rows[0:4] = r.norm_grad[...].astype(LOW)
        extra = product(own.picker[...], r.norm_rows[...], 1, 1).astype(LOW)
        half = width // 2
        r.extra[...] = extra
        columns = pl.ds(4 * width, NORM_COLS)
        copies.start(r.extra.at[pl.ds(0, half)], r.send.at[:, columns])
        copies.start(r.extra.at[pl.ds(half, half)], r.keep.at[:, columns])
        copies.finish()

    given = dict(
        lengths=(SCALARS, lengths),
        first=(VECTORS, first),
        first_low=(VECTORS, first_low),
        qkv=(VECTORS, qkv),
        lse=(VECTORS, lse),
        norm_grad=(VECTORS, norm_grad),
        att=(IN_HBM, att),
    )
    given |= {name: (IN_HBM, value) for name, value in late.items()}
    own = {name: pltpu.VMEM(value.shape, LOW) for name, value in late.items()}
    scratch = dict(
        held=pltpu.VMEM((width, 4 * width), LOW),
        mask=pltpu.VMEM((count, count), f32),
        mixed_grad=pltpu.VMEM(size, LOW),
        qkv_grad=pltpu.VMEM((count, 3 * width), LOW),
        turned=pltpu.VMEM((width, 2 * count), LOW),
        whole=pltpu.VMEM((width, 4 * width), LOW),
        norm_rows=pltpu.VMEM((NORM_COLS, width), LOW),
        extra=pltpu.VMEM((width, NORM_COLS), LOW),
        sem=pltpu.SemaphoreType.DMA((4 + len(late) + 2 + 2 * (4 * width // TILE),)),
    )
    return launch(
        body,
        given,
        dict(
            input_grad=(VECTORS, size, f32),
            send=(IN_HBM, (width // 2, wide), LOW),
            keep=(IN_HBM, (width // 2, wide), LOW),
        ),
        scratch,
        own,
        count * width * 14 * width + 5 * count * count * width,
        16 * width * width,
        60,
    )


AXES = ("dp", "fsdp")


class Route:
    def __init__(self):
        rows, cols = lax.axis_size("dp"), lax.axis_size("fsdp")
        self.inner = cols // 4
        self.ring_size = rows // 2 * self.inner
        self.cols = cols
        self.world = rows * cols
        row, col = lax.axis_index("dp"), lax.axis_index("fsdp")
        self.q = row // 2 * self.inner + col // 4
        self.y, self.x, self.c = row % 2, col // 2 % 2, col % 2

    def joint(self, q, y, x, c):
        return (q // self.inner * 2 + y) * self.cols + q % self.inner * 4 + x * 2 + c

    def move(self, array, step):
        pairs = []
        for q in range(self.ring_size):
            for y in (0, 1):
                for x in (0, 1):
                    for c in (0, 1):
                        to = step(q, y, x, c)
                        pairs.append((self.joint(q, y, x, c), self.joint(*to)))
        return lax.ppermute(array, AXES, pairs)

    def ring(self, array, hops=1):
        return self.move(array, lambda q, y, x, c: ((q + hops) % self.ring_size, y, x, c))

    def core(self, array):
        return self.move(array, lambda q, y, x, c: (q, y, x, 1 - c))

    def first(self, array):
        return self.move(array, lambda q, y, x, c: (q, y ^ c, x ^ (1 - c), c))

    def second(self, array):
        return self.move(array, lambda q, y, x, c: (q, y ^ (1 - c), x ^ c, c))

    def owner(self, back, first, second, core):
        c = self.c ^ core
        x = self.x ^ jnp.where(c == 0, first, second)
        y = self.y ^ jnp.where(c == 0, second, first)
        return self.joint((self.q + self.ring_size - back) % self.ring_size, y, x, c)


def after(value, *earlier):
    return lax.optimization_barrier((value, earlier))[0]


def gather_all(route, att, up, down, besides):
    last = route.ring_size - 1
    pairs = [[jnp.concatenate([piece, route.first(piece)])] for piece in (att, up)]
    chains = (*pairs, [down])
    others = [[route.second(chain[0])] for chain in pairs]
    turns = [2] + [which for _ in range(last - 1) for which in (0, 2)] + [1, 0] + [1] * (last - 1)
    arrived = [(), ()]
    first = crossed = ()
    for turn, which in enumerate(turns):
        early = ()
        if turn == 3:
            early = others[1][0]
        if turn == len(turns) - 1:
            early = crossed
        before = arrived[turn - 1] if which == 1 and len(chains[1]) == 1 and turn else arrived[turn]
        here = after(chains[which][-1], (before, early))
        chains[which].append(route.ring(here))
        arrived.append(chains[which][-1])
        if which < 2 and len(chains[which]) > 2:
            others[which].append(route.second(here))
        if which == 2 and len(chains[2]) > last:
            base = jnp.concatenate(chains[2])
            first = route.first(base)
            both = route.second(after(base, others[0][1]))
            crossed = route.second(after(first, others[0][1]))
    others[0].append(route.second(after(pairs[0][last], first)))
    others[1].append(route.second(after(pairs[1][last], others[0][last])))
    arrays, owners = [[], [], []], [[], [], []]

    def add(which, block, second, blocks, when):
        for core in (0, 1):
            arrays[which].append(route.core(after(block, when)) if core else block)
            owners[which] += [route.owner(back, flip, second, core) for back, flip in blocks]

    for which, chain in enumerate(pairs):
        for k in range(last + 1):
            blocks = [(k, 0), (k, 1)]
            add(which, chain[k], 0, blocks, ())
            add(which, others[which][k], 1, blocks, pairs[1][min(k + 1 + which, last)])
    rows = range(last + 1)
    add(2, base, 0, [(k, 0) for k in rows], (pairs[0][last], besides))
    add(2, first, 0, [(k, 1) for k in rows], pairs[1][max(last - 1, 0)])
    add(2, both, 1, [(k, 0) for k in rows], pairs[1][last])
    add(2, crossed, 1, [(k, 1) for k in rows], pairs[1][last])
    return arrays, owners


def row_picker(owners, shard):
    rows = (jnp.stack(owners)[:, None] * shard + jnp.arange(shard)[None, :]).reshape(-1, 1)
    return (rows == jnp.arange(rows.size)[None, :]).astype(jnp.bfloat16)


def add_all(*terms):
    total = terms[0].astype(jnp.float32)
    for term in terms[1:]:
        total = total + term.astype(jnp.float32)
    return total


def add_low(*terms):
    return add_all(*terms).astype(jnp.bfloat16)


def owners_ring_last(route):
    return [
        route.owner(1 + j, first, second, core)
        for core in (1, 0)
        for second in (1, 0)
        for first in (1, 0)
        for j in range(route.ring_size)
    ]


def owners_ring_middle(route):
    return [
        route.owner(1 + j, first, second, core)
        for core in (1, 0)
        for second in (1, 0)
        for j in range(route.ring_size)
        for first in (1, 0)
    ]


def cut(array, count):
    size = array.shape[0] // count
    return [array[k * size : (k + 1) * size] for k in range(count)]


class SumWhole:
    def __init__(self, route, upper, lower, eager=False):
        self.term = jnp.concatenate([upper, lower])

    def steps(self):
        return iter(())

    def total(self):
        return lax.psum_scatter(self.term, AXES, scatter_dimension=0, tiled=True).astype(
            jnp.float32
        )


class SumRingMiddle:
    def __init__(self, route, send, keep, eager=False):
        self.route, self.terms, self.eager = route, (keep, route.core(send)), eager
        self.result = None

    def steps(self):
        route, terms = self.route, self.terms
        count = route.ring_size
        half = terms[0].shape[0] // 2
        block = half // count
        earlier = yield
        others = []
        for cut in (slice(0, half // 2), slice(half // 2, half)):
            send = add_low(*(part[cut] for part in after(terms, earlier)))
            others.append(route.second(send))
            earlier = yield send
        moving = None
        for j in range(count):
            arrived = [] if moving is None else [route.ring(moving)]
            due = 2 if j and self.eager else 2 * j // count + 1
            near, far, arrived = after((terms, others[:due], arrived), earlier)
            start = half + j * block
            local = [part[start : start + block] for part in near]
            offset = j * block % (half // 2)
            local.append(far[2 * j // count][offset : offset + block])
            local += arrived
            if j < count - 1:
                moving = add_low(*local)
                earlier = yield moving
        shard = block // 2
        turned = add_low(*(part[:shard] for part in local))
        rest = add_all(*(part[shard:] for part in local))
        earlier = yield (turned, rest)
        self.result = rest + after(route.first(turned), earlier).astype(jnp.float32)
        yield self.result

    def total(self):
        return self.result


class SumRingLast:
    def __init__(self, route, send, keep):
        self.route, self.terms = route, [keep, route.core(send)]
        self.result = None

    def steps(self):
        route, terms = self.route, self.terms
        earlier = yield
        start, total = 0, terms[0].shape[0]
        for step in (route.second, route.first):
            half = (total - start) // 2
            near = after(terms, earlier)
            send = add_low(*self.part(near, start, half))
            start += half
            terms = terms + [step(send)]
            earlier = yield send
        block = (total - start) // route.ring_size
        moving = None
        for j in range(route.ring_size):
            arrived = [] if moving is None else [route.ring(moving)]
            near, arrived = after((terms, arrived), earlier)
            local = self.part(near, start + j * block, block) + arrived
            if j < route.ring_size - 1:
                moving = add_low(*local)
                earlier = yield moving
        self.result = add_all(*local)
        yield self.result

    @staticmethod
    def part(terms, start, size):
        total = terms[0].shape[0]
        skips = [start - (total - term.shape[0]) for term in terms]
        return [term[skip : skip + size] for term, skip in zip(terms, skips)]

    def total(self):
        return self.result


def advance(chain, earlier):
    try:
        return chain.send(earlier)
    except StopIteration:
        return None


def update(gradient, master, moment, average, step_rate):
    moment_new = 0.9 * moment + gradient
    master_new = master - step_rate * (gradient + 0.9 * moment_new)
    average_new = 0.8 * average + 0.2 * master_new
    return (gradient, moment_new, master_new, average_new, master_new.astype(jnp.bfloat16))


def shards(
    tokens,
    cotangent,
    seq_lengths,
    att_master,
    ffn_master,
    norm_master,
    att_moment,
    ffn_moment,
    norm_moment,
    att_average,
    ffn_average,
    norm_average,
):
    row_count = tokens.shape[0]
    route = Route()
    shard = att_master.shape[0]
    norm_piece = jnp.pad(norm_master.T, ((0, 0), (0, NORM_COLS - norm_master.shape[0])))
    att_piece = jnp.concatenate([att_master, norm_piece], axis=1).astype(jnp.bfloat16)
    ffn_pieces = ffn_master.astype(jnp.bfloat16)
    width = att_master.shape[1]
    tiled = shard % 16 == 0
    if tiled:
        middle = row_picker(owners_ring_middle(route), shard)
        last = row_picker(owners_ring_last(route), shard)
        arrays, owners = gather_all(route, att_piece, *ffn_pieces, (middle, last))
        sum_middle, sum_last = SumRingMiddle, SumRingLast
    else:
        middle = last = row_picker(list(range(route.world)), shard)
        pieces = (att_piece, *ffn_pieces)
        arrays = [[lax.all_gather(piece, AXES, axis=0, tiled=True)] for piece in pieces]
        owners = [[0]] * 3
        sum_middle = sum_last = SumWhole
    owned = [
        jnp.stack(rows).astype(jnp.int32) if tiled else jnp.zeros(1, jnp.int32) for rows in owners
    ]
    m = both_layers(
        seq_lengths,
        tokens,
        cotangent,
        arrays[0],
        owned[0],
        arrays[1],
        owned[1],
        arrays[2],
        owned[2],
        middle,
    )
    down_sum = sum_middle(route, m.send, m.keep, True)
    down_steps = down_sum.steps()
    next(down_steps, None)
    c = up_gradient((m.hidden_low2, m.hidden_low1), (m.inner_low2, m.inner_low1), middle)
    up_sum = sum_middle(route, c.send, c.keep)
    sends = down_steps.send(c.send) if tiled else ()
    sends = down_steps.send(sends) if tiled else ()
    a = first_attention_backward(
        seq_lengths,
        after(m.first1, sends),
        m.first_low1,
        m.qkv1,
        m.lse1,
        m.att_full,
        tokens,
        m.low2,
        m.qkv_grad2,
        (m.mixed1, m.mixed2),
        m.first_low2,
        m.norm_grad,
        last,
    )
    in_sum = sum_last(route, a.send, a.keep)
    step_rate = 0.1 / math.sqrt(row_count * lax.axis_size(AXES))

    def ffn_update():
        shares = jnp.stack([up_sum.total(), down_sum.total()])
        return update(shares, ffn_master, ffn_moment, ffn_average, step_rate)

    if tiled:
        up_steps, in_steps = up_sum.steps(), in_sum.steps()
        next(up_steps)
        next(in_steps)
        order = [down_steps, up_steps, up_steps, down_steps, up_steps, in_steps, down_steps]
        order += [up_steps, in_steps, down_steps, up_steps, in_steps, down_steps, up_steps]
        order += [in_steps, up_steps, in_steps]
        earlier = a.input_grad
        for chain in order:
            earlier = chain.send(earlier)
        for chain in (down_steps, up_steps):
            for earlier in iter(functools.partial(advance, chain, earlier), None):
                pass
        ffn_out = ffn_update()
        earlier = (earlier, ffn_out)
        for earlier in iter(functools.partial(advance, in_steps, earlier), None):
            pass
    else:
        ffn_out = ffn_update()
    att_total = in_sum.total()
    norm_total = lax.dot_general(
        jnp.eye(norm_master.shape[0], NORM_COLS, dtype=jnp.float32),
        att_total[:, width:],
        (((1,), (1,)), ((), ())),
        precision=lax.Precision.HIGHEST,
    )
    att_out = update(att_total[:, :width], att_master, att_moment, att_average, step_rate)
    norm_out = update(norm_total, norm_master, norm_moment, norm_average, step_rate)
    return (
        m.layer_output,
        a.input_grad,
        att_out[0],
        att_out[1],
        att_out[2],
        att_out[3],
        att_out[4],
        ffn_out[0],
        ffn_out[1],
        ffn_out[2],
        ffn_out[3],
        ffn_out[4],
        norm_out[0],
        norm_out[1],
        norm_out[2],
        norm_out[3],
        norm_out[4],
    )


def solution(mesh):
    return jax.shard_map(
        shards,
        mesh=mesh,
        in_specs=(
            P(("dp", "fsdp"), None),
            P(("dp", "fsdp"), None),
            P(("dp", "fsdp"), None),
            P(("dp", "fsdp"), None),
            P(None, ("dp", "fsdp"), None),
            P(None, ("dp", "fsdp")),
            P(("dp", "fsdp"), None),
            P(None, ("dp", "fsdp"), None),
            P(None, ("dp", "fsdp")),
            P(("dp", "fsdp"), None),
            P(None, ("dp", "fsdp"), None),
            P(None, ("dp", "fsdp")),
        ),
        out_specs=(
            P(("dp", "fsdp"), None),
            P(("dp", "fsdp"), None),
            P(("dp", "fsdp"), None),
            P(("dp", "fsdp"), None),
            P(("dp", "fsdp"), None),
            P(("dp", "fsdp"), None),
            P(("dp", "fsdp"), None),
            P(None, ("dp", "fsdp"), None),
            P(None, ("dp", "fsdp"), None),
            P(None, ("dp", "fsdp"), None),
            P(None, ("dp", "fsdp"), None),
            P(None, ("dp", "fsdp"), None),
            P(None, ("dp", "fsdp")),
            P(None, ("dp", "fsdp")),
            P(None, ("dp", "fsdp")),
            P(None, ("dp", "fsdp")),
            P(None, ("dp", "fsdp")),
        ),
        check_vma=False,
    )
```

```python
import functools
import math
import types

import jax
import jax.numpy as jnp
from jax import lax
from jax.experimental import pallas as pl
from jax.experimental.pallas import tpu as pltpu
from jax.sharding import PartitionSpec as P

HEAD_DIM = 64


LOW = jnp.bfloat16
SCALE = HEAD_DIM ** (-0.5)
PAIR = 2 * HEAD_DIM
TILE = 512
FF_TILE = 1024
ROWS = 32
NORM_COLS = 128
GELU_RATE = math.sqrt(2.0 / math.pi)
ANYWHERE = pl.BlockSpec(memory_space=pl.ANY)
IN_HBM = pl.BlockSpec(memory_space=pltpu.HBM)
SCALARS = pl.BlockSpec(memory_space=pltpu.SMEM)
VECTORS = pl.BlockSpec(memory_space=pltpu.VMEM)


def launch(body, given, made, scratch, own, products, moved, limit):
    names, specs, arrays = [], [], []
    for name, (spec, value) in given.items():
        group = value if isinstance(value, list) else [value]
        names += [(0, name, isinstance(value, list))] * len(group)
        specs += [spec] * len(group)
        arrays += group
    names += [(0, name, False) for name in (*made, *scratch)]
    names += [(1, name, False) for name in own]

    def kernel(*refs):
        held = ({}, {})
        for (which, name, grouped), ref in zip(names, refs):
            if grouped:
                held[which].setdefault(name, []).append(ref)
            else:
                held[which][name] = ref
        body(*(types.SimpleNamespace(**group) for group in held))

    outs = pl.pallas_call(
        kernel,
        out_shape=[jax.ShapeDtypeStruct(shape, kind) for _, shape, kind in made.values()],
        in_specs=specs,
        out_specs=[spec for spec, _, _ in made.values()],
        scratch_shapes=[*scratch.values(), *own.values()],
        cost_estimate=pl.CostEstimate(
            flops=16 * products, bytes_accessed=moved, transcendentals=0
        ),
        compiler_params=pltpu.CompilerParams(vmem_limit_bytes=limit * 2**20),
    )(*arrays)
    return types.SimpleNamespace(**dict(zip(made, outs)))


class Copies:
    def __init__(self, sem):
        self.sem, self.used, self.open = sem, 0, []

    def start(self, source, target, keep=True):
        copy = pltpu.make_async_copy(source, target, self.sem.at[self.used])
        self.used += 1
        copy.start()
        if keep:
            self.open.append(copy)
        return copy

    def rows(self, parts, owners_ref, target):
        if len(parts) == 1:
            return [self.start(parts[0], target, False)]
        shard = target.shape[0] // owners_ref.shape[0]
        copies = []
        for part in parts:
            for local in range(part.shape[0] // shard):
                row = pl.multiple_of(owners_ref[len(copies)] * shard, shard)
                source = part.at[pl.ds(local * shard, shard)]
                copies.append(self.start(source, target.at[pl.ds(row, shard)], False))
        return copies

    def finish(self):
        for copy in self.open:
            copy.wait()


def wait_all(copies):
    for copy in copies:
        copy.wait()


def product(left, right, left_dim=1, right_dim=0):
    dims = (((left_dim,), (right_dim,)), ((), ()))
    return lax.dot_general(left, right, dims, preferred_element_type=jnp.float32)


def tiles(total, size):
    return [slice(start, start + size) for start in range(0, total, size)]


def fill_mask(lengths_ref, mask_ref):
    shape = mask_ref.shape
    key_row = lax.broadcasted_iota(jnp.int32, shape, 0)
    query_row = lax.broadcasted_iota(jnp.int32, shape, 1)
    end = 0
    key_segment = jnp.zeros(shape, jnp.int32)
    query_segment = jnp.zeros(shape, jnp.int32)
    for slot in range(lengths_ref.shape[1]):
        end = end + lengths_ref[0, slot]
        key_segment += (key_row >= end).astype(jnp.int32)
        query_segment += (query_row >= end).astype(jnp.int32)
    mask_ref[...] = jnp.where(key_segment == query_segment, 0.0, -1e30)


def normalize(values, gain, bias):
    centered = values - jnp.mean(values, axis=-1, keepdims=True)
    spread = jnp.mean(centered * centered, axis=-1, keepdims=True)
    inverse = lax.rsqrt(spread + 1e-05)
    unit = centered * inverse
    return unit, inverse, unit * gain + bias


def normalize_back(grad, unit, inverse, gain):
    scaled = grad * gain
    mean = jnp.mean(scaled, axis=-1, keepdims=True)
    along = jnp.mean(scaled * unit, axis=-1, keepdims=True)
    return inverse * (scaled - mean - unit * along)


def half_lanes(rows, half):
    lane = lax.broadcasted_iota(jnp.int32, (rows, PAIR), 1)
    return (lane >= HEAD_DIM) == bool(half)


def add_norm_grad(norm_grad, row, grad, unit):
    norm_grad[row : row + 1] += jnp.sum(grad * unit, axis=0, keepdims=True)
    norm_grad[row + 1 : row + 2] += jnp.sum(grad, axis=0, keepdims=True)


def attend_forward(rows, low, att, att_ready, mask, qkv, mixed, lse, total, norm, hidden, unit, inverse):
    count, width = low.shape
    att_ready()
    for part in tiles(3 * width, TILE):
        qkv[:, part] = product(low[...], att[:, part]).astype(LOW)
    for pair, part in enumerate(tiles(width, PAIR)):
        query = qkv[:, part] * jnp.asarray(SCALE, LOW)
        key = qkv[:, slice(width + part.start, width + part.stop)]
        value = qkv[:, slice(2 * width + part.start, 2 * width + part.stop)]
        halves, sums = [], []
        for half in (0, 1):
            own = jnp.where(half_lanes(count, half), query, jnp.zeros_like(query))
            scores = product(key, own, 1, 1) + mask[...]
            peak = jnp.max(scores, axis=0, keepdims=True)
            weights = jnp.exp(scores - peak)
            sum_all = jnp.sum(weights, axis=0, keepdims=True)
            sums.append(peak + jnp.log(sum_all))
            out = product(value, weights.astype(LOW), 0, 0)
            halves.append(out[half * HEAD_DIM : (half + 1) * HEAD_DIM] * (1.0 / sum_all))
        lse[pair] = jnp.concatenate(sums, axis=0)
        mixed[:, part] = jnp.concatenate(halves, axis=0).T.astype(LOW)
    for part in tiles(width, TILE):
        out = slice(3 * width + part.start, 3 * width + part.stop)
        total[:, part] = rows[:, part].astype(jnp.float32) + product(mixed[...], att[:, out])
    for block in tiles(count, ROWS):
        unit[block], inverse[block], hidden[block] = normalize(total[block], norm[0:1], norm[1:2])


def ffn_forward(hidden, low, up, down, up_ready, down_ready, active, slope, total):
    low[...] = hidden[...].astype(LOW)
    total[...] = hidden[...]
    up_ready()
    for part in tiles(active.shape[1], FF_TILE):
        inner = product(low[...], up[:, part])
        square = inner * inner
        bend = jnp.tanh(GELU_RATE * inner * (1.0 + 0.044715 * square))
        rise = 0.5 + 0.5 * bend
        act = (inner * rise).astype(LOW)
        active[:, part] = act
        slope[:, part] = (
            rise
            + (0.5 * GELU_RATE) * inner * (1.0 - bend * bend) * (1.0 + 3 * 0.044715 * square)
        ).astype(LOW)
        if part.start == 0:
            down_ready()
        total[...] += product(act, down[:, part], 1, 1)


def ffn_backward(second, out_low, slope, up, down, unit, inverse, norm, inner_low, total, first, first_low, norm_grad, ready=None, norm_ready=None):
    count, _ = second.shape
    total[...] = second[...]
    for index, part in enumerate(tiles(slope.shape[1], FF_TILE)):
        if ready:
            ready(index)
        act = product(out_low[...], down[:, part])
        inner = (act * slope[:, part].astype(jnp.float32)).astype(LOW)
        inner_low[:, part] = inner
        total[...] += product(inner, up[:, part], 1, 1)
    if norm_ready:
        norm_ready()
    for block in tiles(count, ROWS):
        grad, unit_rows = total[block], unit[block]
        add_norm_grad(norm_grad, 0, grad, unit_rows)
        out = normalize_back(grad, unit_rows, inverse[block], norm[0:1])
        first[block] = out
        first_low[block] = out.astype(LOW)


def attend_backward(first, first_low, qkv, lse, mask, att, mixed_grad, qkv_grad, rows_grad, ready=None):
    count, width = first.shape
    if ready:
        ready(3)
    for part in tiles(width, TILE):
        mixed_grad[:, part] = product(
            first_low[...], att[part, 3 * width : 4 * width], 1, 1
        ).astype(LOW)
    for pair, part in enumerate(tiles(width, PAIR)):
        key_part = slice(width + part.start, width + part.stop)
        value_part = slice(2 * width + part.start, 2 * width + part.stop)
        query = qkv[:, part] * jnp.asarray(SCALE, LOW)
        key, value, grad = qkv[:, key_part], qkv[:, value_part], mixed_grad[:, part]
        sums = lse[pair]
        key_grads, value_grads, query_grads = [], [], []
        for half in (0, 1):
            lanes = half_lanes(count, half)
            own_query = jnp.where(lanes, query, jnp.zeros_like(query))
            own_grad = jnp.where(lanes, grad, jnp.zeros_like(grad))
            weights = jnp.exp(product(key, own_query, 1, 1) + mask[...] - sums[half : half + 1])
            weight_grad = product(value, own_grad, 1, 1)
            value_grads.append(product(weights.astype(LOW), grad))
            along = jnp.sum(weights * weight_grad, axis=0, keepdims=True)
            low = (weights * (weight_grad - along)).astype(LOW)
            key_grads.append(product(low, query))
            back = product(key, low, 0, 0)
            query_grads.append(back[half * HEAD_DIM : (half + 1) * HEAD_DIM])
        lanes = half_lanes(count, 1)
        qkv_grad[:, part] = (jnp.concatenate(query_grads, axis=0).T * SCALE).astype(LOW)
        qkv_grad[:, key_part] = jnp.where(lanes, key_grads[1], key_grads[0]).astype(LOW)
        qkv_grad[:, value_part] = jnp.where(lanes, value_grads[1], value_grads[0]).astype(LOW)
    if ready:
        for chunk in range(3):
            ready(chunk)
    for part in tiles(width, TILE):
        rows_grad[:, part] = first[:, part] + product(qkv_grad[...], att[part, : 3 * width], 1, 1)


def weight_sum(picker, lefts, rights, turned, whole, copies, send, keep, offset=0, ready=None):
    count = lefts[0].shape[0]
    half = send.shape[0]
    for layer, left in enumerate(lefts):
        turned[:, layer * count : (layer + 1) * count] = product(
            picker[...], left[...], 1, 1
        ).astype(LOW)
    for index, part in enumerate(tiles(rights[0].shape[1], TILE)):
        if ready:
            ready(index)
        right = jnp.concatenate([ref[:, part] for ref in rights], axis=0)
        start = offset + part.start
        whole[:, start : start + TILE] = product(turned[...], right).astype(LOW)
        columns = pl.ds(start, TILE)
        copies.start(whole.at[pl.ds(0, half), columns], send.at[:, columns])
        copies.start(whole.at[pl.ds(half, half), columns], keep.at[:, columns])


def both_layers(lengths, tokens, cotangent, att_parts, att_owners, up_parts, up_owners, down_parts, down_owners, picker):
    count, width = tokens.shape
    inner = up_parts[0].shape[1]
    wide = att_parts[0].shape[1]
    size, f32 = (count, width), jnp.float32
    results = dict(
        qkv1=((count, 3 * width), LOW),
        mixed1=(size, LOW),
        lse1=((width // PAIR, 2, count), f32),
        hidden_low1=(size, LOW),
        active1=((count, inner), LOW),
        inner_low1=((count, inner), LOW),
        first_low1=(size, LOW),
        low2=(size, LOW),
        mixed2=(size, LOW),
        hidden_low2=(size, LOW),
        layer_output=(size, LOW),
        inner_low2=((count, inner), LOW),
        first_low2=(size, LOW),
        qkv_grad2=((count, 3 * width), LOW),
        norm_grad=((4, width), f32),
    )

    def body(r, own):
        copies = Copies(r.sem)
        att_rows = copies.rows(r.att_parts, r.att_owners, r.held_att)
        up_rows = copies.rows(r.up_parts, r.up_owners, r.held_up)
        down_rows = copies.rows(r.down_parts, r.down_owners, r.held_down)
        picker_copy = copies.start(r.picker, r.held_picker, False)
        fill_mask(r.lengths, r.mask)

        def up_ready():
            wait_all(up_rows)

        def down_ready():
            wait_all(down_rows)

        def give(name):
            copies.start(getattr(own, name), getattr(r, name))

        def att_ready():
            wait_all(att_rows)
            copies.start(r.held_att.at[:, pl.ds(0, 4 * width)], r.att_full)
            turned = r.held_att[:, 4 * width :].astype(f32).T
            r.norm[...] = turned[0:4]

        attend_forward(
            r.tokens,
            r.tokens,
            r.held_att,
            att_ready,
            r.mask,
            own.qkv1,
            own.mixed1,
            own.lse1,
            r.total,
            r.norm,
            r.hidden2,
            r.unit_first,
            r.inverse_first,
        )
        for name in ("qkv1", "mixed1", "lse1"):
            give(name)
        ffn_forward(
            r.hidden2,
            own.hidden_low1,
            r.held_up,
            r.held_down,
            up_ready,
            down_ready,
            own.active1,
            own.inner_low1,
            r.total,
        )
        for name in ("hidden_low1", "active1"):
            give(name)
        for block in tiles(count, ROWS):
            r.unit2[block], r.inverse2[block], rows = normalize(
                r.total[block], r.norm[2:3], r.norm[3:4]
            )
            r.rows[block] = rows
            own.low2[block] = rows.astype(LOW)
        give("low2")
        attend_forward(
            r.rows,
            own.low2,
            r.held_att,
            lambda: None,
            r.mask,
            r.qkv,
            own.mixed2,
            r.lse,
            r.total,
            r.norm,
            r.hidden2,
            r.unit1,
            r.inverse1,
        )
        give("mixed2")
        ffn_forward(
            r.hidden2,
            own.hidden_low2,
            r.held_up,
            r.held_down,
            lambda: None,
            lambda: None,
            r.active2,
            own.inner_low2,
            r.total,
        )
        give("hidden_low2")
        own.norm_grad[...] = jnp.zeros_like(own.norm_grad)
        live = 0
        for slot in range(r.lengths.shape[1]):
            live = live + r.lengths[0, slot]
        for block in tiles(count, ROWS):
            unit, inverse, rows = normalize(r.total[block], r.norm[2:3], r.norm[3:4])
            own.layer_output[block] = rows.astype(LOW)
            position = block.start + lax.broadcasted_iota(jnp.int32, unit.shape, 0)
            grad = jnp.where(position < live, r.cotangent[block].astype(f32), 0.0)
            add_norm_grad(own.norm_grad, 2, grad, unit)
            second = normalize_back(grad, unit, inverse, r.norm[2:3])
            r.rows[block] = second
            r.out_low2[block] = second.astype(LOW)
        give("layer_output")
        ffn_backward(
            r.rows,
            r.out_low2,
            own.inner_low2,
            r.held_up,
            r.held_down,
            r.unit1,
            r.inverse1,
            r.norm,
            own.inner_low2,
            r.total,
            r.rows,
            own.first_low2,
            own.norm_grad,
        )
        for name in ("inner_low2", "first_low2"):
            give(name)
        attend_backward(
            r.rows,
            own.first_low2,
            r.qkv,
            r.lse,
            r.mask,
            r.held_att,
            r.mixed_grad,
            own.qkv_grad2,
            r.total,
        )
        give("qkv_grad2")
        for block in tiles(count, ROWS):
            grad, unit = r.total[block], r.unit2[block]
            add_norm_grad(own.norm_grad, 2, grad, unit)
            second = normalize_back(grad, unit, r.inverse2[block], r.norm[2:3])
            r.rows[block] = second
            r.out_low1[block] = second.astype(LOW)
        ffn_backward(
            r.rows,
            r.out_low1,
            own.inner_low1,
            r.held_up,
            r.held_down,
            r.unit_first,
            r.inverse_first,
            r.norm,
            own.inner_low1,
            r.total,
            r.rows,
            own.first_low1,
            own.norm_grad,
        )
        copies.start(r.rows, r.first1)
        for name in ("inner_low1", "first_low1", "norm_grad"):
            give(name)
        picker_copy.wait()
        weight_sum(
            r.held_picker,
            (r.out_low2, r.out_low1),
            (r.active2, own.active1),
            r.turned,
            r.held_up,
            copies,
            r.send,
            r.keep,
        )
        copies.finish()

    made = {name: (IN_HBM, shape, kind) for name, (shape, kind) in results.items()}
    made |= dict(
        att_full=(IN_HBM, (width, 4 * width), LOW),
        first1=(IN_HBM, size, f32),
        send=(IN_HBM, (width // 2, inner), LOW),
        keep=(IN_HBM, (width // 2, inner), LOW),
    )
    own = {name: pltpu.VMEM(shape, kind) for name, (shape, kind) in results.items()}
    rows_f32 = pltpu.VMEM(size, f32)
    scratch = dict(
        held_up=pltpu.VMEM((width, inner), LOW),
        held_down=pltpu.VMEM((width, inner), LOW),
        held_att=pltpu.VMEM((width, wide), LOW),
        held_picker=pltpu.VMEM((width, width), LOW),
        turned=pltpu.VMEM((width, 2 * count), LOW),
        mask=pltpu.VMEM((count, count), f32),
        qkv=pltpu.VMEM((count, 3 * width), LOW),
        lse=pltpu.VMEM((width // PAIR, 2, count), f32),
        active2=pltpu.VMEM((count, inner), LOW),
        out_low1=pltpu.VMEM(size, LOW),
        out_low2=pltpu.VMEM(size, LOW),
        unit_first=rows_f32,
        inverse_first=pltpu.VMEM((count, 1), f32),
        mixed_grad=pltpu.VMEM(size, LOW),
        inverse1=pltpu.VMEM((count, 1), f32),
        inverse2=pltpu.VMEM((count, 1), f32),
        norm=pltpu.VMEM((4, width), f32),
        total=rows_f32,
        rows=rows_f32,
        hidden2=rows_f32,
        unit1=rows_f32,
        unit2=rows_f32,
    )
    loads = 3 * up_owners.size
    copies = loads + len(results) + 5 + 2 * (inner // TILE)
    scratch |= dict(sem=pltpu.SemaphoreType.DMA((copies,)))
    return launch(
        body,
        dict(
            lengths=(SCALARS, lengths),
            up_owners=(SCALARS, up_owners),
            down_owners=(SCALARS, down_owners),
            att_owners=(SCALARS, att_owners),
            tokens=(VECTORS, tokens),
            cotangent=(VECTORS, cotangent),
            att_parts=(IN_HBM, att_parts),
            picker=(IN_HBM, picker),
            up_parts=(IN_HBM, up_parts),
            down_parts=(IN_HBM, down_parts),
        ),
        made,
        scratch,
        own,
        count * width * (10 * inner + 12 * width) + 9 * count * count * width,
        12 * width * inner,
        60,
    )


def up_gradient(lefts, rights, picker):
    count, width = lefts[0].shape
    inner = rights[0].shape[1]

    def body(r, own):
        copies = Copies(r.sem)
        parts = []
        for part in tiles(inner, TILE):
            part = pl.ds(part.start, TILE)
            pair = zip(r.rights, (own.right_a, own.right_b))
            parts.append([copies.start(a.at[:, part], b.at[:, part], False) for a, b in pair])
        weight_sum(
            r.picker,
            r.lefts,
            (own.right_a, own.right_b),
            r.turned,
            r.whole,
            copies,
            r.send,
            r.keep,
            0,
            lambda index: wait_all(parts[index]),
        )
        copies.finish()

    right = pltpu.VMEM((count, inner), LOW)
    return launch(
        body,
        dict(
            picker=(VECTORS, picker),
            lefts=(VECTORS, list(lefts)),
            rights=(IN_HBM, list(rights)),
        ),
        dict(
            send=(IN_HBM, (width // 2, inner), LOW),
            keep=(IN_HBM, (width // 2, inner), LOW),
        ),
        dict(
            whole=pltpu.VMEM((width, inner), LOW),
            turned=pltpu.VMEM((width, 2 * count), LOW),
            sem=pltpu.SemaphoreType.DMA((4 * (inner // TILE),)),
        ),
        dict(right_a=right, right_b=right),
        count * width * 2 * (inner + width),
        4 * width * inner,
        60,
    )


def first_attention_backward(lengths, first, first_low, qkv, lse, att, tokens, low2, qkv_grad2, mixed, first_low2, norm_grad, picker):
    count, width = first.shape
    size, f32 = (count, width), jnp.float32
    late = dict(
        first_low=first_low,
        qkv=qkv,
        picker=picker,
        low2=low2,
        tokens=tokens,
        qkv_grad2=qkv_grad2,
        mixed1=mixed[0],
        mixed2=mixed[1],
        first_low2=first_low2,
    )
    wide = 4 * width + NORM_COLS

    def body(r, own):
        copies = Copies(r.sem)
        chunks = [None] * 4
        loads = []
        for chunk in (3, 0, 1, 2):
            part = pl.ds(chunk * width, width)
            chunks[chunk] = copies.start(r.att.at[:, part], r.held.at[:, part], False)
            if chunk == 3:
                loads = [copies.start(getattr(r, n), getattr(own, n), False) for n in late]
        first_copy = copies.start(r.first, r.total, False)
        fill_mask(r.lengths, r.mask)
        def ready(chunk):
            chunks[chunk].wait()
            if chunk == 3:
                wait_all(loads[:2])
            if chunk == 0:
                first_copy.wait()

        attend_backward(
            r.total,
            own.first_low,
            own.qkv,
            r.lse,
            r.mask,
            r.held,
            r.mixed_grad,
            r.qkv_grad,
            r.total,
            ready,
        )
        copies.start(r.total, r.input_grad)
        wait_all(loads[2:])
        weight_sum(
            own.picker,
            (own.low2, own.tokens),
            (own.qkv_grad2, r.qkv_grad),
            r.turned,
            r.whole,
            copies,
            r.send,
            r.keep,
        )
        weight_sum(
            own.picker,
            (own.mixed2, own.mixed1),
            (own.first_low2, own.first_low),
            r.turned,
            r.whole,
            copies,
            r.send,
            r.keep,
            3 * width,
        )
        r.norm_rows[...] = jnp.zeros_like(r.norm_rows)
        r.norm_rows[0:4] = r.norm_grad[...].astype(LOW)
        extra = product(own.picker[...], r.norm_rows[...], 1, 1).astype(LOW)
        half = width // 2
        r.extra[...] = extra
        columns = pl.ds(4 * width, NORM_COLS)
        copies.start(r.extra.at[pl.ds(0, half)], r.send.at[:, columns])
        copies.start(r.extra.at[pl.ds(half, half)], r.keep.at[:, columns])
        copies.finish()

    given = dict(
        lengths=(SCALARS, lengths),
        first=(IN_HBM, first),
        lse=(VECTORS, lse),
        norm_grad=(VECTORS, norm_grad),
        att=(IN_HBM, att),
    )
    given |= {name: (IN_HBM, value) for name, value in late.items()}
    own = {name: pltpu.VMEM(value.shape, LOW) for name, value in late.items()}
    scratch = dict(
        held=pltpu.VMEM((width, 4 * width), LOW),
        mask=pltpu.VMEM((count, count), f32),
        mixed_grad=pltpu.VMEM(size, LOW),
        total=pltpu.VMEM(size, f32),
        qkv_grad=pltpu.VMEM((count, 3 * width), LOW),
        turned=pltpu.VMEM((width, 2 * count), LOW),
        whole=pltpu.VMEM((width, 4 * width), LOW),
        norm_rows=pltpu.VMEM((NORM_COLS, width), LOW),
        extra=pltpu.VMEM((width, NORM_COLS), LOW),
        sem=pltpu.SemaphoreType.DMA((6 + len(late) + 2 + 2 * (4 * width // TILE),)),
    )
    return launch(
        body,
        given,
        dict(
            input_grad=(IN_HBM, size, f32),
            send=(IN_HBM, (width // 2, wide), LOW),
            keep=(IN_HBM, (width // 2, wide), LOW),
        ),
        scratch,
        own,
        count * width * 14 * width + 5 * count * count * width,
        16 * width * width,
        60,
    )


AXES = ("dp", "fsdp")


class Route:
    def __init__(self):
        rows, cols = lax.axis_size("dp"), lax.axis_size("fsdp")
        self.inner = cols // 4
        self.ring_size = rows // 2 * self.inner
        self.cols = cols
        self.world = rows * cols
        row, col = lax.axis_index("dp"), lax.axis_index("fsdp")
        self.q = row // 2 * self.inner + col // 4
        self.y, self.x, self.c = row % 2, col // 2 % 2, col % 2

    def joint(self, q, y, x, c):
        return (q // self.inner * 2 + y) * self.cols + q % self.inner * 4 + x * 2 + c

    def move(self, array, step):
        pairs = []
        for q in range(self.ring_size):
            for y in (0, 1):
                for x in (0, 1):
                    for c in (0, 1):
                        to = step(q, y, x, c)
                        pairs.append((self.joint(q, y, x, c), self.joint(*to)))
        return lax.ppermute(array, AXES, pairs)

    def ring(self, array, hops=1):
        return self.move(array, lambda q, y, x, c: ((q + hops) % self.ring_size, y, x, c))

    def core(self, array):
        return self.move(array, lambda q, y, x, c: (q, y, x, 1 - c))

    def first(self, array):
        return self.move(array, lambda q, y, x, c: (q, y ^ c, x ^ (1 - c), c))

    def second(self, array):
        return self.move(array, lambda q, y, x, c: (q, y ^ (1 - c), x ^ c, c))

    def owner(self, back, first, second, core):
        c = self.c ^ core
        x = self.x ^ jnp.where(c == 0, first, second)
        y = self.y ^ jnp.where(c == 0, second, first)
        return self.joint((self.q + self.ring_size - back) % self.ring_size, y, x, c)


def after(value, *earlier):
    return lax.optimization_barrier((value, earlier))[0]


def gather_all(route, att, up, down, besides):
    last = route.ring_size - 1
    pairs = [[jnp.concatenate([piece, route.first(piece)])] for piece in (att, up)]
    chains = (*pairs, [down])
    others = [[route.second(chain[0])] for chain in pairs]
    turns = [2] + [which for _ in range(last - 1) for which in (0, 2)] + [1, 0] + [1] * (last - 1)
    arrived = [(), ()]
    first = crossed = ()
    for turn, which in enumerate(turns):
        early = ()
        if turn == 3:
            early = others[1][0]
        if turn == len(turns) - 1:
            early = crossed
        before = arrived[turn - 1] if which == 1 and len(chains[1]) == 1 and turn else arrived[turn]
        here = after(chains[which][-1], (before, early))
        chains[which].append(route.ring(here))
        arrived.append(chains[which][-1])
        if which < 2 and len(chains[which]) > 2:
            others[which].append(route.second(here))
        if which == 2 and len(chains[2]) > last:
            base = jnp.concatenate(chains[2])
            first = route.first(base)
            both = route.second(after(base, others[0][1]))
            crossed = route.second(after(first, others[0][1]))
    others[0].append(route.second(after(pairs[0][last], first)))
    others[1].append(route.second(after(pairs[1][last], others[0][last])))
    arrays, owners = [[], [], []], [[], [], []]

    def add(which, block, second, blocks, when):
        for core in (0, 1):
            arrays[which].append(route.core(after(block, when)) if core else block)
            owners[which] += [route.owner(back, flip, second, core) for back, flip in blocks]

    for which, chain in enumerate(pairs):
        for k in range(last + 1):
            blocks = [(k, 0), (k, 1)]
            add(which, chain[k], 0, blocks, ())
            add(which, others[which][k], 1, blocks, pairs[1][min(k + 1 + which, last)])
    rows = range(last + 1)
    add(2, base, 0, [(k, 0) for k in rows], (pairs[0][last], besides))
    add(2, first, 0, [(k, 1) for k in rows], pairs[1][max(last - 1, 0)])
    add(2, both, 1, [(k, 0) for k in rows], pairs[1][last])
    add(2, crossed, 1, [(k, 1) for k in rows], pairs[1][last])
    return arrays, owners


def row_picker(owners, shard):
    rows = (jnp.stack(owners)[:, None] * shard + jnp.arange(shard)[None, :]).reshape(-1, 1)
    return (rows == jnp.arange(rows.size)[None, :]).astype(jnp.bfloat16)


def add_all(*terms):
    total = terms[0].astype(jnp.float32)
    for term in terms[1:]:
        total = total + term.astype(jnp.float32)
    return total


def add_low(*terms):
    return add_all(*terms).astype(jnp.bfloat16)


def owners_ring_last(route):
    return [
        route.owner(1 + j, first, second, core)
        for core in (1, 0)
        for second in (1, 0)
        for first in (1, 0)
        for j in range(route.ring_size)
    ]


def owners_ring_middle(route):
    return [
        route.owner(1 + j, first, second, core)
        for core in (1, 0)
        for second in (1, 0)
        for j in range(route.ring_size)
        for first in (1, 0)
    ]


def cut(array, count):
    size = array.shape[0] // count
    return [array[k * size : (k + 1) * size] for k in range(count)]


class SumWhole:
    def __init__(self, route, upper, lower, eager=False):
        self.term = jnp.concatenate([upper, lower])

    def steps(self):
        return iter(())

    def total(self):
        return lax.psum_scatter(self.term, AXES, scatter_dimension=0, tiled=True).astype(
            jnp.float32
        )


class SumRingMiddle:
    def __init__(self, route, send, keep, eager=False):
        self.route, self.terms, self.eager = route, (keep, route.core(send)), eager
        self.result = None

    def steps(self):
        route, terms = self.route, self.terms
        count = route.ring_size
        half = terms[0].shape[0] // 2
        block = half // count
        earlier = yield
        others = []
        for cut in (slice(0, half // 2), slice(half // 2, half)):
            send = add_low(*(part[cut] for part in after(terms, earlier)))
            others.append(route.second(send))
            self.others = others
            earlier = yield send
        moving = None
        for j in range(count):
            arrived = [] if moving is None else [route.ring(moving)]
            due = 2 if j and self.eager else 2 * j // count + 1
            near, far, arrived = after((terms, others[:due], arrived), earlier)
            start = half + j * block
            local = [part[start : start + block] for part in near]
            offset = j * block % (half // 2)
            local.append(far[2 * j // count][offset : offset + block])
            local += arrived
            if j < count - 1:
                moving = add_low(*local)
                earlier = yield moving
        shard = block // 2
        turned = add_low(*(part[:shard] for part in local))
        rest = add_all(*(part[shard:] for part in local))
        earlier = yield (turned, rest)
        self.result = rest + after(route.first(turned), earlier).astype(jnp.float32)
        yield self.result

    def total(self):
        return self.result


class SumRingLast:
    def __init__(self, route, send, keep):
        self.route, self.terms = route, [keep, route.core(send)]
        self.result = None

    def steps(self):
        route, terms = self.route, self.terms
        earlier = yield
        start, total = 0, terms[0].shape[0]
        for step in (route.second, route.first):
            half = (total - start) // 2
            near = after(terms, earlier)
            send = add_low(*self.part(near, start, half))
            start += half
            terms = terms + [step(send)]
            earlier = yield send
        block = (total - start) // route.ring_size
        moving = None
        for j in range(route.ring_size):
            arrived = [] if moving is None else [route.ring(moving)]
            near, arrived = after((terms, arrived), earlier)
            local = self.part(near, start + j * block, block) + arrived
            if j < route.ring_size - 1:
                moving = add_low(*local)
                earlier = yield moving
        self.result = add_all(*local)
        yield self.result

    @staticmethod
    def part(terms, start, size):
        total = terms[0].shape[0]
        skips = [start - (total - term.shape[0]) for term in terms]
        return [term[skip : skip + size] for term, skip in zip(terms, skips)]

    def total(self):
        return self.result


def advance(chain, earlier):
    try:
        return chain.send(earlier)
    except StopIteration:
        return None


def update(gradient, master, moment, average, step_rate):
    moment_new = 0.9 * moment + gradient
    master_new = master - step_rate * (gradient + 0.9 * moment_new)
    average_new = 0.8 * average + 0.2 * master_new
    return (gradient, moment_new, master_new, average_new, master_new.astype(jnp.bfloat16))


def shards(
    tokens,
    cotangent,
    seq_lengths,
    att_master,
    ffn_master,
    norm_master,
    att_moment,
    ffn_moment,
    norm_moment,
    att_average,
    ffn_average,
    norm_average,
):
    row_count = tokens.shape[0]
    route = Route()
    shard = att_master.shape[0]
    norm_piece = jnp.pad(norm_master.T, ((0, 0), (0, NORM_COLS - norm_master.shape[0])))
    att_piece = jnp.concatenate([att_master, norm_piece], axis=1).astype(jnp.bfloat16)
    ffn_pieces = ffn_master.astype(jnp.bfloat16)
    width = att_master.shape[1]
    tiled = shard % 16 == 0
    if tiled:
        middle = row_picker(owners_ring_middle(route), shard)
        last = row_picker(owners_ring_last(route), shard)
        arrays, owners = gather_all(route, att_piece, *ffn_pieces, (middle, last))
        sum_middle, sum_last = SumRingMiddle, SumRingLast
    else:
        middle = last = row_picker(list(range(route.world)), shard)
        pieces = (att_piece, *ffn_pieces)
        arrays = [[lax.all_gather(piece, AXES, axis=0, tiled=True)] for piece in pieces]
        owners = [[0]] * 3
        sum_middle = sum_last = SumWhole
    owned = [
        jnp.stack(rows).astype(jnp.int32) if tiled else jnp.zeros(1, jnp.int32) for rows in owners
    ]
    m = both_layers(
        seq_lengths,
        tokens,
        cotangent,
        arrays[0],
        owned[0],
        arrays[1],
        owned[1],
        arrays[2],
        owned[2],
        middle,
    )
    down_sum = sum_middle(route, m.send, m.keep, True)
    down_steps = down_sum.steps()
    next(down_steps, None)
    c = up_gradient((m.hidden_low2, m.hidden_low1), (m.inner_low2, m.inner_low1), middle)
    up_sum = sum_middle(route, c.send, c.keep)
    sends = down_steps.send(c.send) if tiled else ()
    sends = down_steps.send(sends) if tiled else ()
    a = first_attention_backward(
        seq_lengths,
        after(m.first1, sends),
        m.first_low1,
        m.qkv1,
        m.lse1,
        m.att_full,
        tokens,
        m.low2,
        m.qkv_grad2,
        (m.mixed1, m.mixed2),
        m.first_low2,
        m.norm_grad,
        last,
    )
    in_sum = sum_last(route, a.send, a.keep)
    step_rate = 0.1 / math.sqrt(row_count * lax.axis_size(AXES))

    def ffn_update():
        shares = jnp.stack([up_sum.total(), down_sum.total()])
        return update(shares, ffn_master, ffn_moment, ffn_average, step_rate)

    if tiled:
        up_steps, in_steps = up_sum.steps(), in_sum.steps()
        next(up_steps)
        next(in_steps)
        order = [down_steps, up_steps, up_steps, down_steps, up_steps, in_steps, down_steps]
        order += [up_steps, in_steps, down_steps, in_steps, up_steps, down_steps, in_steps]
        order += [up_steps, in_steps, up_steps]
        earlier = a.input_grad
        for turn, chain in enumerate(order):
            earlier = chain.send((earlier, up_sum.others) if turn == 6 else earlier)
        for chain in (down_steps, up_steps):
            for earlier in iter(functools.partial(advance, chain, earlier), None):
                pass
        ffn_out = ffn_update()
        earlier = (earlier, ffn_out)
        for earlier in iter(functools.partial(advance, in_steps, earlier), None):
            pass
    else:
        ffn_out = ffn_update()
    att_total = in_sum.total()
    norm_total = lax.dot_general(
        jnp.eye(norm_master.shape[0], NORM_COLS, dtype=jnp.float32),
        att_total[:, width:],
        (((1,), (1,)), ((), ())),
        precision=lax.Precision.HIGHEST,
    )
    att_out = update(att_total[:, :width], att_master, att_moment, att_average, step_rate)
    norm_out = update(norm_total, norm_master, norm_moment, norm_average, step_rate)
    return (
        m.layer_output,
        a.input_grad,
        att_out[0],
        att_out[1],
        att_out[2],
        att_out[3],
        att_out[4],
        ffn_out[0],
        ffn_out[1],
        ffn_out[2],
        ffn_out[3],
        ffn_out[4],
        norm_out[0],
        norm_out[1],
        norm_out[2],
        norm_out[3],
        norm_out[4],
    )


def solution(mesh):
    return jax.shard_map(
        shards,
        mesh=mesh,
        in_specs=(
            P(("dp", "fsdp"), None),
            P(("dp", "fsdp"), None),
            P(("dp", "fsdp"), None),
            P(("dp", "fsdp"), None),
            P(None, ("dp", "fsdp"), None),
            P(None, ("dp", "fsdp")),
            P(("dp", "fsdp"), None),
            P(None, ("dp", "fsdp"), None),
            P(None, ("dp", "fsdp")),
            P(("dp", "fsdp"), None),
            P(None, ("dp", "fsdp"), None),
            P(None, ("dp", "fsdp")),
        ),
        out_specs=(
            P(("dp", "fsdp"), None),
            P(("dp", "fsdp"), None),
            P(("dp", "fsdp"), None),
            P(("dp", "fsdp"), None),
            P(("dp", "fsdp"), None),
            P(("dp", "fsdp"), None),
            P(("dp", "fsdp"), None),
            P(None, ("dp", "fsdp"), None),
            P(None, ("dp", "fsdp"), None),
            P(None, ("dp", "fsdp"), None),
            P(None, ("dp", "fsdp"), None),
            P(None, ("dp", "fsdp"), None),
            P(None, ("dp", "fsdp")),
            P(None, ("dp", "fsdp")),
            P(None, ("dp", "fsdp")),
            P(None, ("dp", "fsdp")),
            P(None, ("dp", "fsdp")),
        ),
        check_vma=False,
    )
```

```python
import functools
import math
import types

import jax
import jax.numpy as jnp
from jax import lax
from jax.experimental import pallas as pl
from jax.experimental.pallas import tpu as pltpu
from jax.sharding import PartitionSpec as P

HEAD_DIM = 64


LOW = jnp.bfloat16
SCALE = HEAD_DIM ** (-0.5)
PAIR = 2 * HEAD_DIM
TILE = 512
FF_TILE = 1024
ROWS = 32
NORM_COLS = 128
GELU_RATE = math.sqrt(2.0 / math.pi)
ANYWHERE = pl.BlockSpec(memory_space=pl.ANY)
IN_HBM = pl.BlockSpec(memory_space=pltpu.HBM)
SCALARS = pl.BlockSpec(memory_space=pltpu.SMEM)
VECTORS = pl.BlockSpec(memory_space=pltpu.VMEM)


def launch(body, given, made, scratch, own, products, moved, limit):
    names, specs, arrays = [], [], []
    for name, (spec, value) in given.items():
        group = value if isinstance(value, list) else [value]
        names += [(0, name, isinstance(value, list))] * len(group)
        specs += [spec] * len(group)
        arrays += group
    names += [(0, name, False) for name in (*made, *scratch)]
    names += [(1, name, False) for name in own]

    def kernel(*refs):
        held = ({}, {})
        for (which, name, grouped), ref in zip(names, refs):
            if grouped:
                held[which].setdefault(name, []).append(ref)
            else:
                held[which][name] = ref
        body(*(types.SimpleNamespace(**group) for group in held))

    outs = pl.pallas_call(
        kernel,
        out_shape=[jax.ShapeDtypeStruct(shape, kind) for _, shape, kind in made.values()],
        in_specs=specs,
        out_specs=[spec for spec, _, _ in made.values()],
        scratch_shapes=[*scratch.values(), *own.values()],
        cost_estimate=pl.CostEstimate(
            flops=16 * products, bytes_accessed=moved, transcendentals=0
        ),
        compiler_params=pltpu.CompilerParams(vmem_limit_bytes=limit * 2**20),
    )(*arrays)
    return types.SimpleNamespace(**dict(zip(made, outs)))


class Copies:
    def __init__(self, sem):
        self.sem, self.used, self.open = sem, 0, []

    def start(self, source, target, keep=True):
        copy = pltpu.make_async_copy(source, target, self.sem.at[self.used])
        self.used += 1
        copy.start()
        if keep:
            self.open.append(copy)
        return copy

    def rows(self, parts, owners_ref, target):
        if len(parts) == 1:
            return [self.start(parts[0], target, False)]
        shard = target.shape[0] // owners_ref.shape[0]
        copies = []
        for part in parts:
            for local in range(part.shape[0] // shard):
                row = pl.multiple_of(owners_ref[len(copies)] * shard, shard)
                source = part.at[pl.ds(local * shard, shard)]
                copies.append(self.start(source, target.at[pl.ds(row, shard)], False))
        return copies

    def finish(self):
        for copy in self.open:
            copy.wait()


def wait_all(copies):
    for copy in copies:
        copy.wait()


def product(left, right, left_dim=1, right_dim=0):
    dims = (((left_dim,), (right_dim,)), ((), ()))
    return lax.dot_general(left, right, dims, preferred_element_type=jnp.float32)


def tiles(total, size):
    return [slice(start, start + size) for start in range(0, total, size)]


def fill_mask(lengths_ref, mask_ref):
    shape = mask_ref.shape
    key_row = lax.broadcasted_iota(jnp.int32, shape, 0)
    query_row = lax.broadcasted_iota(jnp.int32, shape, 1)
    end = 0
    key_segment = jnp.zeros(shape, jnp.int32)
    query_segment = jnp.zeros(shape, jnp.int32)
    for slot in range(lengths_ref.shape[1]):
        end = end + lengths_ref[0, slot]
        key_segment += (key_row >= end).astype(jnp.int32)
        query_segment += (query_row >= end).astype(jnp.int32)
    mask_ref[...] = jnp.where(key_segment == query_segment, 0.0, -1e30)


def normalize(values, gain, bias):
    centered = values - jnp.mean(values, axis=-1, keepdims=True)
    spread = jnp.mean(centered * centered, axis=-1, keepdims=True)
    inverse = lax.rsqrt(spread + 1e-05)
    unit = centered * inverse
    return unit, inverse, unit * gain + bias


def normalize_back(grad, unit, inverse, gain):
    scaled = grad * gain
    mean = jnp.mean(scaled, axis=-1, keepdims=True)
    along = jnp.mean(scaled * unit, axis=-1, keepdims=True)
    return inverse * (scaled - mean - unit * along)


def half_lanes(rows, half):
    lane = lax.broadcasted_iota(jnp.int32, (rows, PAIR), 1)
    return (lane >= HEAD_DIM) == bool(half)


def add_norm_grad(norm_grad, row, grad, unit):
    norm_grad[row : row + 1] += jnp.sum(grad * unit, axis=0, keepdims=True)
    norm_grad[row + 1 : row + 2] += jnp.sum(grad, axis=0, keepdims=True)


def attend_forward(rows, low, att, att_ready, mask, qkv, mixed, lse, total, norm, hidden, unit, inverse):
    count, width = low.shape
    att_ready()
    for part in tiles(3 * width, TILE):
        qkv[:, part] = product(low[...], att[:, part]).astype(LOW)
    for pair, part in enumerate(tiles(width, PAIR)):
        query = qkv[:, part] * jnp.asarray(SCALE, LOW)
        key = qkv[:, slice(width + part.start, width + part.stop)]
        value = qkv[:, slice(2 * width + part.start, 2 * width + part.stop)]
        halves, sums = [], []
        for half in (0, 1):
            own = jnp.where(half_lanes(count, half), query, jnp.zeros_like(query))
            scores = product(key, own, 1, 1) + mask[...]
            peak = jnp.max(scores, axis=0, keepdims=True)
            weights = jnp.exp(scores - peak)
            sum_all = jnp.sum(weights, axis=0, keepdims=True)
            sums.append(peak + jnp.log(sum_all))
            out = product(value, weights.astype(LOW), 0, 0)
            halves.append(out[half * HEAD_DIM : (half + 1) * HEAD_DIM] * (1.0 / sum_all))
        lse[pair] = jnp.concatenate(sums, axis=0)
        mixed[:, part] = jnp.concatenate(halves, axis=0).T.astype(LOW)
    for part in tiles(width, TILE):
        out = slice(3 * width + part.start, 3 * width + part.stop)
        total[:, part] = rows[:, part].astype(jnp.float32) + product(mixed[...], att[:, out])
    for block in tiles(count, ROWS):
        unit[block], inverse[block], hidden[block] = normalize(total[block], norm[0:1], norm[1:2])


def ffn_forward(hidden, low, up, down, up_ready, down_ready, active, slope, total):
    low[...] = hidden[...].astype(LOW)
    total[...] = hidden[...]
    up_ready()
    for part in tiles(active.shape[1], FF_TILE):
        inner = product(low[...], up[:, part])
        square = inner * inner
        bend = jnp.tanh(GELU_RATE * inner * (1.0 + 0.044715 * square))
        rise = 0.5 + 0.5 * bend
        act = (inner * rise).astype(LOW)
        active[:, part] = act
        slope[:, part] = (
            rise
            + (0.5 * GELU_RATE) * inner * (1.0 - bend * bend) * (1.0 + 3 * 0.044715 * square)
        ).astype(LOW)
        if part.start == 0:
            down_ready()
        total[...] += product(act, down[:, part], 1, 1)


def ffn_backward(second, out_low, slope, up, down, unit, inverse, norm, inner_low, total, first, first_low, norm_grad, ready=None, norm_ready=None):
    count, _ = second.shape
    total[...] = second[...]
    for index, part in enumerate(tiles(slope.shape[1], FF_TILE)):
        if ready:
            ready(index)
        act = product(out_low[...], down[:, part])
        inner = (act * slope[:, part].astype(jnp.float32)).astype(LOW)
        inner_low[:, part] = inner
        total[...] += product(inner, up[:, part], 1, 1)
    if norm_ready:
        norm_ready()
    for block in tiles(count, ROWS):
        grad, unit_rows = total[block], unit[block]
        add_norm_grad(norm_grad, 0, grad, unit_rows)
        out = normalize_back(grad, unit_rows, inverse[block], norm[0:1])
        first[block] = out
        first_low[block] = out.astype(LOW)


def attend_backward(first, first_low, qkv, lse, mask, att, mixed_grad, qkv_grad, rows_grad, ready=None):
    count, width = first.shape
    if ready:
        ready(3)
    for part in tiles(width, TILE):
        mixed_grad[:, part] = product(
            first_low[...], att[part, 3 * width : 4 * width], 1, 1
        ).astype(LOW)
    for pair, part in enumerate(tiles(width, PAIR)):
        key_part = slice(width + part.start, width + part.stop)
        value_part = slice(2 * width + part.start, 2 * width + part.stop)
        query = qkv[:, part] * jnp.asarray(SCALE, LOW)
        key, value, grad = qkv[:, key_part], qkv[:, value_part], mixed_grad[:, part]
        sums = lse[pair]
        key_grads, value_grads, query_grads = [], [], []
        for half in (0, 1):
            lanes = half_lanes(count, half)
            own_query = jnp.where(lanes, query, jnp.zeros_like(query))
            own_grad = jnp.where(lanes, grad, jnp.zeros_like(grad))
            weights = jnp.exp(product(key, own_query, 1, 1) + mask[...] - sums[half : half + 1])
            weight_grad = product(value, own_grad, 1, 1)
            value_grads.append(product(weights.astype(LOW), grad))
            along = jnp.sum(weights * weight_grad, axis=0, keepdims=True)
            low = (weights * (weight_grad - along)).astype(LOW)
            key_grads.append(product(low, query))
            back = product(key, low, 0, 0)
            query_grads.append(back[half * HEAD_DIM : (half + 1) * HEAD_DIM])
        lanes = half_lanes(count, 1)
        qkv_grad[:, part] = (jnp.concatenate(query_grads, axis=0).T * SCALE).astype(LOW)
        qkv_grad[:, key_part] = jnp.where(lanes, key_grads[1], key_grads[0]).astype(LOW)
        qkv_grad[:, value_part] = jnp.where(lanes, value_grads[1], value_grads[0]).astype(LOW)
    if ready:
        for chunk in range(3):
            ready(chunk)
    for part in tiles(width, TILE):
        rows_grad[:, part] = first[:, part] + product(qkv_grad[...], att[part, : 3 * width], 1, 1)


def weight_sum(picker, lefts, rights, turned, whole, copies, send, keep, offset=0, ready=None):
    count = lefts[0].shape[0]
    half = send.shape[0]
    for layer, left in enumerate(lefts):
        turned[:, layer * count : (layer + 1) * count] = product(
            picker[...], left[...], 1, 1
        ).astype(LOW)
    for index, part in enumerate(tiles(rights[0].shape[1], TILE)):
        if ready:
            ready(index)
        right = jnp.concatenate([ref[:, part] for ref in rights], axis=0)
        start = offset + part.start
        whole[:, start : start + TILE] = product(turned[...], right).astype(LOW)
        columns = pl.ds(start, TILE)
        copies.start(whole.at[pl.ds(0, half), columns], send.at[:, columns])
        copies.start(whole.at[pl.ds(half, half), columns], keep.at[:, columns])


def both_layers(lengths, tokens, cotangent, att_parts, att_owners, up_parts, up_owners, down_parts, down_owners, picker):
    count, width = tokens.shape
    inner = up_parts[0].shape[1]
    wide = att_parts[0].shape[1]
    size, f32 = (count, width), jnp.float32
    results = dict(
        qkv1=((count, 3 * width), LOW),
        mixed1=(size, LOW),
        lse1=((width // PAIR, 2, count), f32),
        hidden_low1=(size, LOW),
        active1=((count, inner), LOW),
        inner_low1=((count, inner), LOW),
        first_low1=(size, LOW),
        low2=(size, LOW),
        mixed2=(size, LOW),
        hidden_low2=(size, LOW),
        layer_output=(size, LOW),
        inner_low2=((count, inner), LOW),
        first_low2=(size, LOW),
        qkv_grad2=((count, 3 * width), LOW),
        norm_grad=((4, width), f32),
    )

    def body(r, own):
        copies = Copies(r.sem)
        att_rows = copies.rows(r.att_parts, r.att_owners, r.held_att)
        up_rows = copies.rows(r.up_parts, r.up_owners, r.held_up)
        down_rows = copies.rows(r.down_parts, r.down_owners, r.held_down)
        picker_copy = copies.start(r.picker, r.held_picker, False)
        fill_mask(r.lengths, r.mask)

        def up_ready():
            wait_all(up_rows)

        def down_ready():
            wait_all(down_rows)

        def give(name):
            copies.start(getattr(own, name), getattr(r, name))

        def att_ready():
            wait_all(att_rows)
            copies.start(r.held_att.at[:, pl.ds(0, 4 * width)], r.att_full)
            turned = r.held_att[:, 4 * width :].astype(f32).T
            r.norm[...] = turned[0:4]

        attend_forward(
            r.tokens,
            r.tokens,
            r.held_att,
            att_ready,
            r.mask,
            own.qkv1,
            own.mixed1,
            own.lse1,
            r.total,
            r.norm,
            r.hidden2,
            r.unit_first,
            r.inverse_first,
        )
        for name in ("qkv1", "mixed1", "lse1"):
            give(name)
        ffn_forward(
            r.hidden2,
            own.hidden_low1,
            r.held_up,
            r.held_down,
            up_ready,
            down_ready,
            own.active1,
            own.inner_low1,
            r.total,
        )
        for name in ("hidden_low1", "active1"):
            give(name)
        for block in tiles(count, ROWS):
            r.unit2[block], r.inverse2[block], rows = normalize(
                r.total[block], r.norm[2:3], r.norm[3:4]
            )
            r.rows[block] = rows
            own.low2[block] = rows.astype(LOW)
        give("low2")
        attend_forward(
            r.rows,
            own.low2,
            r.held_att,
            lambda: None,
            r.mask,
            r.qkv,
            own.mixed2,
            r.lse,
            r.total,
            r.norm,
            r.hidden2,
            r.unit1,
            r.inverse1,
        )
        give("mixed2")
        ffn_forward(
            r.hidden2,
            own.hidden_low2,
            r.held_up,
            r.held_down,
            lambda: None,
            lambda: None,
            r.active2,
            own.inner_low2,
            r.total,
        )
        give("hidden_low2")
        own.norm_grad[...] = jnp.zeros_like(own.norm_grad)
        live = 0
        for slot in range(r.lengths.shape[1]):
            live = live + r.lengths[0, slot]
        for block in tiles(count, ROWS):
            unit, inverse, rows = normalize(r.total[block], r.norm[2:3], r.norm[3:4])
            own.layer_output[block] = rows.astype(LOW)
            position = block.start + lax.broadcasted_iota(jnp.int32, unit.shape, 0)
            grad = jnp.where(position < live, r.cotangent[block].astype(f32), 0.0)
            add_norm_grad(own.norm_grad, 2, grad, unit)
            second = normalize_back(grad, unit, inverse, r.norm[2:3])
            r.rows[block] = second
            r.out_low2[block] = second.astype(LOW)
        give("layer_output")
        ffn_backward(
            r.rows,
            r.out_low2,
            own.inner_low2,
            r.held_up,
            r.held_down,
            r.unit1,
            r.inverse1,
            r.norm,
            own.inner_low2,
            r.total,
            r.rows,
            own.first_low2,
            own.norm_grad,
        )
        for name in ("inner_low2", "first_low2"):
            give(name)
        attend_backward(
            r.rows,
            own.first_low2,
            r.qkv,
            r.lse,
            r.mask,
            r.held_att,
            r.mixed_grad,
            own.qkv_grad2,
            r.total,
        )
        give("qkv_grad2")
        for block in tiles(count, ROWS):
            grad, unit = r.total[block], r.unit2[block]
            add_norm_grad(own.norm_grad, 2, grad, unit)
            second = normalize_back(grad, unit, r.inverse2[block], r.norm[2:3])
            r.rows[block] = second
            r.out_low1[block] = second.astype(LOW)
        ffn_backward(
            r.rows,
            r.out_low1,
            own.inner_low1,
            r.held_up,
            r.held_down,
            r.unit_first,
            r.inverse_first,
            r.norm,
            own.inner_low1,
            r.total,
            r.rows,
            own.first_low1,
            own.norm_grad,
        )
        copies.start(r.rows, r.first1)
        for name in ("inner_low1", "first_low1", "norm_grad"):
            give(name)
        picker_copy.wait()
        weight_sum(
            r.held_picker,
            (r.out_low2, r.out_low1),
            (r.active2, own.active1),
            r.turned,
            r.held_up,
            copies,
            r.send,
            r.keep,
        )
        copies.finish()

    made = {name: (IN_HBM, shape, kind) for name, (shape, kind) in results.items()}
    made |= dict(
        att_full=(IN_HBM, (width, 4 * width), LOW),
        first1=(IN_HBM, size, f32),
        send=(IN_HBM, (width // 2, inner), LOW),
        keep=(IN_HBM, (width // 2, inner), LOW),
    )
    own = {name: pltpu.VMEM(shape, kind) for name, (shape, kind) in results.items()}
    rows_f32 = pltpu.VMEM(size, f32)
    scratch = dict(
        held_up=pltpu.VMEM((width, inner), LOW),
        held_down=pltpu.VMEM((width, inner), LOW),
        held_att=pltpu.VMEM((width, wide), LOW),
        held_picker=pltpu.VMEM((width, width), LOW),
        turned=pltpu.VMEM((width, 2 * count), LOW),
        mask=pltpu.VMEM((count, count), f32),
        qkv=pltpu.VMEM((count, 3 * width), LOW),
        lse=pltpu.VMEM((width // PAIR, 2, count), f32),
        active2=pltpu.VMEM((count, inner), LOW),
        out_low1=pltpu.VMEM(size, LOW),
        out_low2=pltpu.VMEM(size, LOW),
        unit_first=rows_f32,
        inverse_first=pltpu.VMEM((count, 1), f32),
        mixed_grad=pltpu.VMEM(size, LOW),
        inverse1=pltpu.VMEM((count, 1), f32),
        inverse2=pltpu.VMEM((count, 1), f32),
        norm=pltpu.VMEM((4, width), f32),
        total=rows_f32,
        rows=rows_f32,
        hidden2=rows_f32,
        unit1=rows_f32,
        unit2=rows_f32,
    )
    loads = 3 * up_owners.size
    copies = loads + len(results) + 5 + 2 * (inner // TILE)
    scratch |= dict(sem=pltpu.SemaphoreType.DMA((copies,)))
    return launch(
        body,
        dict(
            lengths=(SCALARS, lengths),
            up_owners=(SCALARS, up_owners),
            down_owners=(SCALARS, down_owners),
            att_owners=(SCALARS, att_owners),
            tokens=(VECTORS, tokens),
            cotangent=(VECTORS, cotangent),
            att_parts=(IN_HBM, att_parts),
            picker=(IN_HBM, picker),
            up_parts=(IN_HBM, up_parts),
            down_parts=(IN_HBM, down_parts),
        ),
        made,
        scratch,
        own,
        count * width * (10 * inner + 12 * width) + 9 * count * count * width,
        12 * width * inner,
        60,
    )


def up_gradient(lefts, rights, picker):
    count, width = lefts[0].shape
    inner = rights[0].shape[1]

    def body(r, own):
        copies = Copies(r.sem)
        parts = []
        for part in tiles(inner, TILE):
            part = pl.ds(part.start, TILE)
            pair = zip(r.rights, (own.right_a, own.right_b))
            parts.append([copies.start(a.at[:, part], b.at[:, part], False) for a, b in pair])
        weight_sum(
            r.picker,
            r.lefts,
            (own.right_a, own.right_b),
            r.turned,
            r.whole,
            copies,
            r.send,
            r.keep,
            0,
            lambda index: wait_all(parts[index]),
        )
        copies.finish()

    right = pltpu.VMEM((count, inner), LOW)
    return launch(
        body,
        dict(
            picker=(VECTORS, picker),
            lefts=(VECTORS, list(lefts)),
            rights=(IN_HBM, list(rights)),
        ),
        dict(
            send=(IN_HBM, (width // 2, inner), LOW),
            keep=(IN_HBM, (width // 2, inner), LOW),
        ),
        dict(
            whole=pltpu.VMEM((width, inner), LOW),
            turned=pltpu.VMEM((width, 2 * count), LOW),
            sem=pltpu.SemaphoreType.DMA((4 * (inner // TILE),)),
        ),
        dict(right_a=right, right_b=right),
        count * width * 2 * (inner + width),
        4 * width * inner,
        60,
    )


def first_attention_backward(lengths, first, first_low, qkv, lse, att, tokens, low2, qkv_grad2, mixed, first_low2, norm_grad, picker):
    count, width = first.shape
    size, f32 = (count, width), jnp.float32
    late = dict(
        first_low=first_low,
        qkv=qkv,
        picker=picker,
        low2=low2,
        tokens=tokens,
        qkv_grad2=qkv_grad2,
        mixed1=mixed[0],
        mixed2=mixed[1],
        first_low2=first_low2,
    )
    wide = 4 * width + NORM_COLS

    def body(r, own):
        copies = Copies(r.sem)
        chunks = [None] * 4
        loads = []
        for chunk in (3, 0, 1, 2):
            part = pl.ds(chunk * width, width)
            chunks[chunk] = copies.start(r.att.at[:, part], r.held.at[:, part], False)
            if chunk == 3:
                loads = [copies.start(getattr(r, n), getattr(own, n), False) for n in late]
        first_copy = copies.start(r.first, r.total, False)
        fill_mask(r.lengths, r.mask)
        def ready(chunk):
            chunks[chunk].wait()
            if chunk == 3:
                wait_all(loads[:2])
            if chunk == 0:
                first_copy.wait()

        attend_backward(
            r.total,
            own.first_low,
            own.qkv,
            r.lse,
            r.mask,
            r.held,
            r.mixed_grad,
            r.qkv_grad,
            r.total,
            ready,
        )
        copies.start(r.total, r.input_grad)
        wait_all(loads[2:])
        weight_sum(
            own.picker,
            (own.low2, own.tokens),
            (own.qkv_grad2, r.qkv_grad),
            r.turned,
            r.whole,
            copies,
            r.send,
            r.keep,
        )
        weight_sum(
            own.picker,
            (own.mixed2, own.mixed1),
            (own.first_low2, own.first_low),
            r.turned,
            r.whole,
            copies,
            r.send,
            r.keep,
            3 * width,
        )
        r.norm_rows[...] = jnp.zeros_like(r.norm_rows)
        r.norm_rows[0:4] = r.norm_grad[...].astype(LOW)
        extra = product(own.picker[...], r.norm_rows[...], 1, 1).astype(LOW)
        half = width // 2
        r.extra[...] = extra
        columns = pl.ds(4 * width, NORM_COLS)
        copies.start(r.extra.at[pl.ds(0, half)], r.send.at[:, columns])
        copies.start(r.extra.at[pl.ds(half, half)], r.keep.at[:, columns])
        copies.finish()

    given = dict(
        lengths=(SCALARS, lengths),
        first=(IN_HBM, first),
        lse=(VECTORS, lse),
        norm_grad=(VECTORS, norm_grad),
        att=(IN_HBM, att),
    )
    given |= {name: (IN_HBM, value) for name, value in late.items()}
    own = {name: pltpu.VMEM(value.shape, LOW) for name, value in late.items()}
    scratch = dict(
        held=pltpu.VMEM((width, 4 * width), LOW),
        mask=pltpu.VMEM((count, count), f32),
        mixed_grad=pltpu.VMEM(size, LOW),
        total=pltpu.VMEM(size, f32),
        qkv_grad=pltpu.VMEM((count, 3 * width), LOW),
        turned=pltpu.VMEM((width, 2 * count), LOW),
        whole=pltpu.VMEM((width, 4 * width), LOW),
        norm_rows=pltpu.VMEM((NORM_COLS, width), LOW),
        extra=pltpu.VMEM((width, NORM_COLS), LOW),
        sem=pltpu.SemaphoreType.DMA((6 + len(late) + 2 + 2 * (4 * width // TILE),)),
    )
    return launch(
        body,
        given,
        dict(
            input_grad=(IN_HBM, size, f32),
            send=(IN_HBM, (width // 2, wide), LOW),
            keep=(IN_HBM, (width // 2, wide), LOW),
        ),
        scratch,
        own,
        count * width * 14 * width + 5 * count * count * width,
        16 * width * width,
        60,
    )


AXES = ("dp", "fsdp")


class Route:
    def __init__(self):
        rows, cols = lax.axis_size("dp"), lax.axis_size("fsdp")
        self.inner = cols // 4
        self.ring_size = rows // 2 * self.inner
        self.cols = cols
        self.world = rows * cols
        row, col = lax.axis_index("dp"), lax.axis_index("fsdp")
        self.q = row // 2 * self.inner + col // 4
        self.y, self.x, self.c = row % 2, col // 2 % 2, col % 2

    def joint(self, q, y, x, c):
        return (q // self.inner * 2 + y) * self.cols + q % self.inner * 4 + x * 2 + c

    def move(self, array, step):
        pairs = []
        for q in range(self.ring_size):
            for y in (0, 1):
                for x in (0, 1):
                    for c in (0, 1):
                        to = step(q, y, x, c)
                        pairs.append((self.joint(q, y, x, c), self.joint(*to)))
        return lax.ppermute(array, AXES, pairs)

    def ring(self, array, hops=1):
        return self.move(array, lambda q, y, x, c: ((q + hops) % self.ring_size, y, x, c))

    def core(self, array):
        return self.move(array, lambda q, y, x, c: (q, y, x, 1 - c))

    def first(self, array):
        return self.move(array, lambda q, y, x, c: (q, y ^ c, x ^ (1 - c), c))

    def second(self, array):
        return self.move(array, lambda q, y, x, c: (q, y ^ (1 - c), x ^ c, c))

    def owner(self, back, first, second, core):
        c = self.c ^ core
        x = self.x ^ jnp.where(c == 0, first, second)
        y = self.y ^ jnp.where(c == 0, second, first)
        return self.joint((self.q + self.ring_size - back) % self.ring_size, y, x, c)


def after(value, *earlier):
    return lax.optimization_barrier((value, earlier))[0]


def gather_all(route, att, up, down, besides):
    last = route.ring_size - 1
    pairs = [[jnp.concatenate([piece, route.first(piece)])] for piece in (att, up)]
    chains = (*pairs, [down])
    others = [[route.second(chain[0])] for chain in pairs]
    turns = [2] + [which for _ in range(last - 1) for which in (0, 2)] + [1, 0] + [1] * (last - 1)
    arrived = [(), ()]
    first = crossed = ()
    for turn, which in enumerate(turns):
        early = ()
        if turn == 3:
            early = others[1][0]
        if turn == len(turns) - 1:
            early = crossed
        before = arrived[turn - 1] if which == 1 and len(chains[1]) == 1 and turn else arrived[turn]
        here = after(chains[which][-1], (before, early))
        chains[which].append(route.ring(here))
        arrived.append(chains[which][-1])
        if which < 2 and len(chains[which]) > 2:
            others[which].append(route.second(here))
        if which == 2 and len(chains[2]) > last:
            base = jnp.concatenate(chains[2])
            first = route.first(base)
            both = route.second(after(base, others[0][1]))
            crossed = route.second(after(first, others[0][1]))
    others[0].append(route.second(after(pairs[0][last], first)))
    others[1].append(route.second(after(pairs[1][last], others[0][last])))
    arrays, owners = [[], [], []], [[], [], []]

    def add(which, block, second, blocks, when):
        for core in (0, 1):
            arrays[which].append(route.core(after(block, when)) if core else block)
            owners[which] += [route.owner(back, flip, second, core) for back, flip in blocks]

    for which, chain in enumerate(pairs):
        for k in range(last + 1):
            blocks = [(k, 0), (k, 1)]
            add(which, chain[k], 0, blocks, ())
            late = others[1][last] if (which, k) == (1, last - 1) else pairs[1][min(k + 1 + which, last)]
            add(which, others[which][k], 1, blocks, late)
    rows = range(last + 1)
    add(2, base, 0, [(k, 0) for k in rows], (pairs[0][last], besides))
    add(2, first, 0, [(k, 1) for k in rows], pairs[1][max(last - 1, 0)])
    add(2, both, 1, [(k, 0) for k in rows], pairs[1][last])
    add(2, crossed, 1, [(k, 1) for k in rows], pairs[1][last])
    return arrays, owners


def row_picker(owners, shard):
    rows = (jnp.stack(owners)[:, None] * shard + jnp.arange(shard)[None, :]).reshape(-1, 1)
    return (rows == jnp.arange(rows.size)[None, :]).astype(jnp.bfloat16)


def add_all(*terms):
    total = terms[0].astype(jnp.float32)
    for term in terms[1:]:
        total = total + term.astype(jnp.float32)
    return total


def add_low(*terms):
    return add_all(*terms).astype(jnp.bfloat16)


def owners_ring_last(route):
    return [
        route.owner(1 + j, first, second, core)
        for core in (1, 0)
        for second in (1, 0)
        for first in (1, 0)
        for j in range(route.ring_size)
    ]


def owners_ring_middle(route):
    return [
        route.owner(1 + j, first, second, core)
        for core in (1, 0)
        for second in (1, 0)
        for j in range(route.ring_size)
        for first in (1, 0)
    ]


def cut(array, count):
    size = array.shape[0] // count
    return [array[k * size : (k + 1) * size] for k in range(count)]


class SumWhole:
    def __init__(self, route, upper, lower, eager=False):
        self.term = jnp.concatenate([upper, lower])

    def steps(self):
        return iter(())

    def total(self):
        return lax.psum_scatter(self.term, AXES, scatter_dimension=0, tiled=True).astype(
            jnp.float32
        )


class SumRingMiddle:
    def __init__(self, route, send, keep, eager=False):
        self.route, self.terms, self.eager = route, (keep, route.core(send)), eager
        self.result = None

    def steps(self):
        route, terms = self.route, self.terms
        count = route.ring_size
        half = terms[0].shape[0] // 2
        block = half // count
        earlier = yield
        others = []
        for cut in (slice(0, half // 2), slice(half // 2, half)):
            send = add_low(*(part[cut] for part in after(terms, earlier)))
            others.append(route.second(send))
            self.others = others
            earlier = yield send
        moving = None
        for j in range(count):
            arrived = [] if moving is None else [route.ring(moving)]
            due = 2 if j and self.eager else 2 * j // count + 1
            near, far, arrived = after((terms, others[:due], arrived), earlier)
            start = half + j * block
            local = [part[start : start + block] for part in near]
            offset = j * block % (half // 2)
            local.append(far[2 * j // count][offset : offset + block])
            local += arrived
            if j < count - 1:
                moving = add_low(*local)
                earlier = yield moving
        shard = block // 2
        turned = add_low(*(part[:shard] for part in local))
        rest = add_all(*(part[shard:] for part in local))
        earlier = yield (turned, rest)
        self.result = rest + after(route.first(turned), earlier).astype(jnp.float32)
        yield self.result

    def total(self):
        return self.result


class SumRingLast:
    def __init__(self, route, send, keep):
        self.route, self.terms = route, [keep, route.core(send)]
        self.result = None

    def steps(self):
        route, terms = self.route, self.terms
        earlier = yield
        start, total = 0, terms[0].shape[0]
        for step in (route.second, route.first):
            half = (total - start) // 2
            near = after(terms, earlier)
            send = add_low(*self.part(near, start, half))
            start += half
            terms = terms + [step(send)]
            earlier = yield send
        block = (total - start) // route.ring_size
        moving = None
        for j in range(route.ring_size):
            arrived = [] if moving is None else [route.ring(moving)]
            near, arrived = after((terms, arrived), earlier)
            local = self.part(near, start + j * block, block) + arrived
            if j < route.ring_size - 1:
                moving = add_low(*local)
                earlier = yield moving
        self.result = add_all(*local)
        yield self.result

    @staticmethod
    def part(terms, start, size):
        total = terms[0].shape[0]
        skips = [start - (total - term.shape[0]) for term in terms]
        return [term[skip : skip + size] for term, skip in zip(terms, skips)]

    def total(self):
        return self.result


def advance(chain, earlier):
    try:
        return chain.send(earlier)
    except StopIteration:
        return None


def update(gradient, master, moment, average, step_rate):
    moment_new = 0.9 * moment + gradient
    master_new = master - step_rate * (gradient + 0.9 * moment_new)
    average_new = 0.8 * average + 0.2 * master_new
    return (gradient, moment_new, master_new, average_new, master_new.astype(jnp.bfloat16))


def shards(
    tokens,
    cotangent,
    seq_lengths,
    att_master,
    ffn_master,
    norm_master,
    att_moment,
    ffn_moment,
    norm_moment,
    att_average,
    ffn_average,
    norm_average,
):
    row_count = tokens.shape[0]
    route = Route()
    shard = att_master.shape[0]
    norm_piece = jnp.pad(norm_master.T, ((0, 0), (0, NORM_COLS - norm_master.shape[0])))
    att_piece = jnp.concatenate([att_master, norm_piece], axis=1).astype(jnp.bfloat16)
    ffn_pieces = ffn_master.astype(jnp.bfloat16)
    width = att_master.shape[1]
    tiled = shard % 16 == 0
    if tiled:
        middle = row_picker(owners_ring_middle(route), shard)
        last = row_picker(owners_ring_last(route), shard)
        arrays, owners = gather_all(route, att_piece, *ffn_pieces, (middle, last))
        sum_middle, sum_last = SumRingMiddle, SumRingLast
    else:
        middle = last = row_picker(list(range(route.world)), shard)
        pieces = (att_piece, *ffn_pieces)
        arrays = [[lax.all_gather(piece, AXES, axis=0, tiled=True)] for piece in pieces]
        owners = [[0]] * 3
        sum_middle = sum_last = SumWhole
    owned = [
        jnp.stack(rows).astype(jnp.int32) if tiled else jnp.zeros(1, jnp.int32) for rows in owners
    ]
    m = both_layers(
        seq_lengths,
        tokens,
        cotangent,
        arrays[0],
        owned[0],
        arrays[1],
        owned[1],
        arrays[2],
        owned[2],
        middle,
    )
    down_sum = sum_middle(route, m.send, m.keep, True)
    down_steps = down_sum.steps()
    next(down_steps, None)
    c = up_gradient((m.hidden_low2, m.hidden_low1), (m.inner_low2, m.inner_low1), middle)
    up_sum = sum_middle(route, c.send, c.keep)
    sends = down_steps.send(c.send) if tiled else ()
    sends = down_steps.send(sends) if tiled else ()
    a = first_attention_backward(
        seq_lengths,
        after(m.first1, sends),
        m.first_low1,
        m.qkv1,
        m.lse1,
        m.att_full,
        tokens,
        m.low2,
        m.qkv_grad2,
        (m.mixed1, m.mixed2),
        m.first_low2,
        m.norm_grad,
        last,
    )
    in_sum = sum_last(route, a.send, a.keep)
    step_rate = 0.1 / math.sqrt(row_count * lax.axis_size(AXES))

    def ffn_update():
        shares = jnp.stack([up_sum.total(), down_sum.total()])
        return update(shares, ffn_master, ffn_moment, ffn_average, step_rate)

    if tiled:
        up_steps, in_steps = up_sum.steps(), in_sum.steps()
        next(up_steps)
        next(in_steps)
        order = [down_steps, up_steps, up_steps, down_steps, up_steps, in_steps, down_steps]
        order += [up_steps, in_steps, down_steps, in_steps, up_steps, down_steps, in_steps]
        order += [up_steps, in_steps, up_steps]
        earlier = a.input_grad
        for turn, chain in enumerate(order):
            earlier = chain.send((earlier, up_sum.others) if turn == 6 else earlier)
        for chain in (down_steps, up_steps):
            for earlier in iter(functools.partial(advance, chain, earlier), None):
                pass
        ffn_out = ffn_update()
        earlier = (earlier, ffn_out)
        for earlier in iter(functools.partial(advance, in_steps, earlier), None):
            pass
    else:
        ffn_out = ffn_update()
    att_total = in_sum.total()
    norm_total = lax.dot_general(
        jnp.eye(norm_master.shape[0], NORM_COLS, dtype=jnp.float32),
        att_total[:, width:],
        (((1,), (1,)), ((), ())),
        precision=lax.Precision.HIGHEST,
    )
    att_out = update(att_total[:, :width], att_master, att_moment, att_average, step_rate)
    norm_out = update(norm_total, norm_master, norm_moment, norm_average, step_rate)
    return (
        m.layer_output,
        a.input_grad,
        att_out[0],
        att_out[1],
        att_out[2],
        att_out[3],
        att_out[4],
        ffn_out[0],
        ffn_out[1],
        ffn_out[2],
        ffn_out[3],
        ffn_out[4],
        norm_out[0],
        norm_out[1],
        norm_out[2],
        norm_out[3],
        norm_out[4],
    )


def solution(mesh):
    return jax.shard_map(
        shards,
        mesh=mesh,
        in_specs=(
            P(("dp", "fsdp"), None),
            P(("dp", "fsdp"), None),
            P(("dp", "fsdp"), None),
            P(("dp", "fsdp"), None),
            P(None, ("dp", "fsdp"), None),
            P(None, ("dp", "fsdp")),
            P(("dp", "fsdp"), None),
            P(None, ("dp", "fsdp"), None),
            P(None, ("dp", "fsdp")),
            P(("dp", "fsdp"), None),
            P(None, ("dp", "fsdp"), None),
            P(None, ("dp", "fsdp")),
        ),
        out_specs=(
            P(("dp", "fsdp"), None),
            P(("dp", "fsdp"), None),
            P(("dp", "fsdp"), None),
            P(("dp", "fsdp"), None),
            P(("dp", "fsdp"), None),
            P(("dp", "fsdp"), None),
            P(("dp", "fsdp"), None),
            P(None, ("dp", "fsdp"), None),
            P(None, ("dp", "fsdp"), None),
            P(None, ("dp", "fsdp"), None),
            P(None, ("dp", "fsdp"), None),
            P(None, ("dp", "fsdp"), None),
            P(None, ("dp", "fsdp")),
            P(None, ("dp", "fsdp")),
            P(None, ("dp", "fsdp")),
            P(None, ("dp", "fsdp")),
            P(None, ("dp", "fsdp")),
        ),
        check_vma=False,
    )
```
